32 devices in a mesh: leaf: 4 (over y, x), row: 2 (over core), col: 4 (over z).
Axes of the slice: x: 2, y: 2, z: 4, core: 2. Of those that a mesh axis runs over, the one named last changes fastest.
Arguments:
- sigma_top: float32 [1024, 1024], P(('leaf', 'row'), 'col')
- panels: float32 [4, 7, 1024, 512], P('leaf', None, 'row', 'col'), may hold values from -0.1875 to 0.1875
- inverse_diag: float32 [4, 7, 512, 512], P('leaf', None, 'col')
- slot_lists: int32 [4, 6, 8], P('leaf'), may hold values from -1 to 11, as said below
- parent_links: int32 [4, 4], P('leaf'), may hold values from 1 to 2
Outputs:
- ancestor_block: float32 [4, 7, 1024, 512], P('leaf', None, 'row', 'col')
- diagonal_block: float32 [4, 7, 512, 512], P('leaf', None, None, 'col')
The draws below stay inside these ranges and needn't reach their ends.
Inputs may be any that keep to these rules, and one draw needn't show every extreme that they name: `slot_lists`: in every row, entries 0 to 3 are 8 to 11 in order (the parent's own tiles); then come 1 to 3 distinct parent ancestor slots, below 8 for supernodes 1 and 2 and below 4 for supernodes 3 to 6; the rest are -1, so every row has padding. `parent_links`: each supernode 3 to 6 has supernode 1 or 2 as its parent. `sigma_top`: symmetric.
All inputs are finite; a program needn't handle non-finite values.
Results may differ from the reference program's by a relative error of at most 0.0001.
Values sent between devices are 32-bit elements; how exact they have to be, the bound alone decides.
No kernel may reach another device: no remote copies, remote signals or barrier semaphores. Data moves between devices by JAX's collectives and lax.ppermute only.
A program may use at most 128 MiB of HBM per device.

```python
import jax
import jax.numpy as jnp
from jax import lax

TILE = 128
NA = 8
NJ = 4
NODES = 7
SEC = 4


def draw_sigma_top(key, part):
    order = NA * TILE
    key_noise, key_diag = jax.random.split(key, 2)
    random_part = jax.random.normal(key_noise, (order, order), jnp.float32)
    symmetric = (random_part + random_part.T) * (0.35 / jnp.sqrt(2.0 * order))
    positions = jnp.arange(order)
    identity = (positions[:, None] == positions[None, :]).astype(jnp.float32)
    diagonal_values = jax.random.uniform(key_diag, (order,), jnp.float32, 0.8, 1.3)
    matrix = symmetric + identity * diagonal_values[:, None]
    return matrix


def draw_inverse_diag(key, part):
    order = NJ * TILE
    key_noise, key_diag = jax.random.split(key, 2)
    positions = jnp.arange(order)
    strictly_lower = (positions[:, None] > positions[None, :]).astype(jnp.float32)
    identity = (positions[:, None] == positions[None, :]).astype(jnp.float32)
    off_part = jax.random.normal(key_noise, (SEC, NODES, order, order), jnp.float32) * (0.4 / jnp.sqrt(1.0 * order))
    diagonal_values = jax.random.uniform(key_diag, (SEC, NODES, order), jnp.float32, 0.7, 1.3)
    return off_part * strictly_lower + identity * diagonal_values[..., None]


def draw_slot_lists(key, part):
    key_count, key_score = jax.random.split(key, 2)
    rows_total = NODES - 1
    head_part = jnp.broadcast_to(NA + jnp.arange(NJ, dtype=jnp.int32), (SEC, rows_total, NJ))
    counts = jax.random.randint(key_count, (SEC, rows_total), 1, NA - NJ, dtype=jnp.int32)
    scores = jax.random.randint(key_score, (SEC, rows_total, NA), 0, 2 ** 20, dtype=jnp.int32)
    candidates = jnp.arange(NA, dtype=jnp.int32)
    limits = jnp.where(jnp.arange(rows_total) < 2, NA, NJ).astype(jnp.int32)
    outside = (candidates[None, None, :] >= limits[None, :, None]).astype(jnp.int32)
    sort_keys = outside * 2 ** 26 + scores * NA + candidates[None, None, :]
    ordering = jnp.argsort(sort_keys, axis=-1).astype(jnp.int32)
    tail_picks = ordering[:, :, :NA - NJ]
    tail_positions = jnp.arange(NA - NJ, dtype=jnp.int32)
    tail_part = jnp.where(tail_positions[None, None, :] < counts[:, :, None], tail_picks, -1)
    return jnp.concatenate([head_part, tail_part], axis=-1).astype(jnp.int32)


def plant(array, rng, least, high):
    shape = array.shape
    spot = [jax.random.randint(jax.random.fold_in(rng, axis), (), 0, shape[axis]) for axis in range(len(shape))]
    array = array.at[tuple(spot)].set(least)
    longest = shape.index(max(shape))
    spot[longest] = (spot[longest] + 1) % shape[longest]
    return array.at[tuple(spot)].set(high)


def block_levels(stream_key, shape, shards, smallest, top_value):
    def one(position, parts):
        heights = jax.random.uniform(jax.random.fold_in(jax.random.fold_in(stream_key, 6), position), (parts,), jnp.float32, smallest / len(shards), top_value / len(shards))
        return jnp.repeat(jnp.exp(heights), shape[position] // parts).reshape((-1,) + (1,) * (len(shape) - position - 1))

    level = one(*shards[0])
    for cut in shards[1:]:
        level = level * one(*cut)
    return level


def centred(key, shape, spread, most, cuts=(), kind=jnp.bfloat16):
    values = jax.random.normal(key, shape, jnp.float32) * spread
    if len(cuts) > 0:
        values = block_levels(key, shape, cuts, -0.22, 0.18) * values
    return jnp.clip(values, min=-most, max=most).astype(kind)


def setup_inputs(seed: int = 0) -> dict:
    streams_of = jax.random.split(jax.random.key(seed), 6)
    return {
        "sigma_top": draw_sigma_top(jax.random.fold_in(streams_of[5], 71), 0),
        "panels": centred(streams_of[1], (SEC, NODES, NA * TILE, NJ * TILE), (NA * TILE) ** -0.5, 0.1875, ((0, 4), (2, 2), (3, 4)), jnp.float32),
        "inverse_diag": draw_inverse_diag(jax.random.fold_in(streams_of[5], 71), 0),
        "slot_lists": draw_slot_lists(jax.random.fold_in(streams_of[5], 71), 0),
        "parent_links": plant(jax.random.randint(streams_of[4], (SEC, NODES - 3), 1, 3), jax.random.fold_in(streams_of[4], 1), 1, 2).astype(jnp.int32),
    }


HIGHEST = lax.Precision.HIGHEST


def select_block(extended, picks):
    count_tiles = extended.shape[0] // TILE
    blocks = extended.reshape(count_tiles, TILE, count_tiles, TILE)
    living = picks >= 0
    indices = jnp.maximum(picks, 0).astype(jnp.int32)
    chosen = jnp.take(blocks, indices, axis=0)
    chosen = jnp.take(chosen, indices, axis=2)
    weights = (living[:, None] & living[None, :]).astype(jnp.float32)
    chosen = chosen * weights[:, None, :, None]
    return chosen.reshape(picks.shape[0] * TILE, picks.shape[0] * TILE)


def extend_block(ancestor, product, diagonal):
    upper = jnp.concatenate([ancestor, -product], axis=1)
    lower = jnp.concatenate([-product.T, diagonal], axis=1)
    return jnp.concatenate([upper, lower], axis=0)


def node_step(ancestor, factor_u, gram):
    product = jnp.dot(ancestor, factor_u, precision=HIGHEST, preferred_element_type=jnp.float32)
    diagonal = gram + jnp.dot(factor_u.T, product, precision=HIGHEST, preferred_element_type=jnp.float32)
    return product, diagonal


def reference(sigma_top, panels, inverse_diag, slot_lists, parent_links):
    ancestor_out = []
    diagonal_out = []
    for section in range(SEC):
        picks_all = slot_lists[section]
        living = jnp.concatenate([jnp.ones((1, NA), jnp.bool_), picks_all >= 0], axis=0)
        row_weight = jnp.repeat(living.astype(jnp.float32), TILE, axis=1)
        factors = jnp.einsum("vak,vkj->vaj", panels[section], inverse_diag[section], precision=HIGHEST)
        factors = factors * row_weight[:, :, None]
        grams = jnp.einsum("vki,vkj->vij", inverse_diag[section], inverse_diag[section], precision=HIGHEST)
        extended_list = []
        products = []
        diagonals = []
        for node in range(NODES):
            if node == 0:
                ancestor = sigma_top
            elif node < 3:
                ancestor = select_block(extended_list[0], picks_all[node - 1])
            else:
                parent = parent_links[section, node - 3]
                source = jnp.where(parent == 1, extended_list[1], extended_list[2])
                ancestor = select_block(source, picks_all[node - 1])
            product, diagonal = node_step(ancestor, factors[node], grams[node])
            products.append(-product)
            diagonals.append(diagonal)
            if node < 3:
                extended_list.append(extend_block(ancestor, product, diagonal))
        ancestor_out.append(jnp.stack(products))
        diagonal_out.append(jnp.stack(diagonals))
    return jnp.stack(ancestor_out), jnp.stack(diagonal_out)
```

```python
import functools

import jax
import jax.numpy as jnp
from jax import lax
from jax.experimental import pallas as pl
from jax.experimental.pallas import tpu as pltpu
from jax.sharding import PartitionSpec as P

TILE = 128
F32 = jnp.float32
BF16 = jnp.bfloat16
VMEM_LIMIT = 56 * 2**20


def split(x):
    high = x.astype(BF16)
    return high, (x - high.astype(F32)).astype(BF16)


def dot3(a, b, contract):
    dims = ((contract, contract if contract == (0,) else (0,)), ((), ()))
    dot = functools.partial(lax.dot_general, dimension_numbers=dims, preferred_element_type=F32)
    return dot(a[0], b[0]) + (dot(a[0], b[1]) + dot(a[1], b[0]))


def put(pair, index, value):
    high, low = split(value)
    pair[0][index] = high
    pair[1][index] = low


def get(pair, index):
    return pair[0][index], pair[1][index]


def at(start, size, unit=TILE):
    return pl.ds(pl.multiple_of(start, unit), size)


def load_panels(blocks, r, p, d, half):
    quarter = TILE // 2
    for slot in range(4):
        for turn in range(2):
            ref = blocks[2 * slot + turn]
            side = r if turn == 0 else 1 - r
            put(p, (at(side * half, half), slice(slot * TILE, (slot + 1) * TILE)), ref[0:half, :])
            for j in range(4):
                rows = at(slot * TILE + side * quarter, quarter, quarter)
                put(d, (rows, slice(j * TILE, (j + 1) * TILE)), ref[half + j * quarter:half + (j + 1) * quarter, :])


def solve(p, d, a, dc, f, w, t, base, weights, emit_ab, emit_dg):
    width = dc[0].shape[1]
    slots = a[0].shape[0] // TILE
    dc[0][...] = d[0][:, at(base, width)]
    dc[1][...] = d[1][:, at(base, width)]
    step = 2 * TILE
    for m in range(0, slots * TILE, step):
        rows = slice(m, m + step)
        value = dot3(get(p, (rows, slice(None))), get(dc, (slice(None), slice(None))), (1,))
        if weights is not None:
            k = m // TILE
            value = jnp.concatenate([value[:TILE] * weights[k], value[TILE:] * weights[k + 1]], axis=0)
        put(f, (rows, slice(None)), value)
    for m in range(0, slots * TILE, step):
        rows = slice(m, m + step)
        value = dot3(get(a, (rows, slice(None))), get(f, (slice(None), slice(None))), (1,))
        emit_ab(m, -value)
        put(w, (rows, slice(None)), value)
    for m in range(0, d[0].shape[0], step):
        cols = slice(m, m + step)
        value = dot3(get(p, (slice(None), cols)), get(w, (slice(None), slice(None))), (0,))
        put(t, (cols, slice(None)), value + dc[0][cols, :].astype(F32) + dc[1][cols, :].astype(F32))
    for m in range(0, d[0].shape[0], step):
        cols = slice(m, m + step)
        emit_dg(m, dot3(get(d, (slice(None), cols)), get(t, (slice(None), slice(None))), (0,)))


def pair_of(rows, cols):
    return [pltpu.VMEM((rows, cols), BF16)] * 2


def scratch_for(order, own, width):
    shapes = []
    for rows, cols in ((order, own), (own, own), (order, order), (own, width), (order, width), (order, width), (own, width)):
        shapes += pair_of(rows, cols)
    return shapes


def pairs(refs):
    return [(refs[i], refs[i + 1]) for i in range(0, len(refs), 2)]


def call(kernel, scalars, operands, outs, scratch, flops):
    whole = pl.BlockSpec(memory_space=pltpu.VMEM)
    traffic = sum(x.size * 4 for x in operands) + sum(4 * rows * cols for rows, cols in outs)
    return pl.pallas_call(
        kernel,
        out_shape=[jax.ShapeDtypeStruct(o, F32) for o in outs],
        in_specs=[pl.BlockSpec(memory_space=pltpu.SMEM)] + [whole] * len(operands),
        out_specs=[whole] * len(outs),
        scratch_shapes=scratch,
        compiler_params=pltpu.CompilerParams(vmem_limit_bytes=VMEM_LIMIT),
        cost_estimate=pl.CostEstimate(flops=flops, bytes_accessed=traffic, transcendentals=0),
    )(scalars, *operands)


def tail_of(s, start, own_tiles, tail):
    index = [jnp.maximum(s[start + own_tiles + j], 0) for j in range(tail)]
    weight = [(s[start + own_tiles + j] >= 0).astype(F32) for j in range(tail)]
    return index, weight


def weights_of(s, start, slots):
    return [(s[start + j] >= 0).astype(F32) for j in range(slots)]


LIST = 4


def root_kernel(s, *refs):
    blocks, mine, other = refs[:8], refs[8:12], refs[12:16]
    ext, corner = refs[16:18]
    p, d, a, dc, f, w, t = pairs(refs[18:])
    r, c, leaf = s[0], s[1], s[2]
    order = a[0].shape[0]
    own = d[0].shape[0]
    width = dc[0].shape[1]
    far = c // 2
    places = (c, 3 * far, 3 - c, 3 - 3 * far)
    band, span = mine[0].shape[0], mine[0].shape[1] // 4
    for m in range(4):
        for turn, ref in ((0, mine[m]), (1, other[m])):
            side = r if turn == 0 else 1 - r
            rows = at(((leaf ^ m) * 2 + side) * band, band)
            for k in range(4):
                put(a, (rows, at(places[k] * span, span)), ref[:, k * span:(k + 1) * span])
    load_panels(blocks, r, p, d, order // 2)

    def emit_ab(m, value):
        ext[m:m + value.shape[0], :] = value

    def emit_dg(m, value):
        ext[order + m:order + m + value.shape[0], :] = value

    solve(p, d, a, dc, f, w, t, r * width, None, emit_ab, emit_dg)
    tail = (order - own) // TILE
    index, weight = tail_of(s, LIST, own // TILE, tail)
    for i in range(tail):
        for j in range(tail):
            high, low = get(a, (at(index[i] * TILE, TILE), at(index[j] * TILE, TILE)))
            value = (high.astype(F32) + low.astype(F32)) * (weight[i] * weight[j])
            corner[i * TILE:(i + 1) * TILE, j * TILE:(j + 1) * TILE] = value


def join_parent(a, x, order, own, offset, index, weight):
    width = x.shape[1]
    put(a, (slice(0, own), at(offset, width)), x[order:order + own, :])
    for j in range(len(index)):
        place = slice(own + j * TILE, own + (j + 1) * TILE)
        value = x[at(index[j] * TILE, TILE), :] * weight[j]
        put(a, (place, at(offset, width)), value)
        put(a, (at(offset, width), place), value.T)


def middle_kernel(s, *refs):
    blocks, mine, other, corner = refs[:8], refs[8], refs[9], refs[10]
    ext, grand = refs[11:13]
    p, d, a, dc, f, w, t = pairs(refs[13:])
    r = s[0]
    order = a[0].shape[0]
    own = d[0].shape[0]
    width = dc[0].shape[1]
    load_panels(blocks, r, p, d, order // 2)
    index, weight = tail_of(s, LIST, own // TILE, (order - own) // TILE)
    span = mine.shape[1]
    join_parent(a, mine, order, own, r * span, index, weight)
    join_parent(a, other, order, own, (1 - r) * span, index, weight)
    put(a, (slice(own, order), slice(own, order)), corner[...])
    grand[:, at(r * span, span)] = mine[order:order + own, :]
    grand[:, at((1 - r) * span, span)] = other[order:order + own, :]
    weights = weights_of(s, LIST, order // TILE)
    for base in range(0, own, width):
        def emit_ab(m, value):
            ext[m:m + value.shape[0], base:base + width] = value

        def emit_dg(m, value):
            ext[order + m:order + m + value.shape[0], base:base + width] = value

        solve(p, d, a, dc, f, w, t, base, weights, emit_ab, emit_dg)


def leaf_kernel(s, *refs):
    blocks, mine, other, grand = refs[:8], refs[8], refs[9], refs[10]
    self_out, core_out, end_out, cross_out = refs[11:15]
    p, d, a, dc, f, w, t = pairs(refs[15:29])
    ab, dg = refs[29:31]
    r, c = s[0], s[1]
    order = a[0].shape[0]
    own = d[0].shape[0]
    width = dc[0].shape[1]
    far = c // 2
    load_panels(blocks, r, p, d, order // 2)
    tail = (order - own) // TILE
    index, weight = tail_of(s, LIST, own // TILE, tail)

    @pl.when(s[3] == 1)
    def _():
        join_parent(a, mine, order, own, 0, index, weight)

    @pl.when(s[3] == 0)
    def _():
        join_parent(a, other, order, own, 0, index, weight)

    for i in range(tail):
        for j in range(tail):
            value = grand[at(index[i] * TILE, TILE), at(index[j] * TILE, TILE)] * (weight[i] * weight[j])
            put(a, (slice(own + i * TILE, own + (i + 1) * TILE), slice(own + j * TILE, own + (j + 1) * TILE)), value)

    def emit_ab(m, value):
        ab[m:m + value.shape[0], :] = value

    def emit_dg(m, value):
        dg[m:m + value.shape[0], :] = value

    solve(p, d, a, dc, f, w, t, far * width, weights_of(s, LIST, order // TILE), emit_ab, emit_dg)
    half = order // 2
    near_cols, end_cols = at((1 - far) * TILE, TILE), at(far * TILE, TILE)
    for out, side, cols in (
        (self_out, r, near_cols), (core_out, 1 - r, near_cols), (end_out, r, end_cols), (cross_out, 1 - r, end_cols)
    ):
        out[0:half, :] = ab[at(side * half, half), cols]
        out[half:, :] = dg[:, cols]


def chip_body(sigma_top, panels, inverse_diag, slot_lists, parent_links):
    r = lax.axis_index("row")
    c = lax.axis_index("col")
    leaf = lax.axis_index("leaf")
    panels, inverse, lists, links = panels[0], inverse_diag[0], slot_lists[0], parent_links[0]
    half = panels.shape[1]
    order = 2 * half
    own = inverse.shape[2]
    slots = order // TILE
    quarter = TILE // 2
    both = ("row", "col")

    routes = (((0, 1), (3, 2)), ((1, 2), (2, 1)), ((0, 2), (3, 1)))
    cross = [[(row * 4 + a, (1 - row) * 4 + b) for row in range(2) for a, b in route] for route in routes]
    middles = (1, 2)
    swap = [(row * 4 + a, (1 - row) * 4 + a) for row in range(2) for a in middles]
    home = ((1, 0), (2, 3))
    home_cross = [(row * 4 + a, (1 - row) * 4 + b) for row in range(2) for a, b in home]

    def straight(x):
        return [lax.ppermute(x, "col", route) for route in routes]

    def crossed(x):
        return [lax.ppermute(x, both, route) for route in cross]

    def swapped(x):
        return lax.ppermute(x, both, swap)

    def pack(node):
        panel = lax.dynamic_index_in_dim(panels, node, 0, keepdims=False)
        band = lax.dynamic_slice(inverse, (node, r * quarter, 0), (1, quarter, own))[0]
        return jnp.concatenate([panel] + [band[:, j:j + TILE] for j in range(0, own, TILE)], axis=0)

    def scalars(row, parent_mine):
        head = jnp.stack([r, c, leaf, parent_mine]).astype(jnp.int32)
        return jnp.concatenate([head, lax.dynamic_index_in_dim(lists, row, 0, keepdims=False)])

    sigma_cols = jnp.concatenate([sigma_top] + straight(sigma_top), axis=1)
    root_pack = pack(0)
    root_mine = [root_pack] + straight(root_pack)
    leaf_route = [
        [((lf * 2 + row) * 4 + a, ((lf ^ m) * 2 + row) * 4 + a) for lf in range(4) for row in range(2) for a in middles]
        for m in range(4)
    ]
    sigma_mine = [sigma_cols] + [
        lax.ppermute(sigma_cols, ("leaf", "row", "col"), leaf_route[m]) for m in range(1, 4)
    ]
    sigma_other = [swapped(x) for x in sigma_mine]
    root_other = [swapped(x) for x in root_mine]

    def gather_pair(first):
        direct = pack(first + r)
        across = pack(first + 1 - r)
        ours = [direct] + straight(direct)
        theirs = [swapped(across)] + crossed(across)
        return [x for two in zip(ours, theirs) for x in two]

    blocks_12 = gather_pair(1)
    blocks_34 = gather_pair(3)
    blocks_56 = gather_pair(5)

    width = 2 * TILE
    ext_shape = order + own
    scratch = scratch_for(order, own, width)
    node_macs = width * (2 * order * own + order * order + own * own)
    zero = jnp.int32(0)
    root_ext, corner = call(
        root_kernel, scalars(r, zero), [x for two in zip(root_mine, root_other) for x in two] + sigma_mine + sigma_other,
        [(ext_shape, width), (order - own, order - own)], scratch, 6 * node_macs,
    )
    root_ext_other = swapped(root_ext)
    mid_ext, grand = call(
        middle_kernel, scalars(r, zero), blocks_12 + [root_ext, root_ext_other, corner],
        [(ext_shape, own), (own, own)], scratch, 12 * node_macs,
    )
    mid_ext_other = swapped(mid_ext)

    def leaves(blocks, first):
        node = first + r
        parent = lax.dynamic_index_in_dim(links, node - 3, 0, keepdims=False)
        results = call(
            leaf_kernel, scalars(node - 1, (parent == 1 + r).astype(jnp.int32)),
            blocks + [mid_ext, mid_ext_other, grand],
            [(half + own, TILE)] * 4, scratch + [pltpu.VMEM((order, width), F32), pltpu.VMEM((own, width), F32)],
            6 * node_macs,
        )
        self_out, core_out, end_out, cross_out = results
        return (
            self_out, swapped(core_out), lax.ppermute(end_out, "col", home), lax.ppermute(cross_out, both, home_cross)
        )

    def column(mine, other, node, col):
        if node == 0:
            source = jnp.where(col // 2 == r, mine, other)
            start = (col % 2) * TILE
        else:
            source = jnp.where(r == node - 1, mine, other)
            start = col * TILE
        top = lax.dynamic_slice(source, (r * half, start), (half, TILE))
        return jnp.concatenate([top, lax.dynamic_slice(source, (order, start), (own, TILE))], axis=0)

    def upper(col):
        return jnp.stack([
            column(root_ext, root_ext_other, 0, col), column(mid_ext, mid_ext_other, 1, col),
            column(mid_ext, mid_ext_other, 2, col),
        ])

    is_middle = (c == 1) | (c == 2)
    upper_out = jnp.where(is_middle, upper(c), lax.ppermute(upper(3 * (c // 2)), "col", home))
    pieces = [upper_out[0], upper_out[1], upper_out[2]]
    for blocks, first in ((blocks_34, 3), (blocks_56, 5)):
        self_out, core_out, end_out, cross_out = leaves(blocks, first)
        same = jnp.where(is_middle, self_out, end_out)
        swapped_out = jnp.where(is_middle, core_out, cross_out)
        pieces.append(jnp.where(r == 0, same, swapped_out))
        pieces.append(jnp.where(r == 0, swapped_out, same))
    ancestor_block = jnp.stack([x[:half] for x in pieces])[None]
    diagonal_block = jnp.stack([x[half:] for x in pieces])[None]
    return (ancestor_block, diagonal_block)


def child_blocks(ancestors, products, diagonals, parent_ids, picks, tile):
    count_parents = ancestors.shape[0]
    slot_count = ancestors.shape[1] // tile
    own_width = diagonals.shape[1]
    own_tiles = own_width // tile
    tail = picks[:, own_tiles:]
    living = tail >= 0
    indices = jnp.maximum(tail, 0)
    child_count = tail.shape[0]
    tail_count = tail.shape[1]
    a_tiles = ancestors.reshape(count_parents, slot_count, tile, slot_count, tile)
    corner = a_tiles[parent_ids[:, None, None], indices[:, :, None], :, indices[:, None, :], :]
    corner = jnp.transpose(corner, (0, 1, 3, 2, 4))
    weights = (living[:, :, None] & living[:, None, :]).astype(jnp.float32)
    corner = corner * weights[:, :, None, :, None]
    corner = corner.reshape(child_count, tail_count * tile, tail_count * tile)
    p_tiles = products.reshape(count_parents, slot_count, tile, own_width)
    side = p_tiles[parent_ids[:, None], indices]
    side = side * living.astype(jnp.float32)[:, :, None, None]
    side = side.reshape(child_count, tail_count * tile, own_width)
    top_left = jnp.take(diagonals, parent_ids, axis=0)
    upper = jnp.concatenate([top_left, -jnp.transpose(side, (0, 2, 1))], axis=2)
    lower = jnp.concatenate([-side, corner], axis=2)
    return jnp.concatenate([upper, lower], axis=1)


def body(sigma_top, panels, inverse_diag, slot_lists, parent_links):
    highest = lax.Precision.HIGHEST
    row_count = lax.axis_size("row")
    col_count = lax.axis_size("col")
    row_index = lax.axis_index("row")
    col_index = lax.axis_index("col")
    panel_local = panels[0]
    inverse_local = inverse_diag[0]
    picks_all = slot_lists[0]
    parents = parent_links[0]
    block_rows = panel_local.shape[1]
    block_cols = panel_local.shape[2]
    diag_width = inverse_local.shape[2]
    diag_rows = diag_width // row_count
    tile = TILE
    top_rows = lax.all_gather(sigma_top, ("leaf", "row"), axis=0, tiled=True)
    top_full = lax.all_gather(top_rows, "col", axis=1, tiled=True)
    partial_factor = jnp.einsum("vrk,vkj->vrj", panel_local, inverse_local, precision=highest)
    inverse_band = lax.dynamic_slice_in_dim(inverse_local, row_index * diag_rows, diag_rows, 2)
    partial_gram = jnp.einsum("vki,vkj->vij", inverse_band, inverse_local, precision=highest)
    factor_rows = lax.psum(partial_factor, "col")
    gram_mine = lax.psum_scatter(partial_gram, "col", scatter_dimension=2, tiled=True)
    slots_here = block_rows // tile
    slot_ids = row_index * slots_here + jnp.arange(slots_here, dtype=jnp.int32)
    listed = jnp.take(picks_all, slot_ids, axis=1) >= 0
    living = jnp.concatenate([jnp.ones((1, slots_here), jnp.bool_), listed], axis=0)
    row_weight = jnp.repeat(living.astype(jnp.float32), tile, axis=1)
    factor_rows = factor_rows * row_weight[:, :, None]
    factor_mine = lax.dynamic_slice_in_dim(factor_rows, col_index * block_cols, block_cols, 2)
    factor_cols = lax.all_gather(factor_mine, "row", axis=1, tiled=True)
    ancestors = top_full[None]
    ancestor_parts = []
    diagonal_parts = []
    bounds = ((0, 1), (1, 3), (3, 7))
    for level_id, (first_node, last_node) in enumerate(bounds):
        own_rows = lax.dynamic_slice_in_dim(ancestors, row_index * block_rows, block_rows, 1)
        product_mine = jnp.einsum(
            "vra,vac->vrc", own_rows, factor_cols[first_node:last_node], precision=highest
        )
        partial_diag = jnp.einsum(
            "vrj,vrc->vjc", factor_rows[first_node:last_node], product_mine, precision=highest
        )
        diag_piece = lax.psum_scatter(partial_diag, "row", scatter_dimension=1, tiled=True)
        diag_piece = diag_piece + gram_mine[first_node:last_node]
        ancestor_parts.append(-product_mine)
        if level_id == 2:
            diag_cols = lax.all_gather(diag_piece, "row", axis=1, tiled=True)
        else:
            width_nodes = last_node - first_node
            product_all, diag_all = (
                lax.all_gather(product_mine[:, None], ("row", "col"), axis=1, tiled=True),
                lax.all_gather(diag_piece[:, None], ("row", "col"), axis=1, tiled=True),
            )
            product_full = product_all.reshape(
                width_nodes, row_count, col_count, block_rows, block_cols
            )
            product_full = product_full.transpose(0, 1, 3, 2, 4).reshape(
                width_nodes, row_count * block_rows, col_count * block_cols
            )
            diag_full = diag_all.reshape(width_nodes, row_count, col_count, diag_rows, block_cols)
            diag_full = diag_full.transpose(0, 1, 3, 2, 4).reshape(
                width_nodes, row_count * diag_rows, col_count * block_cols
            )
            diag_cols = lax.dynamic_slice_in_dim(diag_full, col_index * block_cols, block_cols, 2)
            if level_id == 0:
                parent_ids = jnp.zeros((2,), jnp.int32)
                picks_level = picks_all[0:2]
            else:
                parent_ids = parents - 1
                picks_level = picks_all[2:6]
            ancestors = child_blocks(
                ancestors, product_full, diag_full, parent_ids, picks_level, tile
            )
        diagonal_parts.append(diag_cols)
    ancestor_block = jnp.concatenate(ancestor_parts, axis=0)[None]
    diagonal_block = jnp.concatenate(diagonal_parts, axis=0)[None]
    return (ancestor_block, diagonal_block)


def solution(mesh):
    two_middles = (mesh.shape["leaf"], mesh.shape["row"], mesh.shape["col"]) == (4, 2, 4)
    return jax.shard_map(
        chip_body if two_middles else body,
        mesh=mesh,
        in_specs=(
            P(("leaf", "row"), "col"),
            P("leaf", None, "row", "col"),
            P("leaf", None, "col", None),
            P("leaf", None, None),
            P("leaf", None),
        ),
        out_specs=(P("leaf", None, "row", "col"), P("leaf", None, None, "col")),
        check_vma=False,
    )
```

```python
import functools

import jax
import jax.numpy as jnp
from jax import lax
from jax.experimental import pallas as pl
from jax.experimental.pallas import tpu as pltpu
from jax.sharding import PartitionSpec as P

TILE = 128
STEP = 2 * TILE
QUARTER = TILE // 2
F32 = jnp.float32
BF16 = jnp.bfloat16
VMEM_LIMIT = 56 * 2**20
WHOLE = pl.BlockSpec(memory_space=pltpu.VMEM)
ANY = pl.BlockSpec(memory_space=pl.ANY)


def split(x):
    high = x.astype(BF16)
    return high, (x - high.astype(F32)).astype(BF16)


def dot3(a, b, contract):
    dims = (((contract,), (0,)), ((), ()))
    dot = functools.partial(lax.dot_general, dimension_numbers=dims, preferred_element_type=F32)
    return dot(a[0], b[0]) + (dot(a[0], b[1]) + dot(a[1], b[0]))


def put(pair, index, value):
    high, low = split(value)
    pair[0][index] = high
    pair[1][index] = low


def get(pair, index):
    return pair[0][index], pair[1][index]


def at(start, size, unit=TILE):
    return pl.ds(pl.multiple_of(start, unit), size)


def tiles(size, step=STEP):
    return [slice(m, m + step) for m in range(0, size, step)]


ALL = slice(None)


def load_panels(blocks, r, p, d, half):
    for slot in range(4):
        for turn in range(2):
            ref = blocks[2 * slot + turn]
            side = r if turn == 0 else 1 - r
            put(p, (at(side * half, half), slice(slot * TILE, (slot + 1) * TILE)), ref[0:half, :])
            for j in range(4):
                rows = at(slot * TILE + side * QUARTER, QUARTER, QUARTER)
                place = slice(j * TILE, (j + 1) * TILE)
                put(d, (rows, place), ref[half + j * QUARTER:half + (j + 1) * QUARTER, :])


def solve(p, d, a, dc, f, w, t, weights, emit_ab, emit_dg, join=None):
    width = dc[0].shape[1]
    for rows in tiles(p[0].shape[0]):
        k = rows.start // TILE
        for cols in tiles(width):
            value = dot3(get(p, (rows, ALL)), get(dc, (ALL, cols)), 1)
            value = jnp.concatenate([value[:TILE] * weights[k], value[TILE:] * weights[k + 1]], axis=0)
            put(f, (rows, cols), value)
    if join is not None:
        join()
    for cols in tiles(width):
        for rows in tiles(a[0].shape[0]):
            value = dot3(get(a, (rows, ALL)), get(f, (ALL, cols)), 1)
            emit_ab(rows, cols, -value)
            put(w, (rows, cols), value)
        for rows in tiles(d[0].shape[0]):
            value = dot3(get(p, (ALL, rows)), get(w, (ALL, cols)), 0)
            put(t, (rows, cols), value + dc[0][rows, cols].astype(F32) + dc[1][rows, cols].astype(F32))
        for rows in tiles(d[0].shape[0]):
            emit_dg(rows, cols, dot3(get(d, (ALL, rows)), get(t, (ALL, cols)), 0))


def scratch_pairs(*shapes):
    return [pltpu.VMEM(shape, BF16) for shape in shapes for _ in range(2)]


def pairs(refs):
    return [(refs[i], refs[i + 1]) for i in range(0, len(refs), 2)]


def call(kernel, scalars, operands, outs, scratch, places=None, out_place=WHOLE, micros=1):
    return pl.pallas_call(
        kernel,
        out_shape=[jax.ShapeDtypeStruct(o, F32) for o in outs],
        in_specs=[pl.BlockSpec(memory_space=pltpu.SMEM)] + (places or [WHOLE] * len(operands)),
        out_specs=[out_place] * len(outs),
        scratch_shapes=scratch,
        compiler_params=pltpu.CompilerParams(vmem_limit_bytes=VMEM_LIMIT),
        cost_estimate=pl.CostEstimate(flops=micros * 10**9, bytes_accessed=1, transcendentals=0),
    )(scalars, *operands)


def copy_all(copies, sems):
    started = [pltpu.make_async_copy(src, dst, sems.at[i]) for i, (src, dst) in enumerate(copies)]
    for one in started:
        one.start()
    for one in started:
        one.wait()


def move(kernel, scalars, operands, outs, count):
    return call(
        kernel, scalars, operands, outs, [pltpu.SemaphoreType.DMA((count,))], [ANY] * len(operands), ANY
    )


LIST = 4


def tail_of(s, start, own, order):
    spots = [start + k for k in range(own // TILE, order // TILE)]
    return [jnp.maximum(s[k], 0) for k in spots], [(s[k] >= 0).astype(F32) for k in spots]


def weights_of(s, order):
    return [(s[LIST + j] >= 0).astype(F32) for j in range(order // TILE)]


def pack_kernel(s, panels, inverse, *rest):
    outs, sems = rest[:-1], rest[-1]
    half = panels.shape[1]
    copies = []
    node = 0
    for out in outs:
        for i in range(out.shape[0]):
            copies.append((panels.at[node], out.at[i, pl.ds(0, half)]))
            for j in range(inverse.shape[2] // TILE):
                copies.append((
                    inverse.at[node, at(s[0] * QUARTER, QUARTER, QUARTER), pl.ds(j * TILE, TILE)],
                    out.at[i, pl.ds(half + j * QUARTER, QUARTER)],
                ))
            node += 1
    copy_all(copies, sems)


def join_columns_kernel(s, *refs):
    out, sems = refs[-2:]
    width = refs[0].shape[1]
    copy_all([(ref, out.at[:, pl.ds(k * width, width)]) for k, ref in enumerate(refs[:-2])], sems)


def join_rows_kernel(s, *refs):
    out, sems = refs[-2:]
    height = refs[0].shape[0]
    copy_all([(ref, out.at[pl.ds(k * height, height)]) for k, ref in enumerate(refs[:-2])], sems)


def swap_kernel(s, *refs):
    out, sems = refs[-2:]
    copy_all([(ref.at[1 - s[0]], out.at[k]) for k, ref in enumerate(refs[:-2])], sems)


def join_block(a, own, corner, rows_of, top, index, weight):
    put(a, (slice(0, own), slice(0, own)), top)
    for i in range(len(index)):
        place = slice(own + i * TILE, own + (i + 1) * TILE)
        value = rows_of(i) * weight[i]
        put(a, (place, slice(0, own)), value)
        put(a, (slice(0, own), place), value.T)
        for j in range(len(index)):
            put(a, (place, slice(own + j * TILE, own + (j + 1) * TILE)), corner(i, j) * (weight[i] * weight[j]))


def trunk_kernel(s, *refs):
    mine, theirs, sigma_mine, sigma_other = refs[:4], refs[4:8], refs[8], refs[9]
    ext, grand, self_out, end_out = refs[10:14]
    stage, sigma, sems, corners, ab, dg = refs[14:20]
    p, d, a, f, w, t = pairs(refs[20:-1])
    r, c, leaf = s[0], s[1], s[2]
    order = a[0].shape[0]
    own = d[0].shape[0]
    half = order // 2
    far = c // 2
    count = 3

    def fetch(node, slot):
        found = []
        for k in range(4):
            found.append(pltpu.make_async_copy(mine[k].at[node], stage.at[slot, 2 * k], sems.at[slot, 2 * k]))
            found.append(pltpu.make_async_copy(theirs[k].at[node], stage.at[slot, 2 * k + 1], sems.at[slot, 2 * k + 1]))
        return found

    sigma_copies = [
        pltpu.make_async_copy(ref, sigma.at[k], sems.at[2, k]) for k, ref in enumerate((sigma_mine, sigma_other))
    ]
    for one in fetch(0, 0) + sigma_copies + fetch(1, 1):
        one.start()

    def panels_of(node, slot):
        for one in fetch(node, slot):
            one.wait()
        load_panels([stage.at[slot, k] for k in range(8)], r, p, d, half)

    def emit_ab(rows, cols, value):
        ab[rows, cols] = value

    def emit_dg(rows, cols, value):
        dg[rows, cols] = value

    def columns_out(node):
        for out, col in ((self_out, c), (end_out, 3 * far)):
            out[node, 0:half, :] = ab[at(r * half, half), at(col * TILE, TILE)]
            out[node, half:, :] = dg[:, at(col * TILE, TILE)]

    panels_of(0, 0)

    def join_root():
        places = (c, 3 * far, 3 - c, 3 - 3 * far)
        span = order // 4
        for one in sigma_copies:
            one.wait()
        for m in range(4):
            for turn in range(2):
                side = r if turn == 0 else 1 - r
                rows = at(((leaf ^ m) * 2 + side) * TILE, TILE)
                for k in range(4):
                    value = sigma[turn, m * TILE:(m + 1) * TILE, k * span:(k + 1) * span]
                    put(a, (rows, at(places[k] * span, span)), value)

    solve(p, d, a, d, f, w, t, [1.0] * (order // TILE), emit_ab, emit_dg, join_root)
    columns_out(0)
    grand[...] = dg[...]
    for node in (1, 2):
        index, weight = tail_of(s, LIST + (node - 1) * (order // TILE), own, order)
        for i in range(len(index)):
            for j in range(len(index)):
                high, low = get(a, (at(index[i] * TILE, TILE), at(index[j] * TILE, TILE)))
                value = high.astype(F32) + low.astype(F32)
                corners[node - 1, i * TILE:(i + 1) * TILE, j * TILE:(j + 1) * TILE] = value
    for one in fetch(2, 0):
        one.start()
    root_ab = refs[-1]
    root_ab[...] = ab[...]

    @pl.loop(1, count)
    def _(node):
        start = LIST + (node - 1) * (order // TILE)
        index, weight = tail_of(s, start, own, order)
        panels_of(node, node % 2)

        def join():
            join_block(
                a, own,
                lambda i, j: corners[node - 1, i * TILE:(i + 1) * TILE, j * TILE:(j + 1) * TILE],
                lambda i: root_ab[at(index[i] * TILE, TILE), :], grand[...], index, weight,
            )

        weights = [(s[start + k] >= 0).astype(F32) for k in range(order // TILE)]
        solve(p, d, a, d, f, w, t, weights, emit_ab, emit_dg, join)
        columns_out(node)
        ext[node - 1, 0:half, :] = ab[0:half, :]
        ext[node - 1, half:, :] = dg[...]


def leaf_kernel(s, x0, x1, x2, x3, ex, ext, grand, self_out, core_out, end_out, cross_out, *rest):
    stage, sems, tails, top, grand_in, ab, dg = rest[:7]
    p, d, a, dc, f, w, t = pairs(rest[7:])
    r, c = s[0], s[1]
    order = a[0].shape[0]
    own = d[0].shape[0]
    half = order // 2
    far = c // 2
    index, weight = tail_of(s, LIST, own, order)
    parent = s[3] - 1
    copies = []
    for k, ref in enumerate((x0, x1, x2, x3)):
        copies.append(pltpu.make_async_copy(ref.at[r], stage.at[2 * k], sems.at[2 * k]))
        copies.append(pltpu.make_async_copy(ex.at[k], stage.at[2 * k + 1], sems.at[2 * k + 1]))
    later = [
        pltpu.make_async_copy(ext.at[parent, pl.ds(half, own)], top, sems.at[8]),
        pltpu.make_async_copy(grand, grand_in, sems.at[9]),
    ]
    for j, pick in enumerate(index):
        later.append(pltpu.make_async_copy(ext.at[parent, at(pick * TILE, TILE)], tails.at[j], sems.at[10 + j]))
    for one in copies + later:
        one.start()
    for one in copies:
        one.wait()
    load_panels([stage.at[k] for k in range(8)], r, p, d, half)
    dc[0][...] = d[0][:, at(far * STEP, STEP)]
    dc[1][...] = d[1][:, at(far * STEP, STEP)]

    def join():
        for one in later:
            one.wait()
        join_block(
            a, own, lambda i, j: grand_in[at(index[i] * TILE, TILE), at(index[j] * TILE, TILE)], lambda i: tails[i],
            top[...], index, weight,
        )

    def emit_ab(rows, cols, value):
        ab[rows, cols] = value

    def emit_dg(rows, cols, value):
        dg[rows, cols] = value

    solve(p, d, a, dc, f, w, t, weights_of(s, order), emit_ab, emit_dg, join)
    near_cols, end_cols = at((1 - far) * TILE, TILE), at(far * TILE, TILE)
    for out, side, cols in (
        (self_out, r, near_cols), (core_out, 1 - r, near_cols), (end_out, r, end_cols), (cross_out, 1 - r, end_cols)
    ):
        out[0:half, :] = ab[at(side * half, half), cols]
        out[half:, :] = dg[:, cols]


def output_kernel(s, *refs):
    ab, dg, sems = refs[-3:]
    r, c = s[0], s[1]
    half = ab.shape[1]
    middle = (c == 1) | (c == 2)
    for core in range(2):
        for inner in range(2):
            @pl.when((r == core) & (middle == (inner == 1)))
            def _():
                upper = refs[0] if inner else refs[1]
                found = [upper.at[k] for k in range(3)]
                for start in (2, 6):
                    self_ref, core_ref, end_ref, cross_ref = refs[start:start + 4]
                    same, swapped = (self_ref, core_ref) if inner else (end_ref, cross_ref)
                    found += [same, swapped] if core == 0 else [swapped, same]
                copies = []
                for node, ref in enumerate(found):
                    copies.append((ref.at[pl.ds(0, half)], ab.at[node]))
                    copies.append((ref.at[pl.ds(half, half)], dg.at[node]))
                copy_all(copies, sems)


def after(x, earlier):
    return lax.optimization_barrier((x, earlier))[0]


def chip_body(sigma_top, panels, inverse_diag, slot_lists, parent_links):
    r = lax.axis_index("row")
    c = lax.axis_index("col")
    leaf = lax.axis_index("leaf")
    panels, inverse, lists, links = panels[0], inverse_diag[0], slot_lists[0], parent_links[0]
    half = panels.shape[1]
    order = 2 * half
    own = inverse.shape[2]
    both = ("row", "col")
    routes = (((0, 1), (3, 2)), ((1, 2), (2, 1)), ((0, 2), (3, 1)))
    middles = (1, 2)
    swap = [(row * 4 + a, (1 - row) * 4 + a) for row in range(2) for a in middles]
    home = ((1, 0), (2, 3))
    home_cross = [(row * 4 + a, (1 - row) * 4 + b) for row in range(2) for a, b in home]
    leaf_routes = [
        [((lf * 2 + row) * 4 + a, ((lf ^ m) * 2 + row) * 4 + a) for lf in range(4) for row in range(2) for a in middles]
        for m in range(4)
    ]

    def straight(x):
        return [x] + [lax.ppermute(x, "col", route) for route in routes]

    def swapped(x):
        return lax.ppermute(x, both, swap)

    def scalars(parent, *rows):
        head = jnp.stack([r, c, leaf, parent]).astype(jnp.int32)
        return jnp.concatenate([head] + [lists[row] for row in rows])

    trunk = 3
    here = scalars(jnp.int32(0), 0, 1)
    packed = half + own // 2
    sigma_parts = straight(sigma_top)
    pack_t, pack_34, pack_56 = move(
        pack_kernel, here, [panels, inverse], [(k, packed, TILE) for k in (trunk, 2, 2)], 35
    )
    blocks_t = straight(pack_t)
    sigma_cols = move(join_columns_kernel, here, after(sigma_parts, pack_t), [(TILE, order)], 4)[0]
    sigma_rows = [sigma_cols] + [
        lax.ppermute(sigma_cols, ("leaf", "row", "col"), leaf_routes[m]) for m in range(1, 4)
    ]
    sigma_mine = move(join_rows_kernel, here, sigma_rows, [(half, order)], 4)[0]
    sigma_other = swapped(sigma_mine)
    other_t = [swapped(x) for x in blocks_t]
    blocks_34 = straight(after(pack_34, blocks_t[1:]))
    ext, grand, upper_self, upper_end = call(
        trunk_kernel, here, blocks_t + other_t + [sigma_mine, sigma_other],
        [(2, half + own, own), (own, own)] + [(trunk, half + own, TILE)] * 2,
        [
            pltpu.VMEM((2, 8, packed, TILE), F32), pltpu.VMEM((2, half, order), F32), pltpu.SemaphoreType.DMA((3, 8)),
            pltpu.VMEM((2, order - own, order - own), F32), pltpu.VMEM((order, own), F32), pltpu.VMEM((own, own), F32),
        ] + scratch_pairs((order, own), (own, own), (order, order), (order, own), (order, own), (own, own))
        + [pltpu.VMEM((order, own), F32)],
        [ANY] * 10, micros=60,
    )
    blocks_56 = straight(after(pack_56, (blocks_34[1:], ext)))
    pieces = [upper_self, lax.ppermute(upper_end, "col", home)]
    tails = (order - own) // TILE
    ready = ext
    for blocks, first in ((blocks_34, 3), (blocks_56, 5)):
        node = first + r
        parent = lax.dynamic_index_in_dim(links, node - 3, 0, keepdims=False)
        theirs = swapped(move(swap_kernel, here, after(blocks, ready), [(4, packed, TILE)], 4)[0])
        if first == 5:
            theirs = after(theirs, pieces[1])
        self_out, core_out, end_out, cross_out = call(
            leaf_kernel, scalars(parent, node - 1), blocks + [theirs, ext, grand], [(half + own, TILE)] * 4,
            [
                pltpu.VMEM((8, packed, TILE), F32), pltpu.SemaphoreType.DMA((10 + tails,)),
                pltpu.VMEM((tails, TILE, own), F32), pltpu.VMEM((own, own), F32), pltpu.VMEM((own, own), F32),
                pltpu.VMEM((order, STEP), F32), pltpu.VMEM((own, STEP), F32),
            ] + scratch_pairs(
                (order, own), (own, own), (order, order), (own, STEP), (order, STEP), (order, STEP), (own, STEP)
            ),
            [ANY] * 7, micros=10,
        )
        ready = self_out
        pieces += [
            self_out, swapped(core_out), lax.ppermute(end_out, "col", home), lax.ppermute(cross_out, both, home_cross)
        ]
    count = panels.shape[0]
    ancestor_block, diagonal_block = move(
        output_kernel, here, pieces, [(count, half, TILE), (count, own, TILE)], 2 * count
    )
    return (ancestor_block[None], diagonal_block[None])


def child_blocks(ancestors, products, diagonals, parent_ids, picks, tile):
    count_parents = ancestors.shape[0]
    slot_count = ancestors.shape[1] // tile
    own_width = diagonals.shape[1]
    own_tiles = own_width // tile
    tail = picks[:, own_tiles:]
    living = tail >= 0
    indices = jnp.maximum(tail, 0)
    child_count = tail.shape[0]
    tail_count = tail.shape[1]
    a_tiles = ancestors.reshape(count_parents, slot_count, tile, slot_count, tile)
    corner = a_tiles[parent_ids[:, None, None], indices[:, :, None], :, indices[:, None, :], :]
    corner = jnp.transpose(corner, (0, 1, 3, 2, 4))
    weights = (living[:, :, None] & living[:, None, :]).astype(jnp.float32)
    corner = corner * weights[:, :, None, :, None]
    corner = corner.reshape(child_count, tail_count * tile, tail_count * tile)
    p_tiles = products.reshape(count_parents, slot_count, tile, own_width)
    side = p_tiles[parent_ids[:, None], indices]
    side = side * living.astype(jnp.float32)[:, :, None, None]
    side = side.reshape(child_count, tail_count * tile, own_width)
    top_left = jnp.take(diagonals, parent_ids, axis=0)
    upper = jnp.concatenate([top_left, -jnp.transpose(side, (0, 2, 1))], axis=2)
    lower = jnp.concatenate([-side, corner], axis=2)
    return jnp.concatenate([upper, lower], axis=1)


def body(sigma_top, panels, inverse_diag, slot_lists, parent_links):
    highest = lax.Precision.HIGHEST
    row_count = lax.axis_size("row")
    col_count = lax.axis_size("col")
    row_index = lax.axis_index("row")
    col_index = lax.axis_index("col")
    panel_local = panels[0]
    inverse_local = inverse_diag[0]
    picks_all = slot_lists[0]
    parents = parent_links[0]
    block_rows = panel_local.shape[1]
    block_cols = panel_local.shape[2]
    diag_width = inverse_local.shape[2]
    diag_rows = diag_width // row_count
    tile = TILE
    top_rows = lax.all_gather(sigma_top, ("leaf", "row"), axis=0, tiled=True)
    top_full = lax.all_gather(top_rows, "col", axis=1, tiled=True)
    partial_factor = jnp.einsum("vrk,vkj->vrj", panel_local, inverse_local, precision=highest)
    inverse_band = lax.dynamic_slice_in_dim(inverse_local, row_index * diag_rows, diag_rows, 2)
    partial_gram = jnp.einsum("vki,vkj->vij", inverse_band, inverse_local, precision=highest)
    factor_rows = lax.psum(partial_factor, "col")
    gram_mine = lax.psum_scatter(partial_gram, "col", scatter_dimension=2, tiled=True)
    slots_here = block_rows // tile
    slot_ids = row_index * slots_here + jnp.arange(slots_here, dtype=jnp.int32)
    listed = jnp.take(picks_all, slot_ids, axis=1) >= 0
    living = jnp.concatenate([jnp.ones((1, slots_here), jnp.bool_), listed], axis=0)
    row_weight = jnp.repeat(living.astype(jnp.float32), tile, axis=1)
    factor_rows = factor_rows * row_weight[:, :, None]
    factor_mine = lax.dynamic_slice_in_dim(factor_rows, col_index * block_cols, block_cols, 2)
    factor_cols = lax.all_gather(factor_mine, "row", axis=1, tiled=True)
    ancestors = top_full[None]
    ancestor_parts = []
    diagonal_parts = []
    bounds = ((0, 1), (1, 3), (3, 7))
    for level_id, (first_node, last_node) in enumerate(bounds):
        own_rows = lax.dynamic_slice_in_dim(ancestors, row_index * block_rows, block_rows, 1)
        product_mine = jnp.einsum(
            "vra,vac->vrc", own_rows, factor_cols[first_node:last_node], precision=highest
        )
        partial_diag = jnp.einsum(
            "vrj,vrc->vjc", factor_rows[first_node:last_node], product_mine, precision=highest
        )
        diag_piece = lax.psum_scatter(partial_diag, "row", scatter_dimension=1, tiled=True)
        diag_piece = diag_piece + gram_mine[first_node:last_node]
        ancestor_parts.append(-product_mine)
        if level_id == 2:
            diag_cols = lax.all_gather(diag_piece, "row", axis=1, tiled=True)
        else:
            width_nodes = last_node - first_node
            product_all, diag_all = (
                lax.all_gather(product_mine[:, None], ("row", "col"), axis=1, tiled=True),
                lax.all_gather(diag_piece[:, None], ("row", "col"), axis=1, tiled=True),
            )
            product_full = product_all.reshape(
                width_nodes, row_count, col_count, block_rows, block_cols
            )
            product_full = product_full.transpose(0, 1, 3, 2, 4).reshape(
                width_nodes, row_count * block_rows, col_count * block_cols
            )
            diag_full = diag_all.reshape(width_nodes, row_count, col_count, diag_rows, block_cols)
            diag_full = diag_full.transpose(0, 1, 3, 2, 4).reshape(
                width_nodes, row_count * diag_rows, col_count * block_cols
            )
            diag_cols = lax.dynamic_slice_in_dim(diag_full, col_index * block_cols, block_cols, 2)
            if level_id == 0:
                parent_ids = jnp.zeros((2,), jnp.int32)
                picks_level = picks_all[0:2]
            else:
                parent_ids = parents - 1
                picks_level = picks_all[2:6]
            ancestors = child_blocks(
                ancestors, product_full, diag_full, parent_ids, picks_level, tile
            )
        diagonal_parts.append(diag_cols)
    ancestor_block = jnp.concatenate(ancestor_parts, axis=0)[None]
    diagonal_block = jnp.concatenate(diagonal_parts, axis=0)[None]
    return (ancestor_block, diagonal_block)


def solution(mesh):
    two_middles = (mesh.shape["leaf"], mesh.shape["row"], mesh.shape["col"]) == (4, 2, 4)
    return jax.shard_map(
        chip_body if two_middles else body,
        mesh=mesh,
        in_specs=(
            P(("leaf", "row"), "col"),
            P("leaf", None, "row", "col"),
            P("leaf", None, "col", None),
            P("leaf", None, None),
            P("leaf", None),
        ),
        out_specs=(P("leaf", None, "row", "col"), P("leaf", None, None, "col")),
        check_vma=False,
    )
```

```python
import functools

import jax
import jax.numpy as jnp
from jax import lax
from jax.experimental import pallas as pl
from jax.experimental.pallas import tpu as pltpu
from jax.sharding import PartitionSpec as P

TILE = 128
STEP = 2 * TILE
QUARTER = TILE // 2
F32 = jnp.float32
BF16 = jnp.bfloat16
VMEM_LIMIT = 56 * 2**20
WHOLE = pl.BlockSpec(memory_space=pltpu.VMEM)
ANY = pl.BlockSpec(memory_space=pl.ANY)


def split(x):
    high = x.astype(BF16)
    return high, (x - high.astype(F32)).astype(BF16)


def dot3(a, b):
    dot = functools.partial(jnp.dot, preferred_element_type=F32)
    return dot(a[0], b[0]) + (dot(a[0], b[1]) + dot(a[1], b[0]))


def put(pair, index, value):
    high, low = split(value)
    pair[0][index] = high
    pair[1][index] = low


def get(pair, index):
    return pair[0][index], pair[1][index]


def at(start, size, unit=TILE):
    return pl.ds(pl.multiple_of(start, unit), size)


def tiles(size, step=STEP):
    return [slice(m, m + step) for m in range(0, size, step)]


ALL = slice(None)


def load_panels(blocks, r, p, d, pt, dt, half):
    for slot in range(4):
        for turn in range(2):
            ref = blocks[2 * slot + turn]
            side = r if turn == 0 else 1 - r
            panel = ref[0:half, :]
            put(p, (at(side * half, half), slice(slot * TILE, (slot + 1) * TILE)), panel)
            put(pt, (slice(slot * TILE, (slot + 1) * TILE), at(side * half, half)), panel.T)
            for j in range(4):
                rows = at(slot * TILE + side * QUARTER, QUARTER, QUARTER)
                place = slice(j * TILE, (j + 1) * TILE)
                put(d, (rows, place), ref[half + j * QUARTER:half + (j + 1) * QUARTER, :])
    for slot in range(4):
        for j in range(4):
            rows, cols = slice(slot * TILE, (slot + 1) * TILE), slice(j * TILE, (j + 1) * TILE)
            for whole, turned in zip(d, dt):
                turned[cols, rows] = whole[rows, cols].T


def solve(p, pt, dt, a, dc, f, w, t, weights, emit_ab, emit_dg, join):
    width = dc[0].shape[1]
    for rows in tiles(p[0].shape[0]):
        k = rows.start // TILE
        for cols in tiles(width):
            value = dot3(get(p, (rows, ALL)), get(dc, (ALL, cols)))
            value = jnp.concatenate([value[:TILE] * weights[k], value[TILE:] * weights[k + 1]], axis=0)
            put(f, (rows, cols), value)
    join()
    for cols in tiles(width):
        for rows in tiles(a[0].shape[0]):
            value = dot3(get(a, (rows, ALL)), get(f, (ALL, cols)))
            emit_ab(rows, cols, -value)
            put(w, (rows, cols), value)
        for rows in tiles(pt[0].shape[0]):
            value = dot3(get(pt, (rows, ALL)), get(w, (ALL, cols)))
            put(t, (rows, cols), value + dc[0][rows, cols].astype(F32) + dc[1][rows, cols].astype(F32))
        for rows in tiles(dt[0].shape[0]):
            emit_dg(rows, cols, dot3(get(dt, (rows, ALL)), get(t, (ALL, cols))))


def scratch_pairs(*shapes):
    return [pltpu.VMEM(shape, BF16) for shape in shapes for _ in range(2)]


def pairs(refs):
    return [(refs[i], refs[i + 1]) for i in range(0, len(refs), 2)]


def call(kernel, scalars, operands, outs, scratch, places=None, micros=1):
    return pl.pallas_call(
        kernel,
        out_shape=[jax.ShapeDtypeStruct(o, F32) for o in outs],
        in_specs=[pl.BlockSpec(memory_space=pltpu.SMEM)] + (places or [WHOLE] * len(operands)),
        out_specs=[WHOLE] * len(outs),
        scratch_shapes=scratch,
        compiler_params=pltpu.CompilerParams(vmem_limit_bytes=VMEM_LIMIT),
        cost_estimate=pl.CostEstimate(flops=micros * 10**9, bytes_accessed=1, transcendentals=0),
    )(scalars, *operands)


def copy_all(copies, sems):
    started = [pltpu.make_async_copy(src, dst, sems.at[i]) for i, (src, dst) in enumerate(copies)]
    for one in started:
        one.start()
    for one in started:
        one.wait()


def move(kernel, scalars, operands, outs, count, micros=1):
    return call(
        kernel, scalars, operands, outs, [pltpu.SemaphoreType.DMA((count,))], [ANY] * len(operands), micros
    )


LIST = 4


def tail_of(s, start, own, order):
    spots = [start + k for k in range(own // TILE, order // TILE)]
    return [jnp.maximum(s[k], 0) for k in spots], [(s[k] >= 0).astype(F32) for k in spots]


def weights_of(s, order):
    return [(s[LIST + j] >= 0).astype(F32) for j in range(order // TILE)]


def pack_kernel(s, panels, inverse, *rest):
    outs, sems = rest[:-1], rest[-1]
    half = panels.shape[1]
    copies = []
    node = 0
    for out in outs:
        for i in range(out.shape[0]):
            copies.append((panels.at[node], out.at[i, pl.ds(0, half)]))
            for j in range(inverse.shape[2] // TILE):
                copies.append((
                    inverse.at[node, at(s[0] * QUARTER, QUARTER, QUARTER), pl.ds(j * TILE, TILE)],
                    out.at[i, pl.ds(half + j * QUARTER, QUARTER)],
                ))
            node += 1
    copy_all(copies, sems)


def join_columns_kernel(s, *refs):
    out, sems = refs[-2:]
    width = refs[0].shape[1]
    copy_all([(ref, out.at[:, pl.ds(k * width, width)]) for k, ref in enumerate(refs[:-2])], sems)


def stack_kernel(s, *refs):
    out, sems = refs[-2:]
    copy_all([(ref, out.at[k]) for k, ref in enumerate(refs[:-2])], sems)


def swap_kernel(s, *refs):
    out, sems = refs[-2:]
    copy_all([(ref.at[1 - s[0]], out.at[k]) for k, ref in enumerate(refs[:-2])], sems)


def join_block(a, own, corner, rows_of, top, index, weight):
    put(a, (slice(0, own), slice(0, own)), top)
    for i in range(len(index)):
        place = slice(own + i * TILE, own + (i + 1) * TILE)
        value = rows_of(i) * weight[i]
        put(a, (place, slice(0, own)), value)
        put(a, (slice(0, own), place), value.T)
        for j in range(len(index)):
            put(a, (place, slice(own + j * TILE, own + (j + 1) * TILE)), corner(i, j) * (weight[i] * weight[j]))


def trunk_kernel(s, *refs):
    mine, theirs, sigmas = refs[:4], refs[4], refs[5:10]
    ext, grand, self_out, end_out = refs[10:14]
    stage, sigma, sems, corners, ab, dg = refs[14:20]
    p, d, a, f, w, t, pt, dt = pairs(refs[20:-1])
    r, c, leaf = s[0], s[1], s[2]
    order = a[0].shape[0]
    own = d[0].shape[0]
    half = order // 2
    far = c // 2
    count = 3

    def fetch(node, slot):
        found = []
        for k in range(4):
            found.append(pltpu.make_async_copy(mine[k].at[node], stage.at[slot, 2 * k], sems.at[slot, 2 * k]))
            found.append(pltpu.make_async_copy(theirs.at[k, node], stage.at[slot, 2 * k + 1], sems.at[slot, 2 * k + 1]))
        return found

    sigma_copies = [
        pltpu.make_async_copy(ref, sigma.at[k], sems.at[2, k])
        for k, ref in enumerate(list(sigmas[:4]) + [sigmas[4].at[m] for m in range(4)])
    ]
    for one in fetch(0, 0) + sigma_copies + fetch(1, 1):
        one.start()

    def panels_of(node, slot):
        for one in fetch(node, slot):
            one.wait()
        load_panels([stage.at[slot, k] for k in range(8)], r, p, d, pt, dt, half)

    def emit_ab(rows, cols, value):
        ab[rows, cols] = value

    def emit_dg(rows, cols, value):
        dg[rows, cols] = value

    def columns_out(node):
        for out, col in ((self_out, c), (end_out, 3 * far)):
            out[node, 0:half, :] = ab[at(r * half, half), at(col * TILE, TILE)]
        self_out[node, half:, :] = dg[:, at(c * TILE, TILE)]
        end_out[node, half:, :] = dg[at(r * (own // 2), own // 2), at(3 * far * TILE, TILE)]

    panels_of(0, 0)

    def join_root():
        places = (c, 3 * far, 3 - c, 3 - 3 * far)
        span = order // 4
        for one in sigma_copies:
            one.wait()
        for m in range(4):
            for turn in range(2):
                side = r if turn == 0 else 1 - r
                rows = at(((leaf ^ m) * 2 + side) * TILE, TILE)
                for k in range(4):
                    value = sigma[4 * turn + m, :, k * span:(k + 1) * span]
                    put(a, (rows, at(places[k] * span, span)), value)

    solve(p, pt, dt, a, d, f, w, t, [1.0] * (order // TILE), emit_ab, emit_dg, join_root)
    columns_out(0)
    grand[...] = dg[...]
    for node in (1, 2):
        index, weight = tail_of(s, LIST + (node - 1) * (order // TILE), own, order)
        for i in range(len(index)):
            for j in range(len(index)):
                high, low = get(a, (at(index[i] * TILE, TILE), at(index[j] * TILE, TILE)))
                value = high.astype(F32) + low.astype(F32)
                corners[node - 1, i * TILE:(i + 1) * TILE, j * TILE:(j + 1) * TILE] = value
    for one in fetch(2, 0):
        one.start()
    root_ab = refs[-1]
    root_ab[...] = ab[...]

    @pl.loop(1, count)
    def _(node):
        start = LIST + (node - 1) * (order // TILE)
        index, weight = tail_of(s, start, own, order)
        panels_of(node, node % 2)

        def join():
            join_block(
                a, own,
                lambda i, j: corners[node - 1, i * TILE:(i + 1) * TILE, j * TILE:(j + 1) * TILE],
                lambda i: root_ab[at(index[i] * TILE, TILE), :], grand[...], index, weight,
            )

        weights = [(s[start + k] >= 0).astype(F32) for k in range(order // TILE)]
        solve(p, pt, dt, a, d, f, w, t, weights, emit_ab, emit_dg, join)
        columns_out(node)
        ext[node - 1, 0:half, :] = ab[0:half, :]
        ext[node - 1, half:, :] = dg[...]


def leaf_kernel(s, x0, x1, x2, x3, ex, ext, grand, self_out, core_out, end_out, cross_out, *rest):
    stage, sems, tails, top, grand_in, ab, dg = rest[:7]
    p, d, a, dc, f, w, t, pt, dt = pairs(rest[7:])
    r, c = s[0], s[1]
    blocks = [x for k, ref in enumerate((x0, x1, x2, x3)) for x in (ref.at[r], ex.at[k])]
    order = a[0].shape[0]
    own = d[0].shape[0]
    half = order // 2
    far = c // 2
    index, weight = tail_of(s, LIST, own, order)
    parent = s[3] - 1
    copies = [pltpu.make_async_copy(ref, stage.at[k], sems.at[k]) for k, ref in enumerate(blocks)]
    later = [
        pltpu.make_async_copy(ext.at[parent, pl.ds(half, own)], top, sems.at[8]),
        pltpu.make_async_copy(grand, grand_in, sems.at[9]),
    ]
    for j, pick in enumerate(index):
        later.append(pltpu.make_async_copy(ext.at[parent, at(pick * TILE, TILE)], tails.at[j], sems.at[10 + j]))
    for one in copies + later:
        one.start()
    for one in copies:
        one.wait()
    load_panels([stage.at[k] for k in range(8)], r, p, d, pt, dt, half)
    dc[0][...] = d[0][:, at(far * STEP, STEP)]
    dc[1][...] = d[1][:, at(far * STEP, STEP)]

    def join():
        for one in later:
            one.wait()
        join_block(
            a, own, lambda i, j: grand_in[at(index[i] * TILE, TILE), at(index[j] * TILE, TILE)], lambda i: tails[i],
            top[...], index, weight,
        )

    def emit_ab(rows, cols, value):
        ab[rows, cols] = value

    def emit_dg(rows, cols, value):
        dg[rows, cols] = value

    solve(p, pt, dt, a, dc, f, w, t, weights_of(s, order), emit_ab, emit_dg, join)
    near_cols, end_cols = at((1 - far) * TILE, TILE), at(far * TILE, TILE)
    for out, side, cols in (
        (self_out, r, near_cols), (core_out, 1 - r, near_cols), (end_out, r, end_cols), (cross_out, 1 - r, end_cols)
    ):
        out[0:half, :] = ab[at(side * half, half), cols]
        share = out.shape[0] - half
        out[half:, :] = dg[:, cols] if share == own else dg[at(side * share, share), cols]


def shares_kernel(s, upper, end, cross, core, out, sems):
    c = s[1]
    middle = (c == 1) | (c == 2)
    half = core.shape[0] // 2
    share = upper.shape[1] - half

    @pl.when(middle)
    def _():
        copy_all([(core, out.at[pl.ds(0, 2 * half)])], sems)

    @pl.when(jnp.logical_not(middle))
    def _():
        found = [upper.at[k] for k in range(3)] + [end, cross]
        copy_all([
            (ref.at[pl.ds(half, share)], out.at[pl.ds(k * share, share)]) for k, ref in enumerate(found)
        ], sems)


def output_kernel(s, *refs):
    upper_self, upper_end, self_34, end_34, cross_34, shares, self_56, core_56, end_56, cross_56 = refs[:10]
    ab, dg, sems = refs[-3:]
    r, c = s[0], s[1]
    half = ab.shape[1]
    share = half // 2
    middle = (c == 1) | (c == 2)
    for core in range(2):
        @pl.when((r == core) & middle)
        def _():
            pair = [self_34, shares] if core == 0 else [shares, self_34]
            last = [self_56, core_56] if core == 0 else [core_56, self_56]
            copies = []
            for node, ref in enumerate([upper_self.at[k] for k in range(3)] + pair + last):
                copies.append((ref.at[pl.ds(0, half)], ab.at[node]))
                copies.append((ref.at[pl.ds(half, half)], dg.at[node]))
            copy_all(copies, sems)

        @pl.when((r == core) & jnp.logical_not(middle))
        def _():
            same, swapped = (3, 4) if core == 0 else (4, 3)
            last = [end_56, cross_56] if core == 0 else [cross_56, end_56]
            copies = []
            for node, ref, k in [(k, upper_end.at[k], k) for k in range(3)] + [(same, end_34, 4), (swapped, cross_34, 3)]:
                copies.append((ref.at[pl.ds(0, half)], ab.at[node]))
                copies.append((ref.at[pl.ds(half, share)], dg.at[node, pl.ds(core * share, share)]))
                copies.append((shares.at[pl.ds(k * share, share)], dg.at[node, pl.ds((1 - core) * share, share)]))
            for node, ref in ((5, last[0]), (6, last[1])):
                copies.append((ref.at[pl.ds(0, half)], ab.at[node]))
                copies.append((ref.at[pl.ds(half, half)], dg.at[node]))
            copy_all(copies, sems)


def after(x, earlier):
    return lax.optimization_barrier((x, earlier))[0]


def chip_body(sigma_top, panels, inverse_diag, slot_lists, parent_links):
    r = lax.axis_index("row")
    c = lax.axis_index("col")
    leaf = lax.axis_index("leaf")
    panels, inverse, lists, links = panels[0], inverse_diag[0], slot_lists[0], parent_links[0]
    half = panels.shape[1]
    order = 2 * half
    own = inverse.shape[2]
    both = ("row", "col")
    routes = (((0, 1), (3, 2)), ((1, 2), (2, 1)), ((0, 2), (3, 1)))
    middles = (1, 2)
    swap = [(row * 4 + a, (1 - row) * 4 + a) for row in range(2) for a in middles]
    swap_all = [(row * 4 + a, (1 - row) * 4 + a) for row in range(2) for a in range(4)]
    home = ((1, 0), (2, 3))
    home_cross = [(row * 4 + a, (1 - row) * 4 + b) for row in range(2) for a, b in home]
    leaf_routes = [
        [((lf * 2 + row) * 4 + a, ((lf ^ m) * 2 + row) * 4 + a) for lf in range(4) for row in range(2) for a in middles]
        for m in range(4)
    ]

    def straight(x):
        return [x] + [lax.ppermute(x, "col", route) for route in routes]

    def swapped(x):
        return lax.ppermute(x, both, swap)

    def scalars(parent, *rows):
        head = jnp.stack([r, c, leaf, parent]).astype(jnp.int32)
        return jnp.concatenate([head] + [lists[row] for row in rows])

    trunk = 3
    here = scalars(jnp.int32(0), 0, 1)
    packed = half + own // 2
    sigma_parts = straight(sigma_top)
    pack_t, pack_34, pack_56 = move(
        pack_kernel, here, [panels, inverse], [(k, packed, TILE) for k in (trunk, 2, 2)], 35
    )
    blocks_t = straight(pack_t)
    sigma_cols = move(join_columns_kernel, here, after(sigma_parts, pack_t), [(TILE, order)], 4)[0]
    sigma_rows = [sigma_cols] + [
        lax.ppermute(sigma_cols, ("leaf", "row", "col"), leaf_routes[m]) for m in range(1, 4)
    ]
    sigma_other = swapped(move(stack_kernel, here, sigma_rows, [(4, TILE, order)], 4)[0])
    gathered = after(blocks_t, sigma_rows[1:])
    other_t = swapped(move(stack_kernel, here, gathered, [(4, trunk, packed, TILE)], 4)[0])
    blocks_34 = straight(after(pack_34, blocks_t[1:]))
    ext, grand, upper_self, upper_end = call(
        trunk_kernel, here, blocks_t + [other_t] + sigma_rows + [sigma_other],
        [(2, half + own, own), (own, own), (trunk, half + own, TILE), (trunk, packed, TILE)],
        [
            pltpu.VMEM((2, 8, packed, TILE), F32), pltpu.VMEM((8, TILE, order), F32), pltpu.SemaphoreType.DMA((3, 8)),
            pltpu.VMEM((2, order - own, order - own), F32), pltpu.VMEM((order, own), F32), pltpu.VMEM((own, own), F32),
        ] + scratch_pairs(
            (order, own), (own, own), (order, order), (order, own), (order, own), (own, own), (own, order), (own, own)
        ) + [pltpu.VMEM((order, own), F32)],
        [ANY] * 10, micros=60,
    )
    blocks_56 = straight(after(pack_56, (blocks_34[1:], ext)))
    upper_home = lax.ppermute(upper_end, "col", home)
    tails = (order - own) // TILE
    leaf_scratch = [
        pltpu.VMEM((8, packed, TILE), F32), pltpu.SemaphoreType.DMA((10 + tails,)), pltpu.VMEM((tails, TILE, own), F32),
        pltpu.VMEM((own, own), F32), pltpu.VMEM((own, own), F32), pltpu.VMEM((order, STEP), F32),
        pltpu.VMEM((own, STEP), F32),
    ] + scratch_pairs(
        (order, own), (own, own), (order, order), (own, STEP), (order, STEP), (order, STEP), (own, STEP), (own, order),
        (own, own),
    )

    def leaves(blocks, first, earlier, end_rows):
        node = first + r
        parent = lax.dynamic_index_in_dim(links, node - 3, 0, keepdims=False)
        theirs = swapped(move(swap_kernel, here, after(blocks, earlier), [(4, packed, TILE)], 4)[0])
        self_out, core_out, end_out, cross_out = call(
            leaf_kernel, scalars(parent, node - 1), blocks + [theirs, ext, grand],
            [(half + own, TILE)] * 2 + [(end_rows, TILE)] * 2, leaf_scratch, [ANY] * 7, micros=10,
        )
        return self_out, core_out, lax.ppermute(end_out, "col", home), lax.ppermute(cross_out, both, home_cross)

    self_34, core_34, end_34, cross_34 = leaves(blocks_34, 3, ext, packed)
    shares = move(
        shares_kernel, here, [upper_home, end_34, cross_34, core_34], [((trunk + 2) * (own // 2), TILE)], trunk + 2
    )[0]
    shares = lax.ppermute(shares, both, swap_all)
    self_56, core_56, end_56, cross_56 = leaves(blocks_56, 5, (upper_home, end_34, cross_34), half + own)
    count = panels.shape[0]
    ancestor_block, diagonal_block = move(
        output_kernel, here,
        [upper_self, upper_home, self_34, end_34, cross_34, shares, self_56, swapped(core_56), end_56, cross_56],
        [(count, half, TILE), (count, own, TILE)], 3 * count,
    )
    return (ancestor_block[None], diagonal_block[None])


def child_blocks(ancestors, products, diagonals, parent_ids, picks, tile):
    count_parents = ancestors.shape[0]
    slot_count = ancestors.shape[1] // tile
    own_width = diagonals.shape[1]
    own_tiles = own_width // tile
    tail = picks[:, own_tiles:]
    living = tail >= 0
    indices = jnp.maximum(tail, 0)
    child_count = tail.shape[0]
    tail_count = tail.shape[1]
    a_tiles = ancestors.reshape(count_parents, slot_count, tile, slot_count, tile)
    corner = a_tiles[parent_ids[:, None, None], indices[:, :, None], :, indices[:, None, :], :]
    corner = jnp.transpose(corner, (0, 1, 3, 2, 4))
    weights = (living[:, :, None] & living[:, None, :]).astype(jnp.float32)
    corner = corner * weights[:, :, None, :, None]
    corner = corner.reshape(child_count, tail_count * tile, tail_count * tile)
    p_tiles = products.reshape(count_parents, slot_count, tile, own_width)
    side = p_tiles[parent_ids[:, None], indices]
    side = side * living.astype(jnp.float32)[:, :, None, None]
    side = side.reshape(child_count, tail_count * tile, own_width)
    top_left = jnp.take(diagonals, parent_ids, axis=0)
    upper = jnp.concatenate([top_left, -jnp.transpose(side, (0, 2, 1))], axis=2)
    lower = jnp.concatenate([-side, corner], axis=2)
    return jnp.concatenate([upper, lower], axis=1)


def body(sigma_top, panels, inverse_diag, slot_lists, parent_links):
    highest = lax.Precision.HIGHEST
    row_count = lax.axis_size("row")
    col_count = lax.axis_size("col")
    row_index = lax.axis_index("row")
    col_index = lax.axis_index("col")
    panel_local = panels[0]
    inverse_local = inverse_diag[0]
    picks_all = slot_lists[0]
    parents = parent_links[0]
    block_rows = panel_local.shape[1]
    block_cols = panel_local.shape[2]
    diag_width = inverse_local.shape[2]
    diag_rows = diag_width // row_count
    tile = TILE
    top_rows = lax.all_gather(sigma_top, ("leaf", "row"), axis=0, tiled=True)
    top_full = lax.all_gather(top_rows, "col", axis=1, tiled=True)
    partial_factor = jnp.einsum("vrk,vkj->vrj", panel_local, inverse_local, precision=highest)
    inverse_band = lax.dynamic_slice_in_dim(inverse_local, row_index * diag_rows, diag_rows, 2)
    partial_gram = jnp.einsum("vki,vkj->vij", inverse_band, inverse_local, precision=highest)
    factor_rows = lax.psum(partial_factor, "col")
    gram_mine = lax.psum_scatter(partial_gram, "col", scatter_dimension=2, tiled=True)
    slots_here = block_rows // tile
    slot_ids = row_index * slots_here + jnp.arange(slots_here, dtype=jnp.int32)
    listed = jnp.take(picks_all, slot_ids, axis=1) >= 0
    living = jnp.concatenate([jnp.ones((1, slots_here), jnp.bool_), listed], axis=0)
    row_weight = jnp.repeat(living.astype(jnp.float32), tile, axis=1)
    factor_rows = factor_rows * row_weight[:, :, None]
    factor_mine = lax.dynamic_slice_in_dim(factor_rows, col_index * block_cols, block_cols, 2)
    factor_cols = lax.all_gather(factor_mine, "row", axis=1, tiled=True)
    ancestors = top_full[None]
    ancestor_parts = []
    diagonal_parts = []
    bounds = ((0, 1), (1, 3), (3, 7))
    for level_id, (first_node, last_node) in enumerate(bounds):
        own_rows = lax.dynamic_slice_in_dim(ancestors, row_index * block_rows, block_rows, 1)
        product_mine = jnp.einsum(
            "vra,vac->vrc", own_rows, factor_cols[first_node:last_node], precision=highest
        )
        partial_diag = jnp.einsum(
            "vrj,vrc->vjc", factor_rows[first_node:last_node], product_mine, precision=highest
        )
        diag_piece = lax.psum_scatter(partial_diag, "row", scatter_dimension=1, tiled=True)
        diag_piece = diag_piece + gram_mine[first_node:last_node]
        ancestor_parts.append(-product_mine)
        if level_id == 2:
            diag_cols = lax.all_gather(diag_piece, "row", axis=1, tiled=True)
        else:
            width_nodes = last_node - first_node
            product_all, diag_all = (
                lax.all_gather(product_mine[:, None], ("row", "col"), axis=1, tiled=True),
                lax.all_gather(diag_piece[:, None], ("row", "col"), axis=1, tiled=True),
            )
            product_full = product_all.reshape(
                width_nodes, row_count, col_count, block_rows, block_cols
            )
            product_full = product_full.transpose(0, 1, 3, 2, 4).reshape(
                width_nodes, row_count * block_rows, col_count * block_cols
            )
            diag_full = diag_all.reshape(width_nodes, row_count, col_count, diag_rows, block_cols)
            diag_full = diag_full.transpose(0, 1, 3, 2, 4).reshape(
                width_nodes, row_count * diag_rows, col_count * block_cols
            )
            diag_cols = lax.dynamic_slice_in_dim(diag_full, col_index * block_cols, block_cols, 2)
            if level_id == 0:
                parent_ids = jnp.zeros((2,), jnp.int32)
                picks_level = picks_all[0:2]
            else:
                parent_ids = parents - 1
                picks_level = picks_all[2:6]
            ancestors = child_blocks(
                ancestors, product_full, diag_full, parent_ids, picks_level, tile
            )
        diagonal_parts.append(diag_cols)
    ancestor_block = jnp.concatenate(ancestor_parts, axis=0)[None]
    diagonal_block = jnp.concatenate(diagonal_parts, axis=0)[None]
    return (ancestor_block, diagonal_block)


def solution(mesh):
    two_middles = (mesh.shape["leaf"], mesh.shape["row"], mesh.shape["col"]) == (4, 2, 4)
    return jax.shard_map(
        chip_body if two_middles else body,
        mesh=mesh,
        in_specs=(
            P(("leaf", "row"), "col"),
            P("leaf", None, "row", "col"),
            P("leaf", None, "col", None),
            P("leaf", None, None),
            P("leaf", None),
        ),
        out_specs=(P("leaf", None, "row", "col"), P("leaf", None, None, "col")),
        check_vma=False,
    )
```

```python
import functools

import jax
import jax.numpy as jnp
from jax import lax
from jax.experimental import pallas as pl
from jax.experimental.pallas import tpu as pltpu
from jax.sharding import PartitionSpec as P

TILE = 128
STEP = 2 * TILE
QUARTER = TILE // 2
ROWS = 4 * TILE
F32 = jnp.float32
BF16 = jnp.bfloat16
VMEM_LIMIT = 56 * 2**20
WHOLE = pl.BlockSpec(memory_space=pltpu.VMEM)
ANY = pl.BlockSpec(memory_space=pl.ANY)


def split(x):
    high = x.astype(BF16)
    return high, (x - high.astype(F32)).astype(BF16)


def dot3(a, b):
    dot = functools.partial(jnp.dot, preferred_element_type=F32)
    return dot(a[0], b[0]) + (dot(a[0], b[1]) + dot(a[1], b[0]))


def put(pair, index, value):
    high, low = split(value)
    pair[0][index] = high
    pair[1][index] = low


def get(pair, index):
    return pair[0][index], pair[1][index]


def at(start, size, unit=TILE):
    return pl.ds(pl.multiple_of(start, unit), size)


def tiles(size, step=STEP):
    return [slice(m, m + step) for m in range(0, size, step)]


ALL = slice(None)


def load_panels(blocks, r, p, d, pt, dt, half):
    for slot in range(4):
        for turn in range(2):
            ref = blocks[2 * slot + turn]
            side = r if turn == 0 else 1 - r
            panel = ref[0:half, :]
            put(p, (at(side * half, half), slice(slot * TILE, (slot + 1) * TILE)), panel)
            put(pt, (slice(slot * TILE, (slot + 1) * TILE), at(side * half, half)), panel.T)
            for j in range(4):
                rows = at(slot * TILE + side * QUARTER, QUARTER, QUARTER)
                place = slice(j * TILE, (j + 1) * TILE)
                put(d, (rows, place), ref[half + j * QUARTER:half + (j + 1) * QUARTER, :])
    for slot in range(4):
        for j in range(4):
            rows, cols = slice(slot * TILE, (slot + 1) * TILE), slice(j * TILE, (j + 1) * TILE)
            for whole, turned in zip(d, dt):
                turned[cols, rows] = whole[rows, cols].T


def solve(p, pt, dt, a, dc, f, w, t, weights, emit_ab, emit_dg, join):
    width = dc[0].shape[1]
    for rows in tiles(p[0].shape[0], ROWS):
        k = rows.start // TILE
        for cols in tiles(width):
            value = dot3(get(p, (rows, ALL)), get(dc, (ALL, cols)))
            parts = [value[i * TILE:(i + 1) * TILE] * weights[k + i] for i in range(ROWS // TILE)]
            put(f, (rows, cols), jnp.concatenate(parts, axis=0))
    join()
    for cols in tiles(width):
        for rows in tiles(a[0].shape[0], ROWS):
            value = dot3(get(a, (rows, ALL)), get(f, (ALL, cols)))
            emit_ab(rows, cols, -value)
            put(w, (rows, cols), value)
        for rows in tiles(pt[0].shape[0], ROWS):
            value = dot3(get(pt, (rows, ALL)), get(w, (ALL, cols)))
            put(t, (rows, cols), value + dc[0][rows, cols].astype(F32) + dc[1][rows, cols].astype(F32))
        for rows in tiles(dt[0].shape[0], ROWS):
            emit_dg(rows, cols, dot3(get(dt, (rows, ALL)), get(t, (ALL, cols))))


def scratch_pairs(*shapes):
    return [pltpu.VMEM(shape, BF16) for shape in shapes for _ in range(2)]


def pairs(refs):
    return [(refs[i], refs[i + 1]) for i in range(0, len(refs), 2)]


def call(kernel, scalars, operands, outs, scratch, places=None, micros=1):
    return pl.pallas_call(
        kernel,
        out_shape=[jax.ShapeDtypeStruct(o, F32) for o in outs],
        in_specs=[pl.BlockSpec(memory_space=pltpu.SMEM)] + (places or [WHOLE] * len(operands)),
        out_specs=[WHOLE] * len(outs),
        scratch_shapes=scratch,
        compiler_params=pltpu.CompilerParams(vmem_limit_bytes=VMEM_LIMIT),
        cost_estimate=pl.CostEstimate(flops=micros * 10**9, bytes_accessed=1, transcendentals=0),
    )(scalars, *operands)


def copy_all(copies, sems):
    started = [pltpu.make_async_copy(src, dst, sems.at[i]) for i, (src, dst) in enumerate(copies)]
    for one in started:
        one.start()
    for one in started:
        one.wait()


def move(kernel, scalars, operands, outs, count, micros=1):
    return call(
        kernel, scalars, operands, outs, [pltpu.SemaphoreType.DMA((count,))], [ANY] * len(operands), micros
    )


LIST = 4


def tail_of(s, start, own, order):
    spots = [start + k for k in range(own // TILE, order // TILE)]
    return [jnp.maximum(s[k], 0) for k in spots], [(s[k] >= 0).astype(F32) for k in spots]


def weights_of(s, order):
    return [(s[LIST + j] >= 0).astype(F32) for j in range(order // TILE)]


def pack_kernel(first, s, panels, inverse, *rest):
    outs, sems = rest[:-1], rest[-1]
    half = panels.shape[1]
    copies = []
    node = first
    for out in outs:
        for i in range(out.shape[0]):
            copies.append((panels.at[node], out.at[i, pl.ds(0, half)]))
            for j in range(inverse.shape[2] // TILE):
                copies.append((
                    inverse.at[node, at(s[0] * QUARTER, QUARTER, QUARTER), pl.ds(j * TILE, TILE)],
                    out.at[i, pl.ds(half + j * QUARTER, QUARTER)],
                ))
            node += 1
    copy_all(copies, sems)


def join_columns_kernel(s, *refs):
    out, sems = refs[-2:]
    width = refs[0].shape[1]
    copy_all([(ref, out.at[:, pl.ds(k * width, width)]) for k, ref in enumerate(refs[:-2])], sems)


def stack_kernel(s, *refs):
    out, sems = refs[-2:]
    copy_all([(ref, out.at[k]) for k, ref in enumerate(refs[:-2])], sems)


def swap_kernel(s, *refs):
    out, sems = refs[-2:]
    copy_all([(ref.at[1 - s[0]], out.at[k]) for k, ref in enumerate(refs[:-2])], sems)


def join_block(a, own, corner, rows_of, top, index, weight):
    put(a, (slice(0, own), slice(0, own)), top)
    for i in range(len(index)):
        place = slice(own + i * TILE, own + (i + 1) * TILE)
        value = rows_of(i) * weight[i]
        put(a, (place, slice(0, own)), value)
        put(a, (slice(0, own), place), value.T)
        for j in range(len(index)):
            put(a, (place, slice(own + j * TILE, own + (j + 1) * TILE)), corner(i, j) * (weight[i] * weight[j]))


def emitters(ab, dg):
    def emit_ab(rows, cols, value):
        ab[rows, cols] = value

    def emit_dg(rows, cols, value):
        dg[rows, cols] = value

    return emit_ab, emit_dg


def columns_out(s, ab, dg, self_out, end_out):
    r, c = s[0], s[1]
    half = ab.shape[0] // 2
    own = dg.shape[0]
    share = own // 2
    end_cols = at(3 * (c // 2) * TILE, TILE)
    self_out[0:half, :] = ab[at(r * half, half), at(c * TILE, TILE)]
    self_out[half:, :] = dg[:, at(c * TILE, TILE)]
    end_out[0:half, :] = ab[at(r * half, half), end_cols]
    end_out[half:, :] = dg[at(r * share, share), end_cols]


def root_kernel(s, *refs):
    mine, theirs, sigmas = refs[:4], refs[4], refs[5:13]
    ext, corners, self_out, end_out = refs[13:17]
    stage, sigma, sems = refs[17:20]
    p, d, a, f, w, t, pt, dt = pairs(refs[20:])
    r, c, leaf = s[0], s[1], s[2]
    order = a[0].shape[0]
    own = d[0].shape[0]
    half = order // 2
    far = c // 2
    blocks = [x for k in range(4) for x in (mine[k].at[0], theirs.at[k, 0])]
    copies = [pltpu.make_async_copy(ref, stage.at[k], sems.at[0, k]) for k, ref in enumerate(blocks)]
    later = [pltpu.make_async_copy(ref, sigma.at[k], sems.at[1, k]) for k, ref in enumerate(sigmas)]
    for one in copies + later:
        one.start()
    for one in copies:
        one.wait()
    load_panels([stage.at[k] for k in range(8)], r, p, d, pt, dt, half)

    def join():
        places = (c, 3 * far, 3 - c, 3 - 3 * far)
        span = order // 4
        for one in later:
            one.wait()
        for m in range(4):
            for turn in range(2):
                side = r if turn == 0 else 1 - r
                rows = at(((leaf ^ m) * 2 + side) * TILE, TILE)
                for k in range(4):
                    put(a, (rows, at(places[k] * span, span)), sigma[4 * turn + m, :, k * span:(k + 1) * span])

    ab, dg = ext.at[pl.ds(0, order)], ext.at[pl.ds(order, own)]
    solve(p, pt, dt, a, d, f, w, t, [1.0] * (order // TILE), *emitters(ab, dg), join)
    columns_out(s, ab, dg, self_out, end_out)
    for node in range(2):
        index, weight = tail_of(s, LIST + node * (order // TILE), own, order)
        for i in range(len(index)):
            for j in range(len(index)):
                high, low = get(a, (at(index[i] * TILE, TILE), at(index[j] * TILE, TILE)))
                value = high.astype(F32) + low.astype(F32)
                corners[node, i * TILE:(i + 1) * TILE, j * TILE:(j + 1) * TILE] = value


def middle_kernel(s, *refs):
    mine, theirs, root, corners_in = refs[:4], refs[4], refs[5], refs[6]
    ext, self_out, end_out = refs[7:10]
    stage, root_in, corners, sems, ab, dg = refs[10:16]
    p, d, a, f, w, t, pt, dt = pairs(refs[16:])
    r = s[0]
    order = a[0].shape[0]
    own = d[0].shape[0]
    half = order // 2
    blocks = [[x for k in range(4) for x in (mine[k].at[node], theirs.at[k, node])] for node in (1, 2)]
    copies = [
        pltpu.make_async_copy(ref, stage.at[node, k], sems.at[node, k])
        for node in range(2) for k, ref in enumerate(blocks[node])
    ]
    later = [pltpu.make_async_copy(root, root_in, sems.at[2, 0]), pltpu.make_async_copy(corners_in, corners, sems.at[2, 1])]
    for one in copies[:8] + later + copies[8:]:
        one.start()
    for one in copies + later:
        one.wait()

    @pl.loop(0, 2)
    def _(node):
        start = LIST + node * (order // TILE)
        index, weight = tail_of(s, start, own, order)
        load_panels([stage.at[node, k] for k in range(8)], r, p, d, pt, dt, half)

        def join():
            join_block(
                a, own,
                lambda i, j: corners[node, i * TILE:(i + 1) * TILE, j * TILE:(j + 1) * TILE],
                lambda i: root_in[at(index[i] * TILE, TILE), :], root_in[order:, :], index, weight,
            )

        weights = [(s[start + k] >= 0).astype(F32) for k in range(order // TILE)]
        solve(p, pt, dt, a, d, f, w, t, weights, *emitters(ab, dg), join)
        columns_out(s, ab, dg, self_out.at[node], end_out.at[node])
        ext[node, 0:half, :] = ab[0:half, :]
        ext[node, half:, :] = dg[...]


def leaf_kernel(s, x0, x1, x2, x3, ex, ext, root, self_out, core_out, end_out, cross_out, *rest):
    stage, sems, tails, top, grand_in, ab, dg = rest[:7]
    p, d, a, dc, f, w, t, pt, dt = pairs(rest[7:])
    r, c = s[0], s[1]
    blocks = [x for k, ref in enumerate((x0, x1, x2, x3)) for x in (ref.at[r], ex.at[k])]
    order = a[0].shape[0]
    own = d[0].shape[0]
    half = order // 2
    far = c // 2
    index, weight = tail_of(s, LIST, own, order)
    parent = s[3] - 1
    copies = [pltpu.make_async_copy(ref, stage.at[k], sems.at[k]) for k, ref in enumerate(blocks)]
    later = [
        pltpu.make_async_copy(ext.at[parent, pl.ds(half, own)], top, sems.at[8]),
        pltpu.make_async_copy(root.at[pl.ds(order, own)], grand_in, sems.at[9]),
    ]
    for j, pick in enumerate(index):
        later.append(pltpu.make_async_copy(ext.at[parent, at(pick * TILE, TILE)], tails.at[j], sems.at[10 + j]))
    for one in copies + later:
        one.start()
    for one in copies:
        one.wait()
    load_panels([stage.at[k] for k in range(8)], r, p, d, pt, dt, half)
    dc[0][...] = d[0][:, at(far * STEP, STEP)]
    dc[1][...] = d[1][:, at(far * STEP, STEP)]

    def join():
        for one in later:
            one.wait()
        join_block(
            a, own, lambda i, j: grand_in[at(index[i] * TILE, TILE), at(index[j] * TILE, TILE)], lambda i: tails[i],
            top[...], index, weight,
        )

    solve(p, pt, dt, a, dc, f, w, t, weights_of(s, order), *emitters(ab, dg), join)
    near_cols, end_cols = at((1 - far) * TILE, TILE), at(far * TILE, TILE)
    for out, side, cols in (
        (self_out, r, near_cols), (core_out, 1 - r, near_cols), (end_out, r, end_cols), (cross_out, 1 - r, end_cols)
    ):
        out[0:half, :] = ab[at(side * half, half), cols]
        share = out.shape[0] - half
        out[half:, :] = dg[:, cols] if share == own else dg[at(side * share, share), cols]


def shares_kernel(s, root, upper, end, cross, core, out, sems):
    c = s[1]
    middle = (c == 1) | (c == 2)
    half = core.shape[0] // 2
    share = upper.shape[1] - half

    @pl.when(middle)
    def _():
        copy_all([(core, out.at[pl.ds(0, 2 * half)])], sems)

    @pl.when(jnp.logical_not(middle))
    def _():
        found = [root, upper.at[0], upper.at[1], end, cross]
        copy_all([
            (ref.at[pl.ds(half, share)], out.at[pl.ds(k * share, share)]) for k, ref in enumerate(found)
        ], sems)


def output_kernel(s, *refs):
    root_self, root_end, upper_self, upper_end, self_34, end_34, cross_34, shares = refs[:8]
    self_56, core_56, end_56, cross_56 = refs[8:12]
    ab, dg, sems = refs[-3:]
    r, c = s[0], s[1]
    half = ab.shape[1]
    share = half // 2
    middle = (c == 1) | (c == 2)
    for core in range(2):
        @pl.when((r == core) & middle)
        def _():
            pair = [self_34, shares] if core == 0 else [shares, self_34]
            last = [self_56, core_56] if core == 0 else [core_56, self_56]
            copies = []
            for node, ref in enumerate([root_self, upper_self.at[0], upper_self.at[1]] + pair + last):
                copies.append((ref.at[pl.ds(0, half)], ab.at[node]))
                copies.append((ref.at[pl.ds(half, half)], dg.at[node]))
            copy_all(copies, sems)

        @pl.when((r == core) & jnp.logical_not(middle))
        def _():
            same, swapped = (3, 4) if core == 0 else (4, 3)
            last = [end_56, cross_56] if core == 0 else [cross_56, end_56]
            copies = []
            found = [(0, root_end, 0), (1, upper_end.at[0], 1), (2, upper_end.at[1], 2)]
            for node, ref, k in found + [(same, end_34, 4), (swapped, cross_34, 3)]:
                copies.append((ref.at[pl.ds(0, half)], ab.at[node]))
                copies.append((ref.at[pl.ds(half, share)], dg.at[node, pl.ds(core * share, share)]))
                copies.append((shares.at[pl.ds(k * share, share)], dg.at[node, pl.ds((1 - core) * share, share)]))
            for node, ref in ((5, last[0]), (6, last[1])):
                copies.append((ref.at[pl.ds(0, half)], ab.at[node]))
                copies.append((ref.at[pl.ds(half, half)], dg.at[node]))
            copy_all(copies, sems)


def after(x, earlier):
    return lax.optimization_barrier((x, earlier))[0]


def chip_body(sigma_top, panels, inverse_diag, slot_lists, parent_links):
    r = lax.axis_index("row")
    c = lax.axis_index("col")
    leaf = lax.axis_index("leaf")
    panels, inverse, lists, links = panels[0], inverse_diag[0], slot_lists[0], parent_links[0]
    half = panels.shape[1]
    order = 2 * half
    own = inverse.shape[2]
    both = ("row", "col")
    routes = (((0, 1), (3, 2)), ((1, 2), (2, 1)), ((0, 2), (3, 1)))
    middles = (1, 2)
    swap = [(row * 4 + a, (1 - row) * 4 + a) for row in range(2) for a in middles]
    swap_all = [(row * 4 + a, (1 - row) * 4 + a) for row in range(2) for a in range(4)]
    home = ((1, 0), (2, 3))
    home_cross = [(row * 4 + a, (1 - row) * 4 + b) for row in range(2) for a, b in home]
    leaf_routes = [
        [((lf * 2 + row) * 4 + a, ((lf ^ m) * 2 + row) * 4 + a) for lf in range(4) for row in range(2) for a in middles]
        for m in range(4)
    ]

    def straight(x):
        return [x] + [lax.ppermute(x, "col", route) for route in routes]

    def swapped(x):
        return lax.ppermute(x, both, swap)

    def scalars(parent, *rows):
        head = jnp.stack([r, c, leaf, parent]).astype(jnp.int32)
        return jnp.concatenate([head] + [lists[row] for row in rows])

    here = scalars(jnp.int32(0), 0, 1)
    packed = half + own // 2

    pack_t, pack_34, pack_56 = move(
        functools.partial(pack_kernel, 0), here, [panels, inverse], [(k, packed, TILE) for k in (3, 2, 2)], 35
    )
    sigma_parts = straight(sigma_top)
    blocks_t = straight(pack_t)
    sigma_cols = move(join_columns_kernel, here, after(sigma_parts, pack_t), [(TILE, order)], 4)[0]
    sigma_rows = [sigma_cols] + [
        lax.ppermute(sigma_cols, ("leaf", "row", "col"), leaf_routes[m]) for m in range(1, 4)
    ]
    sigma_other = [swapped(x) for x in sigma_rows]
    gathered = after(blocks_t, sigma_other)
    other_t = swapped(move(stack_kernel, here, gathered, [(4, 3, packed, TILE)], 4)[0])
    blocks_34 = straight(after(pack_34, blocks_t[1:]))
    node_scratch = scratch_pairs(
        (order, own), (own, own), (order, order), (order, own), (order, own), (own, own), (own, order), (own, own)
    )
    root, corners, root_self, root_end = call(
        root_kernel, here, blocks_t + [other_t] + sigma_rows + sigma_other,
        [(order + own, own), (2, order - own, order - own), (half + own, TILE), (packed, TILE)],
        [pltpu.VMEM((8, packed, TILE), F32), pltpu.VMEM((8, TILE, order), F32), pltpu.SemaphoreType.DMA((2, 8))]
        + node_scratch, [ANY] * 13, micros=10,
    )
    root_home = lax.ppermute(root_end, "col", home)
    ext, upper_self, upper_end = call(
        middle_kernel, here, blocks_t + [other_t, root, corners],
        [(2, half + own, own), (2, half + own, TILE), (2, packed, TILE)],
        [
            pltpu.VMEM((2, 8, packed, TILE), F32), pltpu.VMEM((order + own, own), F32),
            pltpu.VMEM((2, order - own, order - own), F32), pltpu.SemaphoreType.DMA((3, 8)),
            pltpu.VMEM((order, own), F32), pltpu.VMEM((own, own), F32),
        ] + node_scratch, [ANY] * 7, micros=25,
    )
    blocks_56 = straight(after(pack_56, (blocks_34[1:], ext)))
    upper_home = lax.ppermute(upper_end, "col", home)
    tails = (order - own) // TILE
    leaf_scratch = [
        pltpu.VMEM((8, packed, TILE), F32), pltpu.SemaphoreType.DMA((10 + tails,)), pltpu.VMEM((tails, TILE, own), F32),
        pltpu.VMEM((own, own), F32), pltpu.VMEM((own, own), F32), pltpu.VMEM((order, STEP), F32),
        pltpu.VMEM((own, STEP), F32),
    ] + scratch_pairs(
        (order, own), (own, own), (order, order), (own, STEP), (order, STEP), (order, STEP), (own, STEP), (own, order),
        (own, own),
    )

    def leaves(blocks, first, earlier, end_rows):
        node = first + r
        parent = lax.dynamic_index_in_dim(links, node - 3, 0, keepdims=False)
        theirs = swapped(move(swap_kernel, here, after(blocks, earlier), [(4, packed, TILE)], 4)[0])
        self_out, core_out, end_out, cross_out = call(
            leaf_kernel, scalars(parent, node - 1), blocks + [theirs, ext, root],
            [(half + own, TILE)] * 2 + [(end_rows, TILE)] * 2, leaf_scratch, [ANY] * 7, micros=10,
        )
        return self_out, core_out, lax.ppermute(end_out, "col", home), lax.ppermute(cross_out, both, home_cross)

    self_34, core_34, end_34, cross_34 = leaves(blocks_34, 3, (ext, root_home), packed)
    shares = move(
        shares_kernel, here, [root_home, upper_home, end_34, cross_34, core_34], [(5 * (own // 2), TILE)], 5
    )[0]
    shares = lax.ppermute(shares, both, swap_all)
    self_56, core_56, end_56, cross_56 = leaves(blocks_56, 5, (upper_home, end_34, cross_34), half + own)
    count = panels.shape[0]
    ancestor_block, diagonal_block = move(
        output_kernel, here,
        [
            root_self, root_home, upper_self, upper_home, self_34, end_34, cross_34, shares, self_56, swapped(core_56),
            end_56, cross_56,
        ],
        [(count, half, TILE), (count, own, TILE)], 3 * count,
    )
    return (ancestor_block[None], diagonal_block[None])


def child_blocks(ancestors, products, diagonals, parent_ids, picks, tile):
    count_parents = ancestors.shape[0]
    slot_count = ancestors.shape[1] // tile
    own_width = diagonals.shape[1]
    own_tiles = own_width // tile
    tail = picks[:, own_tiles:]
    living = tail >= 0
    indices = jnp.maximum(tail, 0)
    child_count = tail.shape[0]
    tail_count = tail.shape[1]
    a_tiles = ancestors.reshape(count_parents, slot_count, tile, slot_count, tile)
    corner = a_tiles[parent_ids[:, None, None], indices[:, :, None], :, indices[:, None, :], :]
    corner = jnp.transpose(corner, (0, 1, 3, 2, 4))
    weights = (living[:, :, None] & living[:, None, :]).astype(jnp.float32)
    corner = corner * weights[:, :, None, :, None]
    corner = corner.reshape(child_count, tail_count * tile, tail_count * tile)
    p_tiles = products.reshape(count_parents, slot_count, tile, own_width)
    side = p_tiles[parent_ids[:, None], indices]
    side = side * living.astype(jnp.float32)[:, :, None, None]
    side = side.reshape(child_count, tail_count * tile, own_width)
    top_left = jnp.take(diagonals, parent_ids, axis=0)
    upper = jnp.concatenate([top_left, -jnp.transpose(side, (0, 2, 1))], axis=2)
    lower = jnp.concatenate([-side, corner], axis=2)
    return jnp.concatenate([upper, lower], axis=1)


def body(sigma_top, panels, inverse_diag, slot_lists, parent_links):
    highest = lax.Precision.HIGHEST
    row_count = lax.axis_size("row")
    col_count = lax.axis_size("col")
    row_index = lax.axis_index("row")
    col_index = lax.axis_index("col")
    panel_local = panels[0]
    inverse_local = inverse_diag[0]
    picks_all = slot_lists[0]
    parents = parent_links[0]
    block_rows = panel_local.shape[1]
    block_cols = panel_local.shape[2]
    diag_width = inverse_local.shape[2]
    diag_rows = diag_width // row_count
    tile = TILE
    top_rows = lax.all_gather(sigma_top, ("leaf", "row"), axis=0, tiled=True)
    top_full = lax.all_gather(top_rows, "col", axis=1, tiled=True)
    partial_factor = jnp.einsum("vrk,vkj->vrj", panel_local, inverse_local, precision=highest)
    inverse_band = lax.dynamic_slice_in_dim(inverse_local, row_index * diag_rows, diag_rows, 2)
    partial_gram = jnp.einsum("vki,vkj->vij", inverse_band, inverse_local, precision=highest)
    factor_rows = lax.psum(partial_factor, "col")
    gram_mine = lax.psum_scatter(partial_gram, "col", scatter_dimension=2, tiled=True)
    slots_here = block_rows // tile
    slot_ids = row_index * slots_here + jnp.arange(slots_here, dtype=jnp.int32)
    listed = jnp.take(picks_all, slot_ids, axis=1) >= 0
    living = jnp.concatenate([jnp.ones((1, slots_here), jnp.bool_), listed], axis=0)
    row_weight = jnp.repeat(living.astype(jnp.float32), tile, axis=1)
    factor_rows = factor_rows * row_weight[:, :, None]
    factor_mine = lax.dynamic_slice_in_dim(factor_rows, col_index * block_cols, block_cols, 2)
    factor_cols = lax.all_gather(factor_mine, "row", axis=1, tiled=True)
    ancestors = top_full[None]
    ancestor_parts = []
    diagonal_parts = []
    bounds = ((0, 1), (1, 3), (3, 7))
    for level_id, (first_node, last_node) in enumerate(bounds):
        own_rows = lax.dynamic_slice_in_dim(ancestors, row_index * block_rows, block_rows, 1)
        product_mine = jnp.einsum(
            "vra,vac->vrc", own_rows, factor_cols[first_node:last_node], precision=highest
        )
        partial_diag = jnp.einsum(
            "vrj,vrc->vjc", factor_rows[first_node:last_node], product_mine, precision=highest
        )
        diag_piece = lax.psum_scatter(partial_diag, "row", scatter_dimension=1, tiled=True)
        diag_piece = diag_piece + gram_mine[first_node:last_node]
        ancestor_parts.append(-product_mine)
        if level_id == 2:
            diag_cols = lax.all_gather(diag_piece, "row", axis=1, tiled=True)
        else:
            width_nodes = last_node - first_node
            product_all, diag_all = (
                lax.all_gather(product_mine[:, None], ("row", "col"), axis=1, tiled=True),
                lax.all_gather(diag_piece[:, None], ("row", "col"), axis=1, tiled=True),
            )
            product_full = product_all.reshape(
                width_nodes, row_count, col_count, block_rows, block_cols
            )
            product_full = product_full.transpose(0, 1, 3, 2, 4).reshape(
                width_nodes, row_count * block_rows, col_count * block_cols
            )
            diag_full = diag_all.reshape(width_nodes, row_count, col_count, diag_rows, block_cols)
            diag_full = diag_full.transpose(0, 1, 3, 2, 4).reshape(
                width_nodes, row_count * diag_rows, col_count * block_cols
            )
            diag_cols = lax.dynamic_slice_in_dim(diag_full, col_index * block_cols, block_cols, 2)
            if level_id == 0:
                parent_ids = jnp.zeros((2,), jnp.int32)
                picks_level = picks_all[0:2]
            else:
                parent_ids = parents - 1
                picks_level = picks_all[2:6]
            ancestors = child_blocks(
                ancestors, product_full, diag_full, parent_ids, picks_level, tile
            )
        diagonal_parts.append(diag_cols)
    ancestor_block = jnp.concatenate(ancestor_parts, axis=0)[None]
    diagonal_block = jnp.concatenate(diagonal_parts, axis=0)[None]
    return (ancestor_block, diagonal_block)


def solution(mesh):
    two_middles = (mesh.shape["leaf"], mesh.shape["row"], mesh.shape["col"]) == (4, 2, 4)
    return jax.shard_map(
        chip_body if two_middles else body,
        mesh=mesh,
        in_specs=(
            P(("leaf", "row"), "col"),
            P("leaf", None, "row", "col"),
            P("leaf", None, "col", None),
            P("leaf", None, None),
            P("leaf", None),
        ),
        out_specs=(P("leaf", None, "row", "col"), P("leaf", None, None, "col")),
        check_vma=False,
    )
```

```python
import functools

import jax
import jax.numpy as jnp
from jax import lax
from jax.experimental import pallas as pl
from jax.experimental.pallas import tpu as pltpu
from jax.sharding import PartitionSpec as P

TILE = 128
STEP = 2 * TILE
QUARTER = TILE // 2
F32 = jnp.float32
BF16 = jnp.bfloat16
VMEM_LIMIT = 56 * 2**20
WHOLE = pl.BlockSpec(memory_space=pltpu.VMEM)
ANY = pl.BlockSpec(memory_space=pl.ANY)


def split(x):
    high = x.astype(BF16)
    return high, (x - high.astype(F32)).astype(BF16)


def dot3(a, b):
    dot = functools.partial(jnp.dot, preferred_element_type=F32)
    return dot(a[0], b[0]) + (dot(a[0], b[1]) + dot(a[1], b[0]))


def put(pair, index, value):
    high, low = split(value)
    pair[0][index] = high
    pair[1][index] = low


def get(pair, index):
    return pair[0][index], pair[1][index]


def at(start, size, unit=TILE):
    return pl.ds(pl.multiple_of(start, unit), size)


def tiles(size, step=STEP):
    return [slice(m, m + step) for m in range(0, size, step)]


ALL = slice(None)


def load_panels(blocks, r, p, d, pt, dt, half):
    for slot in range(4):
        for turn in range(2):
            ref = blocks[2 * slot + turn]
            side = r if turn == 0 else 1 - r
            panel = ref[0:half, :]
            put(p, (at(side * half, half), slice(slot * TILE, (slot + 1) * TILE)), panel)
            put(pt, (slice(slot * TILE, (slot + 1) * TILE), at(side * half, half)), panel.T)
            for j in range(4):
                rows = at(slot * TILE + side * QUARTER, QUARTER, QUARTER)
                place = slice(j * TILE, (j + 1) * TILE)
                put(d, (rows, place), ref[half + j * QUARTER:half + (j + 1) * QUARTER, :])
    for slot in range(4):
        for j in range(4):
            rows, cols = slice(slot * TILE, (slot + 1) * TILE), slice(j * TILE, (j + 1) * TILE)
            for whole, turned in zip(d, dt):
                turned[cols, rows] = whole[rows, cols].T


def solve(p, pt, dt, a, dc, f, w, t, weights, emit_ab, emit_dg, join):
    width = dc[0].shape[1]
    for rows in tiles(p[0].shape[0]):
        k = rows.start // TILE
        for cols in tiles(width):
            value = dot3(get(p, (rows, ALL)), get(dc, (ALL, cols)))
            value = jnp.concatenate([value[:TILE] * weights[k], value[TILE:] * weights[k + 1]], axis=0)
            put(f, (rows, cols), value)
    join()
    for cols in tiles(width):
        for rows in tiles(a[0].shape[0]):
            value = dot3(get(a, (rows, ALL)), get(f, (ALL, cols)))
            emit_ab(rows, cols, -value)
            put(w, (rows, cols), value)
        for rows in tiles(pt[0].shape[0]):
            value = dot3(get(pt, (rows, ALL)), get(w, (ALL, cols)))
            put(t, (rows, cols), value + dc[0][rows, cols].astype(F32) + dc[1][rows, cols].astype(F32))
        for rows in tiles(dt[0].shape[0]):
            emit_dg(rows, cols, dot3(get(dt, (rows, ALL)), get(t, (ALL, cols))))


def scratch_pairs(*shapes):
    return [pltpu.VMEM(shape, BF16) for shape in shapes for _ in range(2)]


def pairs(refs):
    return [(refs[i], refs[i + 1]) for i in range(0, len(refs), 2)]


def call(kernel, scalars, operands, outs, scratch, places=None, micros=1):
    return pl.pallas_call(
        kernel,
        out_shape=[jax.ShapeDtypeStruct(o, F32) for o in outs],
        in_specs=[pl.BlockSpec(memory_space=pltpu.SMEM)] + (places or [WHOLE] * len(operands)),
        out_specs=[WHOLE] * len(outs),
        scratch_shapes=scratch,
        compiler_params=pltpu.CompilerParams(vmem_limit_bytes=VMEM_LIMIT),
        cost_estimate=pl.CostEstimate(flops=micros * 10**9, bytes_accessed=1, transcendentals=0),
    )(scalars, *operands)


def copy_all(copies, sems):
    started = [pltpu.make_async_copy(src, dst, sems.at[i]) for i, (src, dst) in enumerate(copies)]
    for one in started:
        one.start()
    for one in started:
        one.wait()


def move(kernel, scalars, operands, outs, count, micros=1):
    return call(
        kernel, scalars, operands, outs, [pltpu.SemaphoreType.DMA((count,))], [ANY] * len(operands), micros
    )


LINKS, LIST = 4, 8


def tail_of(s, start, own, order):
    spots = [start + k for k in range(own // TILE, order // TILE)]
    return [jnp.maximum(s[k], 0) for k in spots], [(s[k] >= 0).astype(F32) for k in spots]


def weights_of(s, start, order):
    return [(s[start + j] >= 0).astype(F32) for j in range(order // TILE)]


def pack_kernel(first, s, panels, inverse, *rest):
    outs, sems = rest[:-1], rest[-1]
    half = panels.shape[1]
    copies = []
    node = first
    for out in outs:
        for i in range(out.shape[0]):
            copies.append((panels.at[node], out.at[i, pl.ds(0, half)]))
            for j in range(inverse.shape[2] // TILE):
                copies.append((
                    inverse.at[node, at(s[0] * QUARTER, QUARTER, QUARTER), pl.ds(j * TILE, TILE)],
                    out.at[i, pl.ds(half + j * QUARTER, QUARTER)],
                ))
            node += 1
    copy_all(copies, sems)


def leaf_pack_kernel(s, panels, inverse, pair, every, last, sems):
    half = panels.shape[1]
    targets = [(3 + k, pair.at[k]) for k in range(2)] + [(3 + k, every.at[k]) for k in range(4)]
    targets += [(5 + k, last.at[k]) for k in range(2)]
    copies = []
    for node, out in targets:
        copies.append((panels.at[node], out.at[pl.ds(0, half)]))
        for j in range(inverse.shape[2] // TILE):
            copies.append((
                inverse.at[node, at(s[0] * QUARTER, QUARTER, QUARTER), pl.ds(j * TILE, TILE)],
                out.at[pl.ds(half + j * QUARTER, QUARTER)],
            ))
    copy_all(copies, sems)


def join_columns_kernel(s, *refs):
    out, sems = refs[-2:]
    width = refs[0].shape[1]
    copy_all([(ref, out.at[:, pl.ds(k * width, width)]) for k, ref in enumerate(refs[:-2])], sems)


def stack_kernel(s, *refs):
    out, sems = refs[-2:]
    copy_all([(ref, out.at[k]) for k, ref in enumerate(refs[:-2])], sems)


def swap_kernel(skips, s, *refs):
    out, sems = refs[-2:]
    copy_all([(ref.at[skips[k] + 1 - s[0]], out.at[k]) for k, ref in enumerate(refs[:-2])], sems)


def join_block(a, own, corner, rows_of, top, index, weight):
    put(a, (slice(0, own), slice(0, own)), top)
    for i in range(len(index)):
        place = slice(own + i * TILE, own + (i + 1) * TILE)
        value = rows_of(i) * weight[i]
        put(a, (place, slice(0, own)), value)
        put(a, (slice(0, own), place), value.T)
        for j in range(len(index)):
            put(a, (place, slice(own + j * TILE, own + (j + 1) * TILE)), corner(i, j) * (weight[i] * weight[j]))


def trunk_kernel(s, *refs):
    mine, theirs, sigmas = refs[:4], refs[4], refs[5:10]
    ext, grand, self_out, end_out = refs[10:14]
    stage, sigma, sems, corners, ab, dg = refs[14:20]
    p, d, a, f, w, t, pt, dt = pairs(refs[20:-1])
    r, c, leaf = s[0], s[1], s[2]
    order = a[0].shape[0]
    own = d[0].shape[0]
    half = order // 2
    far = c // 2
    count = 3

    def fetch(node, slot):
        found = []
        for k in range(4):
            found.append(pltpu.make_async_copy(mine[k].at[node], stage.at[slot, 2 * k], sems.at[slot, 2 * k]))
            found.append(pltpu.make_async_copy(theirs.at[k, node], stage.at[slot, 2 * k + 1], sems.at[slot, 2 * k + 1]))
        return found

    sigma_copies = [
        pltpu.make_async_copy(ref, sigma.at[k], sems.at[2, k])
        for k, ref in enumerate(list(sigmas[:4]) + [sigmas[4].at[m] for m in range(4)])
    ]
    for one in fetch(0, 0) + sigma_copies + fetch(1, 1):
        one.start()

    def panels_of(node, slot):
        for one in fetch(node, slot):
            one.wait()
        load_panels([stage.at[slot, k] for k in range(8)], r, p, d, pt, dt, half)

    def emit_ab(rows, cols, value):
        ab[rows, cols] = value

    def emit_dg(rows, cols, value):
        dg[rows, cols] = value

    def columns_out(node):
        for out, col in ((self_out, c), (end_out, 3 * far)):
            out[node, 0:half, :] = ab[at(r * half, half), at(col * TILE, TILE)]
        self_out[node, half:, :] = dg[:, at(c * TILE, TILE)]
        end_out[node, half:, :] = dg[at(r * (own // 2), own // 2), at(3 * far * TILE, TILE)]

    panels_of(0, 0)

    def join_root():
        places = (c, 3 * far, 3 - c, 3 - 3 * far)
        span = order // 4
        for one in sigma_copies:
            one.wait()
        for m in range(4):
            for turn in range(2):
                side = r if turn == 0 else 1 - r
                rows = at(((leaf ^ m) * 2 + side) * TILE, TILE)
                for k in range(4):
                    value = sigma[4 * turn + m, :, k * span:(k + 1) * span]
                    put(a, (rows, at(places[k] * span, span)), value)

    solve(p, pt, dt, a, d, f, w, t, [1.0] * (order // TILE), emit_ab, emit_dg, join_root)
    columns_out(0)
    grand[...] = dg[...]
    for node in (1, 2):
        index, weight = tail_of(s, LIST + (node - 1) * (order // TILE), own, order)
        for i in range(len(index)):
            for j in range(len(index)):
                high, low = get(a, (at(index[i] * TILE, TILE), at(index[j] * TILE, TILE)))
                value = high.astype(F32) + low.astype(F32)
                corners[node - 1, i * TILE:(i + 1) * TILE, j * TILE:(j + 1) * TILE] = value
    for one in fetch(2, 0):
        one.start()
    root_ab = refs[-1]
    root_ab[...] = ab[...]

    @pl.loop(1, count)
    def _(node):
        start = LIST + (node - 1) * (order // TILE)
        index, weight = tail_of(s, start, own, order)
        panels_of(node, node % 2)

        def join():
            join_block(
                a, own,
                lambda i, j: corners[node - 1, i * TILE:(i + 1) * TILE, j * TILE:(j + 1) * TILE],
                lambda i: root_ab[at(index[i] * TILE, TILE), :], grand[...], index, weight,
            )

        solve(p, pt, dt, a, d, f, w, t, weights_of(s, start, order), emit_ab, emit_dg, join)
        columns_out(node)
        ext[node - 1, 0:half, :] = ab[0:half, :]
        ext[node - 1, half:, :] = dg[...]


def leaf_kernel(first, skips, s, x0, x1, x2, x3, ex, ext, grand, self_out, core_out, end_out, cross_out, *rest):
    stage, sems, tails, top, grand_in, ab, dg = rest[:7]
    p, d, a, dc, f, w, t, pt, dt = pairs(rest[7:])
    r, c = s[0], s[1]
    blocks = [x for k, ref in enumerate((x0, x1, x2, x3)) for x in (ref.at[skips[k] + r], ex.at[k])]
    order = a[0].shape[0]
    own = d[0].shape[0]
    half = order // 2
    far = c // 2
    node = first + r
    start = LIST + (node - 1) * (order // TILE)
    index, weight = tail_of(s, start, own, order)
    parent = s[LINKS + node - 3] - 1
    copies = [pltpu.make_async_copy(ref, stage.at[k], sems.at[k]) for k, ref in enumerate(blocks)]
    later = [
        pltpu.make_async_copy(ext.at[parent, pl.ds(half, own)], top, sems.at[8]),
        pltpu.make_async_copy(grand, grand_in, sems.at[9]),
    ]
    for j, pick in enumerate(index):
        later.append(pltpu.make_async_copy(ext.at[parent, at(pick * TILE, TILE)], tails.at[j], sems.at[10 + j]))
    for one in copies + later:
        one.start()
    for one in copies:
        one.wait()
    load_panels([stage.at[k] for k in range(8)], r, p, d, pt, dt, half)
    dc[0][...] = d[0][:, at(far * STEP, STEP)]
    dc[1][...] = d[1][:, at(far * STEP, STEP)]

    def join():
        for one in later:
            one.wait()
        join_block(
            a, own, lambda i, j: grand_in[at(index[i] * TILE, TILE), at(index[j] * TILE, TILE)], lambda i: tails[i],
            top[...], index, weight,
        )

    def emit_ab(rows, cols, value):
        ab[rows, cols] = value

    def emit_dg(rows, cols, value):
        dg[rows, cols] = value

    solve(p, pt, dt, a, dc, f, w, t, weights_of(s, start, order), emit_ab, emit_dg, join)
    near_cols, end_cols = at((1 - far) * TILE, TILE), at(far * TILE, TILE)
    for out, side, cols in (
        (self_out, r, near_cols), (core_out, 1 - r, near_cols), (end_out, r, end_cols), (cross_out, 1 - r, end_cols)
    ):
        out[0:half, :] = ab[at(side * half, half), cols]
        share = out.shape[0] - half
        out[half:, :] = dg[:, cols] if share == own else dg[at(side * share, share), cols]


def shares_kernel(s, upper, end, cross, core, out, sems):
    c = s[1]
    middle = (c == 1) | (c == 2)
    half = core.shape[0] // 2
    share = upper.shape[1] - half

    @pl.when(middle)
    def _():
        copy_all([(core, out.at[pl.ds(0, 2 * half)])], sems)

    @pl.when(jnp.logical_not(middle))
    def _():
        found = [upper.at[k] for k in range(3)] + [end, cross]
        copy_all([
            (ref.at[pl.ds(half, share)], out.at[pl.ds(k * share, share)]) for k, ref in enumerate(found)
        ], sems)


def output_kernel(s, *refs):
    upper_self, upper_end, self_34, end_34, cross_34, shares, self_56, core_56, end_56, cross_56 = refs[:10]
    ab, dg, sems = refs[-3:]
    r, c = s[0], s[1]
    half = ab.shape[1]
    share = half // 2
    middle = (c == 1) | (c == 2)
    for core in range(2):
        @pl.when((r == core) & middle)
        def _():
            pair = [self_34, shares] if core == 0 else [shares, self_34]
            last = [self_56, core_56] if core == 0 else [core_56, self_56]
            copies = []
            for node, ref in enumerate([upper_self.at[k] for k in range(3)] + pair + last):
                copies.append((ref.at[pl.ds(0, half)], ab.at[node]))
                copies.append((ref.at[pl.ds(half, half)], dg.at[node]))
            copy_all(copies, sems)

        @pl.when((r == core) & jnp.logical_not(middle))
        def _():
            same, swapped = (3, 4) if core == 0 else (4, 3)
            last = [end_56, cross_56] if core == 0 else [cross_56, end_56]
            copies = []
            for node, ref, k in [(k, upper_end.at[k], k) for k in range(3)] + [(same, end_34, 4), (swapped, cross_34, 3)]:
                copies.append((ref.at[pl.ds(0, half)], ab.at[node]))
                copies.append((ref.at[pl.ds(half, share)], dg.at[node, pl.ds(core * share, share)]))
                copies.append((shares.at[pl.ds(k * share, share)], dg.at[node, pl.ds((1 - core) * share, share)]))
            for node, ref in ((5, last[0]), (6, last[1])):
                copies.append((ref.at[pl.ds(0, half)], ab.at[node]))
                copies.append((ref.at[pl.ds(half, half)], dg.at[node]))
            copy_all(copies, sems)


def after(x, earlier):
    return lax.optimization_barrier((x, earlier))[0]


def chip_body(sigma_top, panels, inverse_diag, slot_lists, parent_links):
    r = lax.axis_index("row")
    c = lax.axis_index("col")
    leaf = lax.axis_index("leaf")
    panels, inverse, lists, links = panels[0], inverse_diag[0], slot_lists[0], parent_links[0]
    half = panels.shape[1]
    order = 2 * half
    own = inverse.shape[2]
    both = ("row", "col")
    routes = (((0, 1), (3, 2)), ((1, 2), (2, 1)), ((0, 2), (3, 1)))
    middles = (1, 2)
    swap = [(row * 4 + a, (1 - row) * 4 + a) for row in range(2) for a in middles]
    swap_all = [(row * 4 + a, (1 - row) * 4 + a) for row in range(2) for a in range(4)]
    home = ((1, 0), (2, 3))
    home_cross = [(row * 4 + a, (1 - row) * 4 + b) for row in range(2) for a, b in home]
    leaf_routes = [
        [((lf * 2 + row) * 4 + a, ((lf ^ m) * 2 + row) * 4 + a) for lf in range(4) for row in range(2) for a in middles]
        for m in range(4)
    ]

    def straight(x):
        return [x] + [lax.ppermute(x, "col", route) for route in routes]

    def swapped(x):
        return lax.ppermute(x, both, swap)

    here = jnp.concatenate([jnp.stack([r, c, leaf, jnp.int32(0)]).astype(jnp.int32), links, lists.reshape(-1)])
    trunk = 3
    packed = half + own // 2

    def pack(first, *counts):
        return move(
            functools.partial(pack_kernel, first), here, [panels, inverse], [(k, packed, TILE) for k in counts],
            5 * sum(counts),
        )

    def pack_leaves(sources):
        return move(leaf_pack_kernel, here, sources, [(k, packed, TILE) for k in (2, 4, 2)], 40)

    sigma_parts = straight(sigma_top)
    pack_t = pack(0, trunk)[0]
    blocks_t = straight(pack_t)
    sigma_cols = move(join_columns_kernel, here, after(sigma_parts, pack_t), [(TILE, order)], 4)[0]
    sigma_rows = [sigma_cols] + [
        lax.ppermute(sigma_cols, ("leaf", "row", "col"), leaf_routes[m]) for m in range(1, 4)
    ]
    sigma_mine = move(stack_kernel, here, sigma_rows, [(4, TILE, order)], 4)[0]
    sigma_other = swapped(sigma_mine)
    pack_34, pack_all, pack_56 = pack_leaves(after((panels, inverse), pack_t))
    gathered = after(blocks_t, (sigma_mine, pack_34))
    other_t = swapped(move(stack_kernel, here, gathered, [(4, trunk, packed, TILE)], 4)[0])
    pack_34, pack_all = after((pack_34, pack_all), blocks_t[1:])
    near, between, far = routes
    across = lax.ppermute(pack_all, "col", between)
    blocks_34 = [pack_34, lax.ppermute(pack_34, "col", near), across, lax.ppermute(pack_34, "col", far)]
    ext, grand, upper_self, upper_end = call(
        trunk_kernel, here, blocks_t + [other_t] + sigma_rows + [sigma_other],
        [(2, half + own, own), (own, own), (trunk, half + own, TILE), (trunk, packed, TILE)],
        [
            pltpu.VMEM((2, 8, packed, TILE), F32), pltpu.VMEM((8, TILE, order), F32), pltpu.SemaphoreType.DMA((3, 8)),
            pltpu.VMEM((2, order - own, order - own), F32), pltpu.VMEM((order, own), F32), pltpu.VMEM((own, own), F32),
        ] + scratch_pairs(
            (order, own), (own, own), (order, order), (order, own), (order, own), (own, own), (own, order), (own, own)
        ) + [pltpu.VMEM((order, own), F32)],
        [ANY] * 10, micros=60,
    )
    last = after(pack_56, ext)
    blocks_56 = [pack_56, lax.ppermute(last, "col", near), across, lax.ppermute(last, "col", far)]
    upper_home = lax.ppermute(upper_end, "col", home)
    tails = (order - own) // TILE
    leaf_scratch = [
        pltpu.VMEM((8, packed, TILE), F32), pltpu.SemaphoreType.DMA((10 + tails,)), pltpu.VMEM((tails, TILE, own), F32),
        pltpu.VMEM((own, own), F32), pltpu.VMEM((own, own), F32), pltpu.VMEM((order, STEP), F32),
        pltpu.VMEM((own, STEP), F32),
    ] + scratch_pairs(
        (order, own), (own, own), (order, order), (own, STEP), (order, STEP), (order, STEP), (own, STEP), (own, order),
        (own, own),
    )

    def leaves(blocks, first, skips, earlier, end_rows):
        chosen = after(blocks, earlier)
        theirs = swapped(move(functools.partial(swap_kernel, skips), here, chosen, [(4, packed, TILE)], 4)[0])
        self_out, core_out, end_out, cross_out = call(
            functools.partial(leaf_kernel, first, skips), here, blocks + [theirs, ext, grand],
            [(half + own, TILE)] * 2 + [(end_rows, TILE)] * 2, leaf_scratch, [ANY] * 7, micros=10,
        )
        return self_out, core_out, lax.ppermute(end_out, "col", home), lax.ppermute(cross_out, both, home_cross)

    self_34, core_34, end_34, cross_34 = leaves(blocks_34, 3, (0, 0, 0, 0), ext, packed)
    self_56, core_56, end_56, cross_56 = leaves(blocks_56, 5, (0, 0, 2, 0), (upper_home, self_34), half + own)
    shares = move(
        shares_kernel, here, after([upper_home, end_34, cross_34, core_34], self_56), [((trunk + 2) * (own // 2), TILE)], trunk + 2
    )[0]
    shares = lax.ppermute(shares, both, swap_all)
    count = panels.shape[0]
    ancestor_block, diagonal_block = move(
        output_kernel, here,
        [upper_self, upper_home, self_34, end_34, cross_34, shares, self_56, swapped(core_56), end_56, cross_56],
        [(count, half, TILE), (count, own, TILE)], 3 * count,
    )
    return (ancestor_block[None], diagonal_block[None])


def child_blocks(ancestors, products, diagonals, parent_ids, picks, tile):
    count_parents = ancestors.shape[0]
    slot_count = ancestors.shape[1] // tile
    own_width = diagonals.shape[1]
    own_tiles = own_width // tile
    tail = picks[:, own_tiles:]
    living = tail >= 0
    indices = jnp.maximum(tail, 0)
    child_count = tail.shape[0]
    tail_count = tail.shape[1]
    a_tiles = ancestors.reshape(count_parents, slot_count, tile, slot_count, tile)
    corner = a_tiles[parent_ids[:, None, None], indices[:, :, None], :, indices[:, None, :], :]
    corner = jnp.transpose(corner, (0, 1, 3, 2, 4))
    weights = (living[:, :, None] & living[:, None, :]).astype(jnp.float32)
    corner = corner * weights[:, :, None, :, None]
    corner = corner.reshape(child_count, tail_count * tile, tail_count * tile)
    p_tiles = products.reshape(count_parents, slot_count, tile, own_width)
    side = p_tiles[parent_ids[:, None], indices]
    side = side * living.astype(jnp.float32)[:, :, None, None]
    side = side.reshape(child_count, tail_count * tile, own_width)
    top_left = jnp.take(diagonals, parent_ids, axis=0)
    upper = jnp.concatenate([top_left, -jnp.transpose(side, (0, 2, 1))], axis=2)
    lower = jnp.concatenate([-side, corner], axis=2)
    return jnp.concatenate([upper, lower], axis=1)


def body(sigma_top, panels, inverse_diag, slot_lists, parent_links):
    highest = lax.Precision.HIGHEST
    row_count = lax.axis_size("row")
    col_count = lax.axis_size("col")
    row_index = lax.axis_index("row")
    col_index = lax.axis_index("col")
    panel_local = panels[0]
    inverse_local = inverse_diag[0]
    picks_all = slot_lists[0]
    parents = parent_links[0]
    block_rows = panel_local.shape[1]
    block_cols = panel_local.shape[2]
    diag_width = inverse_local.shape[2]
    diag_rows = diag_width // row_count
    tile = TILE
    top_rows = lax.all_gather(sigma_top, ("leaf", "row"), axis=0, tiled=True)
    top_full = lax.all_gather(top_rows, "col", axis=1, tiled=True)
    partial_factor = jnp.einsum("vrk,vkj->vrj", panel_local, inverse_local, precision=highest)
    inverse_band = lax.dynamic_slice_in_dim(inverse_local, row_index * diag_rows, diag_rows, 2)
    partial_gram = jnp.einsum("vki,vkj->vij", inverse_band, inverse_local, precision=highest)
    factor_rows = lax.psum(partial_factor, "col")
    gram_mine = lax.psum_scatter(partial_gram, "col", scatter_dimension=2, tiled=True)
    slots_here = block_rows // tile
    slot_ids = row_index * slots_here + jnp.arange(slots_here, dtype=jnp.int32)
    listed = jnp.take(picks_all, slot_ids, axis=1) >= 0
    living = jnp.concatenate([jnp.ones((1, slots_here), jnp.bool_), listed], axis=0)
    row_weight = jnp.repeat(living.astype(jnp.float32), tile, axis=1)
    factor_rows = factor_rows * row_weight[:, :, None]
    factor_mine = lax.dynamic_slice_in_dim(factor_rows, col_index * block_cols, block_cols, 2)
    factor_cols = lax.all_gather(factor_mine, "row", axis=1, tiled=True)
    ancestors = top_full[None]
    ancestor_parts = []
    diagonal_parts = []
    bounds = ((0, 1), (1, 3), (3, 7))
    for level_id, (first_node, last_node) in enumerate(bounds):
        own_rows = lax.dynamic_slice_in_dim(ancestors, row_index * block_rows, block_rows, 1)
        product_mine = jnp.einsum(
            "vra,vac->vrc", own_rows, factor_cols[first_node:last_node], precision=highest
        )
        partial_diag = jnp.einsum(
            "vrj,vrc->vjc", factor_rows[first_node:last_node], product_mine, precision=highest
        )
        diag_piece = lax.psum_scatter(partial_diag, "row", scatter_dimension=1, tiled=True)
        diag_piece = diag_piece + gram_mine[first_node:last_node]
        ancestor_parts.append(-product_mine)
        if level_id == 2:
            diag_cols = lax.all_gather(diag_piece, "row", axis=1, tiled=True)
        else:
            width_nodes = last_node - first_node
            product_all, diag_all = (
                lax.all_gather(product_mine[:, None], ("row", "col"), axis=1, tiled=True),
                lax.all_gather(diag_piece[:, None], ("row", "col"), axis=1, tiled=True),
            )
            product_full = product_all.reshape(
                width_nodes, row_count, col_count, block_rows, block_cols
            )
            product_full = product_full.transpose(0, 1, 3, 2, 4).reshape(
                width_nodes, row_count * block_rows, col_count * block_cols
            )
            diag_full = diag_all.reshape(width_nodes, row_count, col_count, diag_rows, block_cols)
            diag_full = diag_full.transpose(0, 1, 3, 2, 4).reshape(
                width_nodes, row_count * diag_rows, col_count * block_cols
            )
            diag_cols = lax.dynamic_slice_in_dim(diag_full, col_index * block_cols, block_cols, 2)
            if level_id == 0:
                parent_ids = jnp.zeros((2,), jnp.int32)
                picks_level = picks_all[0:2]
            else:
                parent_ids = parents - 1
                picks_level = picks_all[2:6]
            ancestors = child_blocks(
                ancestors, product_full, diag_full, parent_ids, picks_level, tile
            )
        diagonal_parts.append(diag_cols)
    ancestor_block = jnp.concatenate(ancestor_parts, axis=0)[None]
    diagonal_block = jnp.concatenate(diagonal_parts, axis=0)[None]
    return (ancestor_block, diagonal_block)


def solution(mesh):
    two_middles = (mesh.shape["leaf"], mesh.shape["row"], mesh.shape["col"]) == (4, 2, 4)
    return jax.shard_map(
        chip_body if two_middles else body,
        mesh=mesh,
        in_specs=(
            P(("leaf", "row"), "col"),
            P("leaf", None, "row", "col"),
            P("leaf", None, "col", None),
            P("leaf", None, None),
            P("leaf", None),
        ),
        out_specs=(P("leaf", None, "row", "col"), P("leaf", None, None, "col")),
        check_vma=False,
    )
```

```python
import functools

import jax
import jax.numpy as jnp
from jax import lax
from jax.experimental import pallas as pl
from jax.experimental.pallas import tpu as pltpu
from jax.sharding import PartitionSpec as P

TILE = 128
STEP = 2 * TILE
QUARTER = TILE // 2
F32 = jnp.float32
BF16 = jnp.bfloat16
VMEM_LIMIT = 56 * 2**20
WHOLE = pl.BlockSpec(memory_space=pltpu.VMEM)
ANY = pl.BlockSpec(memory_space=pl.ANY)


def split(x):
    high = x.astype(BF16)
    return high, (x - high.astype(F32)).astype(BF16)


def dot3(a, b):
    dot = functools.partial(jnp.dot, preferred_element_type=F32)
    return dot(a[0], b[0]) + (dot(a[0], b[1]) + dot(a[1], b[0]))


def put(pair, index, value):
    high, low = split(value)
    pair[0][index] = high
    pair[1][index] = low


def get(pair, index):
    return pair[0][index], pair[1][index]


def at(start, size, unit=TILE):
    return pl.ds(pl.multiple_of(start, unit), size)


def tiles(size, step=STEP):
    return [slice(m, m + step) for m in range(0, size, step)]


ALL = slice(None)


def load_panels(blocks, r, p, d, pt, dt, half):
    for slot in range(4):
        for turn in range(2):
            ref = blocks[2 * slot + turn]
            side = r if turn == 0 else 1 - r
            panel = ref[0:half, :]
            put(p, (at(side * half, half), slice(slot * TILE, (slot + 1) * TILE)), panel)
            put(pt, (slice(slot * TILE, (slot + 1) * TILE), at(side * half, half)), panel.T)
            for j in range(4):
                rows = at(slot * TILE + side * QUARTER, QUARTER, QUARTER)
                place = slice(j * TILE, (j + 1) * TILE)
                put(d, (rows, place), ref[half + j * QUARTER:half + (j + 1) * QUARTER, :])
    for slot in range(4):
        for j in range(4):
            rows, cols = slice(slot * TILE, (slot + 1) * TILE), slice(j * TILE, (j + 1) * TILE)
            for whole, turned in zip(d, dt):
                turned[cols, rows] = whole[rows, cols].T


def solve(p, pt, dt, a, dc, f, w, t, weights, emit_ab, emit_dg, join):
    width = dc[0].shape[1]
    for rows in tiles(p[0].shape[0]):
        k = rows.start // TILE
        for cols in tiles(width):
            value = dot3(get(p, (rows, ALL)), get(dc, (ALL, cols)))
            value = jnp.concatenate([value[:TILE] * weights[k], value[TILE:] * weights[k + 1]], axis=0)
            put(f, (rows, cols), value)
    join()
    for cols in tiles(width):
        for rows in tiles(a[0].shape[0]):
            value = dot3(get(a, (rows, ALL)), get(f, (ALL, cols)))
            emit_ab(rows, cols, -value)
            put(w, (rows, cols), value)
        for rows in tiles(pt[0].shape[0]):
            value = dot3(get(pt, (rows, ALL)), get(w, (ALL, cols)))
            put(t, (rows, cols), value + dc[0][rows, cols].astype(F32) + dc[1][rows, cols].astype(F32))
        for rows in tiles(dt[0].shape[0]):
            emit_dg(rows, cols, dot3(get(dt, (rows, ALL)), get(t, (ALL, cols))))


def scratch_pairs(*shapes):
    return [pltpu.VMEM(shape, BF16) for shape in shapes for _ in range(2)]


def pairs(refs):
    return [(refs[i], refs[i + 1]) for i in range(0, len(refs), 2)]


def call(kernel, scalars, operands, outs, scratch, places=None, micros=1):
    return pl.pallas_call(
        kernel,
        out_shape=[jax.ShapeDtypeStruct(o, F32) for o in outs],
        in_specs=[pl.BlockSpec(memory_space=pltpu.SMEM)] + (places or [WHOLE] * len(operands)),
        out_specs=[WHOLE] * len(outs),
        scratch_shapes=scratch,
        compiler_params=pltpu.CompilerParams(vmem_limit_bytes=VMEM_LIMIT),
        cost_estimate=pl.CostEstimate(flops=micros * 10**9, bytes_accessed=1, transcendentals=0),
    )(scalars, *operands)


def copy_all(copies, sems):
    started = [pltpu.make_async_copy(src, dst, sems.at[i]) for i, (src, dst) in enumerate(copies)]
    for one in started:
        one.start()
    for one in started:
        one.wait()


def move(kernel, scalars, operands, outs, count, micros=1):
    return call(
        kernel, scalars, operands, outs, [pltpu.SemaphoreType.DMA((count,))], [ANY] * len(operands), micros
    )


LINKS, LIST = 4, 8


def tail_of(s, start, own, order):
    spots = [start + k for k in range(own // TILE, order // TILE)]
    return [jnp.maximum(s[k], 0) for k in spots], [(s[k] >= 0).astype(F32) for k in spots]


def weights_of(s, start, order):
    return [(s[start + j] >= 0).astype(F32) for j in range(order // TILE)]


def pack_kernel(first, s, panels, inverse, *rest):
    outs, sems = rest[:-1], rest[-1]
    half = panels.shape[1]
    copies = []
    node = first
    for out in outs:
        for i in range(out.shape[0]):
            copies.append((panels.at[node], out.at[i, pl.ds(0, half)]))
            for j in range(inverse.shape[2] // TILE):
                copies.append((
                    inverse.at[node, at(s[0] * QUARTER, QUARTER, QUARTER), pl.ds(j * TILE, TILE)],
                    out.at[i, pl.ds(half + j * QUARTER, QUARTER)],
                ))
            node += 1
    copy_all(copies, sems)


def join_columns_kernel(s, *refs):
    out, sems = refs[-2:]
    width = refs[0].shape[1]
    copy_all([(ref, out.at[:, pl.ds(k * width, width)]) for k, ref in enumerate(refs[:-2])], sems)


def stack_kernel(s, *refs):
    out, sems = refs[-2:]
    copy_all([(ref, out.at[k]) for k, ref in enumerate(refs[:-2])], sems)


def swap_kernel(s, *refs):
    out, sems = refs[-2:]
    copies = [
        (ref.at[2 * pair + 1 - s[0]], out.at[pair, k]) for pair in range(2) for k, ref in enumerate(refs[:-2])
    ]
    copy_all(copies, sems)


def join_block(a, own, corner, rows_of, top, index, weight):
    put(a, (slice(0, own), slice(0, own)), top)
    for i in range(len(index)):
        place = slice(own + i * TILE, own + (i + 1) * TILE)
        value = rows_of(i) * weight[i]
        put(a, (place, slice(0, own)), value)
        put(a, (slice(0, own), place), value.T)
        for j in range(len(index)):
            put(a, (place, slice(own + j * TILE, own + (j + 1) * TILE)), corner(i, j) * (weight[i] * weight[j]))


def trunk_kernel(s, *refs):
    mine, theirs, sigmas = refs[:4], refs[4], refs[5:10]
    ext, grand, self_out, end_out = refs[10:14]
    stage, sigma, sems, corners, ab, dg = refs[14:20]
    p, d, a, f, w, t, pt, dt = pairs(refs[20:-1])
    r, c, leaf = s[0], s[1], s[2]
    order = a[0].shape[0]
    own = d[0].shape[0]
    half = order // 2
    far = c // 2
    count = 3

    def fetch(node, slot):
        found = []
        for k in range(4):
            found.append(pltpu.make_async_copy(mine[k].at[node], stage.at[slot, 2 * k], sems.at[slot, 2 * k]))
            found.append(pltpu.make_async_copy(theirs.at[k, node], stage.at[slot, 2 * k + 1], sems.at[slot, 2 * k + 1]))
        return found

    sigma_copies = [
        pltpu.make_async_copy(ref, sigma.at[k], sems.at[2, k])
        for k, ref in enumerate(list(sigmas[:4]) + [sigmas[4].at[m] for m in range(4)])
    ]
    for one in fetch(0, 0) + sigma_copies:
        one.start()

    def panels_of(node, slot):
        for one in fetch(node, slot):
            one.wait()
        load_panels([stage.at[slot, k] for k in range(8)], r, p, d, pt, dt, half)

    def emit_ab(rows, cols, value):
        ab[rows, cols] = value

    def emit_dg(rows, cols, value):
        dg[rows, cols] = value

    def columns_out(node):
        for out, col in ((self_out, c), (end_out, 3 * far)):
            out[node, 0:half, :] = ab[at(r * half, half), at(col * TILE, TILE)]
        self_out[node, half:, :] = dg[:, at(c * TILE, TILE)]
        end_out[node, half:, :] = dg[at(r * (own // 2), own // 2), at(3 * far * TILE, TILE)]

    panels_of(0, 0)
    for one in fetch(1, 1):
        one.start()

    def join_root():
        places = (c, 3 * far, 3 - c, 3 - 3 * far)
        span = order // 4
        for one in sigma_copies:
            one.wait()
        for m in range(4):
            for turn in range(2):
                side = r if turn == 0 else 1 - r
                rows = at(((leaf ^ m) * 2 + side) * TILE, TILE)
                for k in range(4):
                    value = sigma[4 * turn + m, :, k * span:(k + 1) * span]
                    put(a, (rows, at(places[k] * span, span)), value)

    solve(p, pt, dt, a, d, f, w, t, [1.0] * (order // TILE), emit_ab, emit_dg, join_root)
    columns_out(0)
    grand[...] = dg[...]
    for node in (1, 2):
        index, weight = tail_of(s, LIST + (node - 1) * (order // TILE), own, order)
        for i in range(len(index)):
            for j in range(len(index)):
                high, low = get(a, (at(index[i] * TILE, TILE), at(index[j] * TILE, TILE)))
                value = high.astype(F32) + low.astype(F32)
                corners[node - 1, i * TILE:(i + 1) * TILE, j * TILE:(j + 1) * TILE] = value
    for one in fetch(2, 0):
        one.start()
    root_ab = refs[-1]
    root_ab[...] = ab[...]

    @pl.loop(1, count)
    def _(node):
        start = LIST + (node - 1) * (order // TILE)
        index, weight = tail_of(s, start, own, order)
        panels_of(node, node % 2)

        def join():
            join_block(
                a, own,
                lambda i, j: corners[node - 1, i * TILE:(i + 1) * TILE, j * TILE:(j + 1) * TILE],
                lambda i: root_ab[at(index[i] * TILE, TILE), :], grand[...], index, weight,
            )

        solve(p, pt, dt, a, d, f, w, t, weights_of(s, start, order), emit_ab, emit_dg, join)
        columns_out(node)
        ext[node - 1, 0:half, :] = ab[0:half, :]
        ext[node - 1, half:, :] = dg[...]


def leaf_kernel(first, s, x0, x1, x2, x3, ex, ext, grand, self_out, core_out, end_out, cross_out, *rest):
    stage, sems, tails, top, grand_in, ab, dg = rest[:7]
    p, d, a, dc, f, w, t, pt, dt = pairs(rest[7:])
    r, c = s[0], s[1]
    blocks = [x for k, ref in enumerate((x0, x1, x2, x3)) for x in (ref.at[first - 3 + r], ex.at[(first - 3) // 2, k])]
    order = a[0].shape[0]
    own = d[0].shape[0]
    half = order // 2
    far = c // 2
    node = first + r
    start = LIST + (node - 1) * (order // TILE)
    index, weight = tail_of(s, start, own, order)
    parent = s[LINKS + node - 3] - 1
    copies = [pltpu.make_async_copy(ref, stage.at[k], sems.at[k]) for k, ref in enumerate(blocks)]
    later = [
        pltpu.make_async_copy(ext.at[parent, pl.ds(half, own)], top, sems.at[8]),
        pltpu.make_async_copy(grand, grand_in, sems.at[9]),
    ]
    for j, pick in enumerate(index):
        later.append(pltpu.make_async_copy(ext.at[parent, at(pick * TILE, TILE)], tails.at[j], sems.at[10 + j]))
    for one in copies + later:
        one.start()
    for one in copies:
        one.wait()
    load_panels([stage.at[k] for k in range(8)], r, p, d, pt, dt, half)
    dc[0][...] = d[0][:, at(far * STEP, STEP)]
    dc[1][...] = d[1][:, at(far * STEP, STEP)]

    def join():
        for one in later:
            one.wait()
        join_block(
            a, own, lambda i, j: grand_in[at(index[i] * TILE, TILE), at(index[j] * TILE, TILE)], lambda i: tails[i],
            top[...], index, weight,
        )

    def emit_ab(rows, cols, value):
        ab[rows, cols] = value

    def emit_dg(rows, cols, value):
        dg[rows, cols] = value

    solve(p, pt, dt, a, dc, f, w, t, weights_of(s, start, order), emit_ab, emit_dg, join)
    near_cols, end_cols = at((1 - far) * TILE, TILE), at(far * TILE, TILE)
    for out, side, cols in (
        (self_out, r, near_cols), (core_out, 1 - r, near_cols), (end_out, r, end_cols), (cross_out, 1 - r, end_cols)
    ):
        out[0:half, :] = ab[at(side * half, half), cols]
        share = out.shape[0] - half
        out[half:, :] = dg[:, cols] if share == own else dg[at(side * share, share), cols]


def shares_kernel(s, *refs):
    out, sems = refs[-2:]
    share = out.shape[0] // len(refs[:-2])
    copy_all([
        (ref.at[pl.ds(ref.shape[0] - share, share)], out.at[pl.ds(k * share, share)]) for k, ref in enumerate(refs[:-2])
    ], sems)


def upper_shares_kernel(s, upper, out, sems):
    shares_kernel(s, upper.at[0], upper.at[1], upper.at[2], out, sems)


def output_kernel(s, *refs):
    upper_self, upper_end, upper_shares, self_34, core_34, end_34, cross_34, shares_34 = refs[:8]
    self_56, core_56, end_56, cross_56 = refs[8:12]
    ab, dg, sems = refs[-3:]
    r, c = s[0], s[1]
    half = ab.shape[1]
    share = half // 2
    middle = (c == 1) | (c == 2)
    for core in range(2):
        @pl.when((r == core) & middle)
        def _():
            pair = [self_34, core_34] if core == 0 else [core_34, self_34]
            last = [self_56, core_56] if core == 0 else [core_56, self_56]
            copies = []
            for node, ref in enumerate([upper_self.at[k] for k in range(3)] + pair + last):
                copies.append((ref.at[pl.ds(0, half)], ab.at[node]))
                copies.append((ref.at[pl.ds(half, half)], dg.at[node]))
            copy_all(copies, sems)

        @pl.when((r == core) & jnp.logical_not(middle))
        def _():
            same, swapped = (3, 4) if core == 0 else (4, 3)
            last = [end_56, cross_56] if core == 0 else [cross_56, end_56]
            found = [(k, upper_end.at[k], upper_shares, k) for k in range(3)]
            found += [(same, end_34, shares_34, 1), (swapped, cross_34, shares_34, 0)]
            copies = []
            for node, ref, shares, k in found:
                copies.append((ref.at[pl.ds(0, half)], ab.at[node]))
                copies.append((ref.at[pl.ds(half, share)], dg.at[node, pl.ds(core * share, share)]))
                copies.append((shares.at[pl.ds(k * share, share)], dg.at[node, pl.ds((1 - core) * share, share)]))
            for node, ref in ((5, last[0]), (6, last[1])):
                copies.append((ref.at[pl.ds(0, half)], ab.at[node]))
                copies.append((ref.at[pl.ds(half, half)], dg.at[node]))
            copy_all(copies, sems)


def after(x, earlier):
    return lax.optimization_barrier((x, earlier))[0]


def chip_body(sigma_top, panels, inverse_diag, slot_lists, parent_links):
    r = lax.axis_index("row")
    c = lax.axis_index("col")
    leaf = lax.axis_index("leaf")
    panels, inverse, lists, links = panels[0], inverse_diag[0], slot_lists[0], parent_links[0]
    half = panels.shape[1]
    order = 2 * half
    own = inverse.shape[2]
    both = ("row", "col")
    routes = (((0, 1), (3, 2)), ((1, 2), (2, 1)), ((0, 2), (3, 1)))
    middles = (1, 2)
    swap = [(row * 4 + a, (1 - row) * 4 + a) for row in range(2) for a in middles]
    swap_ends = [(row * 4 + a, (1 - row) * 4 + a) for row in range(2) for a in (0, 3)]
    home = ((1, 0), (2, 3))
    home_cross = [(row * 4 + a, (1 - row) * 4 + b) for row in range(2) for a, b in home]
    leaf_routes = [
        [((lf * 2 + row) * 4 + a, ((lf ^ m) * 2 + row) * 4 + a) for lf in range(4) for row in range(2) for a in middles]
        for m in range(4)
    ]

    def straight(x):
        return [x] + [lax.ppermute(x, "col", route) for route in routes]

    def swapped(x):
        return lax.ppermute(x, both, swap)

    here = jnp.concatenate([jnp.stack([r, c, leaf, jnp.int32(0)]).astype(jnp.int32), links, lists.reshape(-1)])
    trunk = 3
    packed = half + own // 2

    def pack(first, count, sources):
        return move(functools.partial(pack_kernel, first), here, sources, [(count, packed, TILE)], 5 * count)[0]

    sigma_parts = straight(sigma_top)
    pack_t = pack(0, trunk, [panels, inverse])
    blocks_t = straight(pack_t)
    sigma_cols = move(join_columns_kernel, here, after(sigma_parts, pack_t), [(TILE, order)], 4)[0]
    sigma_rows = [sigma_cols] + [
        lax.ppermute(sigma_cols, ("leaf", "row", "col"), leaf_routes[m]) for m in range(1, 4)
    ]
    sigma_mine = move(stack_kernel, here, sigma_rows, [(4, TILE, order)], 4)[0]
    sigma_other = swapped(sigma_mine)
    pack_l = pack(trunk, 4, after([panels, inverse], pack_t))
    gathered = after(blocks_t, (sigma_mine, pack_l))
    other_t = swapped(move(stack_kernel, here, gathered, [(4, trunk, packed, TILE)], 4)[0])
    blocks_l = straight(after(pack_l, blocks_t[1:]))
    ext, grand, upper_self, upper_end = call(
        trunk_kernel, here, blocks_t + [other_t] + sigma_rows + [sigma_other],
        [(2, half + own, own), (own, own), (trunk, half + own, TILE), (trunk, packed, TILE)],
        [
            pltpu.VMEM((2, 8, packed, TILE), F32), pltpu.VMEM((8, TILE, order), F32), pltpu.SemaphoreType.DMA((3, 8)),
            pltpu.VMEM((2, order - own, order - own), F32), pltpu.VMEM((order, own), F32), pltpu.VMEM((own, own), F32),
        ] + scratch_pairs(
            (order, own), (own, own), (order, order), (order, own), (order, own), (own, own), (own, order), (own, own)
        ) + [pltpu.VMEM((order, own), F32)],
        [ANY] * 10, micros=1,
    )
    upper_home = lax.ppermute(upper_end, "col", home)
    tails = (order - own) // TILE
    leaf_scratch = [
        pltpu.VMEM((8, packed, TILE), F32), pltpu.SemaphoreType.DMA((10 + tails,)), pltpu.VMEM((tails, TILE, own), F32),
        pltpu.VMEM((own, own), F32), pltpu.VMEM((own, own), F32), pltpu.VMEM((order, STEP), F32),
        pltpu.VMEM((own, STEP), F32),
    ] + scratch_pairs(
        (order, own), (own, own), (order, order), (own, STEP), (order, STEP), (order, STEP), (own, STEP), (own, order),
        (own, own),
    )

    def leaves(first, theirs, end_rows):
        self_out, core_out, end_out, cross_out = call(
            functools.partial(leaf_kernel, first), here, blocks_l + [theirs, ext, grand],
            [(half + own, TILE)] * 2 + [(end_rows, TILE)] * 2, leaf_scratch, [ANY] * 7, micros=10,
        )
        return self_out, core_out, lax.ppermute(end_out, "col", home), lax.ppermute(cross_out, both, home_cross)

    chosen = after(blocks_l, (ext, upper_home))
    others = swapped(move(swap_kernel, here, chosen, [(2, 4, packed, TILE)], 8)[0])
    self_34, core_34, end_34, cross_34 = leaves(3, others, packed)
    self_56, core_56, end_56, cross_56 = leaves(5, after(others, self_34), half + own)

    def shared(kernel, parts, count):
        out = move(kernel, here, parts, [(count * (own // 2), TILE)], count)[0]
        return lax.ppermute(out, both, swap_ends)

    upper_shares = shared(upper_shares_kernel, [upper_home], 3)
    shares_34 = shared(shares_kernel, [end_34, cross_34], 2)
    count = panels.shape[0]
    ancestor_block, diagonal_block = move(
        output_kernel, here,
        [
            upper_self, upper_home, upper_shares, self_34, swapped(core_34), end_34, cross_34, shares_34, self_56,
            swapped(core_56), end_56, cross_56,
        ],
        [(count, half, TILE), (count, own, TILE)], 3 * count,
    )
    return (ancestor_block[None], diagonal_block[None])


def child_blocks(ancestors, products, diagonals, parent_ids, picks, tile):
    count_parents = ancestors.shape[0]
    slot_count = ancestors.shape[1] // tile
    own_width = diagonals.shape[1]
    own_tiles = own_width // tile
    tail = picks[:, own_tiles:]
    living = tail >= 0
    indices = jnp.maximum(tail, 0)
    child_count = tail.shape[0]
    tail_count = tail.shape[1]
    a_tiles = ancestors.reshape(count_parents, slot_count, tile, slot_count, tile)
    corner = a_tiles[parent_ids[:, None, None], indices[:, :, None], :, indices[:, None, :], :]
    corner = jnp.transpose(corner, (0, 1, 3, 2, 4))
    weights = (living[:, :, None] & living[:, None, :]).astype(jnp.float32)
    corner = corner * weights[:, :, None, :, None]
    corner = corner.reshape(child_count, tail_count * tile, tail_count * tile)
    p_tiles = products.reshape(count_parents, slot_count, tile, own_width)
    side = p_tiles[parent_ids[:, None], indices]
    side = side * living.astype(jnp.float32)[:, :, None, None]
    side = side.reshape(child_count, tail_count * tile, own_width)
    top_left = jnp.take(diagonals, parent_ids, axis=0)
    upper = jnp.concatenate([top_left, -jnp.transpose(side, (0, 2, 1))], axis=2)
    lower = jnp.concatenate([-side, corner], axis=2)
    return jnp.concatenate([upper, lower], axis=1)


def body(sigma_top, panels, inverse_diag, slot_lists, parent_links):
    highest = lax.Precision.HIGHEST
    row_count = lax.axis_size("row")
    col_count = lax.axis_size("col")
    row_index = lax.axis_index("row")
    col_index = lax.axis_index("col")
    panel_local = panels[0]
    inverse_local = inverse_diag[0]
    picks_all = slot_lists[0]
    parents = parent_links[0]
    block_rows = panel_local.shape[1]
    block_cols = panel_local.shape[2]
    diag_width = inverse_local.shape[2]
    diag_rows = diag_width // row_count
    tile = TILE
    top_rows = lax.all_gather(sigma_top, ("leaf", "row"), axis=0, tiled=True)
    top_full = lax.all_gather(top_rows, "col", axis=1, tiled=True)
    partial_factor = jnp.einsum("vrk,vkj->vrj", panel_local, inverse_local, precision=highest)
    inverse_band = lax.dynamic_slice_in_dim(inverse_local, row_index * diag_rows, diag_rows, 2)
    partial_gram = jnp.einsum("vki,vkj->vij", inverse_band, inverse_local, precision=highest)
    factor_rows = lax.psum(partial_factor, "col")
    gram_mine = lax.psum_scatter(partial_gram, "col", scatter_dimension=2, tiled=True)
    slots_here = block_rows // tile
    slot_ids = row_index * slots_here + jnp.arange(slots_here, dtype=jnp.int32)
    listed = jnp.take(picks_all, slot_ids, axis=1) >= 0
    living = jnp.concatenate([jnp.ones((1, slots_here), jnp.bool_), listed], axis=0)
    row_weight = jnp.repeat(living.astype(jnp.float32), tile, axis=1)
    factor_rows = factor_rows * row_weight[:, :, None]
    factor_mine = lax.dynamic_slice_in_dim(factor_rows, col_index * block_cols, block_cols, 2)
    factor_cols = lax.all_gather(factor_mine, "row", axis=1, tiled=True)
    ancestors = top_full[None]
    ancestor_parts = []
    diagonal_parts = []
    bounds = ((0, 1), (1, 3), (3, 7))
    for level_id, (first_node, last_node) in enumerate(bounds):
        own_rows = lax.dynamic_slice_in_dim(ancestors, row_index * block_rows, block_rows, 1)
        product_mine = jnp.einsum(
            "vra,vac->vrc", own_rows, factor_cols[first_node:last_node], precision=highest
        )
        partial_diag = jnp.einsum(
            "vrj,vrc->vjc", factor_rows[first_node:last_node], product_mine, precision=highest
        )
        diag_piece = lax.psum_scatter(partial_diag, "row", scatter_dimension=1, tiled=True)
        diag_piece = diag_piece + gram_mine[first_node:last_node]
        ancestor_parts.append(-product_mine)
        if level_id == 2:
            diag_cols = lax.all_gather(diag_piece, "row", axis=1, tiled=True)
        else:
            width_nodes = last_node - first_node
            product_all, diag_all = (
                lax.all_gather(product_mine[:, None], ("row", "col"), axis=1, tiled=True),
                lax.all_gather(diag_piece[:, None], ("row", "col"), axis=1, tiled=True),
            )
            product_full = product_all.reshape(
                width_nodes, row_count, col_count, block_rows, block_cols
            )
            product_full = product_full.transpose(0, 1, 3, 2, 4).reshape(
                width_nodes, row_count * block_rows, col_count * block_cols
            )
            diag_full = diag_all.reshape(width_nodes, row_count, col_count, diag_rows, block_cols)
            diag_full = diag_full.transpose(0, 1, 3, 2, 4).reshape(
                width_nodes, row_count * diag_rows, col_count * block_cols
            )
            diag_cols = lax.dynamic_slice_in_dim(diag_full, col_index * block_cols, block_cols, 2)
            if level_id == 0:
                parent_ids = jnp.zeros((2,), jnp.int32)
                picks_level = picks_all[0:2]
            else:
                parent_ids = parents - 1
                picks_level = picks_all[2:6]
            ancestors = child_blocks(
                ancestors, product_full, diag_full, parent_ids, picks_level, tile
            )
        diagonal_parts.append(diag_cols)
    ancestor_block = jnp.concatenate(ancestor_parts, axis=0)[None]
    diagonal_block = jnp.concatenate(diagonal_parts, axis=0)[None]
    return (ancestor_block, diagonal_block)


def solution(mesh):
    two_middles = (mesh.shape["leaf"], mesh.shape["row"], mesh.shape["col"]) == (4, 2, 4)
    return jax.shard_map(
        chip_body if two_middles else body,
        mesh=mesh,
        in_specs=(
            P(("leaf", "row"), "col"),
            P("leaf", None, "row", "col"),
            P("leaf", None, "col", None),
            P("leaf", None, None),
            P("leaf", None),
        ),
        out_specs=(P("leaf", None, "row", "col"), P("leaf", None, None, "col")),
        check_vma=False,
    )
```

```python
import functools

import jax
import jax.numpy as jnp
from jax import lax
from jax.experimental import pallas as pl
from jax.experimental.pallas import tpu as pltpu
from jax.sharding import PartitionSpec as P

TILE = 128
STEP = 2 * TILE
QUARTER = TILE // 2
F32 = jnp.float32
BF16 = jnp.bfloat16
VMEM_LIMIT = 56 * 2**20
WHOLE = pl.BlockSpec(memory_space=pltpu.VMEM)
ANY = pl.BlockSpec(memory_space=pl.ANY)


def split(x):
    high = x.astype(BF16)
    return high, (x - high.astype(F32)).astype(BF16)


def dot3(a, b):
    dot = functools.partial(jnp.dot, preferred_element_type=F32)
    return dot(a[0], b[0]) + (dot(a[0], b[1]) + dot(a[1], b[0]))


def put(pair, index, value):
    high, low = split(value)
    pair[0][index] = high
    pair[1][index] = low


def get(pair, index):
    return pair[0][index], pair[1][index]


def at(start, size, unit=TILE):
    return pl.ds(pl.multiple_of(start, unit), size)


def tiles(size, step=STEP):
    return [slice(m, m + step) for m in range(0, size, step)]


ALL = slice(None)


def load_panels(blocks, r, p, d, pt, dt, half):
    for slot in range(4):
        for turn in range(2):
            ref = blocks[2 * slot + turn]
            side = r if turn == 0 else 1 - r
            panel = ref[0:half, :]
            put(p, (at(side * half, half), slice(slot * TILE, (slot + 1) * TILE)), panel)
            put(pt, (slice(slot * TILE, (slot + 1) * TILE), at(side * half, half)), panel.T)
            for j in range(4):
                rows = at(slot * TILE + side * QUARTER, QUARTER, QUARTER)
                place = slice(j * TILE, (j + 1) * TILE)
                put(d, (rows, place), ref[half + j * QUARTER:half + (j + 1) * QUARTER, :])
    for slot in range(4):
        for j in range(4):
            rows, cols = slice(slot * TILE, (slot + 1) * TILE), slice(j * TILE, (j + 1) * TILE)
            for whole, turned in zip(d, dt):
                turned[cols, rows] = whole[rows, cols].T


def solve(p, pt, dt, a, dc, f, w, t, weights, emit_ab, emit_dg, join):
    width = dc[0].shape[1]
    for rows in tiles(p[0].shape[0]):
        k = rows.start // TILE
        for cols in tiles(width):
            value = dot3(get(p, (rows, ALL)), get(dc, (ALL, cols)))
            value = jnp.concatenate([value[:TILE] * weights[k], value[TILE:] * weights[k + 1]], axis=0)
            put(f, (rows, cols), value)
    join()
    for cols in tiles(width):
        for rows in tiles(a[0].shape[0]):
            value = dot3(get(a, (rows, ALL)), get(f, (ALL, cols)))
            emit_ab(rows, cols, -value)
            put(w, (rows, cols), value)
        for rows in tiles(pt[0].shape[0]):
            value = dot3(get(pt, (rows, ALL)), get(w, (ALL, cols)))
            put(t, (rows, cols), value + dc[0][rows, cols].astype(F32) + dc[1][rows, cols].astype(F32))
        for rows in tiles(dt[0].shape[0]):
            emit_dg(rows, cols, dot3(get(dt, (rows, ALL)), get(t, (ALL, cols))))


def scratch_pairs(*shapes):
    return [pltpu.VMEM(shape, BF16) for shape in shapes for _ in range(2)]


def pairs(refs):
    return [(refs[i], refs[i + 1]) for i in range(0, len(refs), 2)]


def call(kernel, scalars, operands, outs, scratch, places=None, micros=1):
    return pl.pallas_call(
        kernel,
        out_shape=[jax.ShapeDtypeStruct(o, F32) for o in outs],
        in_specs=[pl.BlockSpec(memory_space=pltpu.SMEM)] + (places or [WHOLE] * len(operands)),
        out_specs=[WHOLE] * len(outs),
        scratch_shapes=scratch,
        compiler_params=pltpu.CompilerParams(vmem_limit_bytes=VMEM_LIMIT),
        cost_estimate=pl.CostEstimate(flops=micros * 10**9, bytes_accessed=1, transcendentals=0),
    )(scalars, *operands)


def copy_all(copies, sems):
    started = [pltpu.make_async_copy(src, dst, sems.at[i]) for i, (src, dst) in enumerate(copies)]
    for one in started:
        one.start()
    for one in started:
        one.wait()


def move(kernel, scalars, operands, outs, count, micros=1):
    return call(
        kernel, scalars, operands, outs, [pltpu.SemaphoreType.DMA((count,))], [ANY] * len(operands), micros
    )


LINKS, LIST = 4, 8


def tail_of(s, start, own, order):
    spots = [start + k for k in range(own // TILE, order // TILE)]
    return [jnp.maximum(s[k], 0) for k in spots], [(s[k] >= 0).astype(F32) for k in spots]


def weights_of(s, start, order):
    return [(s[start + j] >= 0).astype(F32) for j in range(order // TILE)]


def pack_kernel(first, s, panels, inverse, *rest):
    outs, sems = rest[:-1], rest[-1]
    half = panels.shape[1]
    copies = []
    node = first
    for out in outs:
        for i in range(out.shape[0]):
            copies.append((panels.at[node], out.at[i, pl.ds(0, half)]))
            for j in range(inverse.shape[2] // TILE):
                copies.append((
                    inverse.at[node, at(s[0] * QUARTER, QUARTER, QUARTER), pl.ds(j * TILE, TILE)],
                    out.at[i, pl.ds(half + j * QUARTER, QUARTER)],
                ))
            node += 1
    copy_all(copies, sems)


def join_columns_kernel(s, *refs):
    out, sems = refs[-2:]
    width = refs[0].shape[1]
    copy_all([(ref, out.at[:, pl.ds(k * width, width)]) for k, ref in enumerate(refs[:-2])], sems)


def stack_kernel(s, *refs):
    out, sems = refs[-2:]
    copy_all([(ref, out.at[k]) for k, ref in enumerate(refs[:-2])], sems)


def swap_kernel(skips, s, *refs):
    out, sems = refs[-2:]
    copy_all([(ref.at[skips[k] + 1 - s[0]], out.at[k]) for k, ref in enumerate(refs[:-2])], sems)


def join_block(a, own, corner, rows_of, top, index, weight):
    put(a, (slice(0, own), slice(0, own)), top)
    for i in range(len(index)):
        place = slice(own + i * TILE, own + (i + 1) * TILE)
        value = rows_of(i) * weight[i]
        put(a, (place, slice(0, own)), value)
        put(a, (slice(0, own), place), value.T)
        for j in range(len(index)):
            put(a, (place, slice(own + j * TILE, own + (j + 1) * TILE)), corner(i, j) * (weight[i] * weight[j]))


def emitters(ab, dg):
    def emit_ab(rows, cols, value):
        ab[rows, cols] = value

    def emit_dg(rows, cols, value):
        dg[rows, cols] = value

    return emit_ab, emit_dg


def columns_out(s, ab, dg, self_out, end_out):
    r, c = s[0], s[1]
    half = ab.shape[0] // 2
    own = dg.shape[0]
    share = own // 2
    end_cols = at(3 * (c // 2) * TILE, TILE)
    self_out[0:half, :] = ab[at(r * half, half), at(c * TILE, TILE)]
    self_out[half:, :] = dg[:, at(c * TILE, TILE)]
    end_out[0:half, :] = ab[at(r * half, half), end_cols]
    end_out[half:, :] = dg[at(r * share, share), end_cols]


def root_kernel(s, *refs):
    mine, theirs, sigmas = refs[:4], refs[4], refs[5:10]
    ext, corners, self_out, end_out = refs[10:14]
    stage, sigma, sems = refs[14:17]
    p, d, a, f, w, t, pt, dt = pairs(refs[17:])
    r, c, leaf = s[0], s[1], s[2]
    order = a[0].shape[0]
    own = d[0].shape[0]
    half = order // 2
    far = c // 2
    blocks = [x for k in range(4) for x in (mine[k].at[0], theirs.at[k, 0])]
    copies = [pltpu.make_async_copy(ref, stage.at[k], sems.at[0, k]) for k, ref in enumerate(blocks)]
    pieces = list(sigmas[:4]) + [sigmas[4].at[m] for m in range(4)]
    later = [pltpu.make_async_copy(ref, sigma.at[k], sems.at[1, k]) for k, ref in enumerate(pieces)]
    for one in copies + later:
        one.start()
    for one in copies:
        one.wait()
    load_panels([stage.at[k] for k in range(8)], r, p, d, pt, dt, half)

    def join():
        places = (c, 3 * far, 3 - c, 3 - 3 * far)
        span = order // 4
        for one in later:
            one.wait()
        for m in range(4):
            for turn in range(2):
                side = r if turn == 0 else 1 - r
                rows = at(((leaf ^ m) * 2 + side) * TILE, TILE)
                for k in range(4):
                    put(a, (rows, at(places[k] * span, span)), sigma[4 * turn + m, :, k * span:(k + 1) * span])

    ab, dg = ext.at[pl.ds(0, order)], ext.at[pl.ds(order, own)]
    solve(p, pt, dt, a, d, f, w, t, [1.0] * (order // TILE), *emitters(ab, dg), join)
    columns_out(s, ab, dg, self_out, end_out)
    for node in range(2):
        index, weight = tail_of(s, LIST + node * (order // TILE), own, order)
        for i in range(len(index)):
            for j in range(len(index)):
                high, low = get(a, (at(index[i] * TILE, TILE), at(index[j] * TILE, TILE)))
                value = high.astype(F32) + low.astype(F32)
                corners[node, i * TILE:(i + 1) * TILE, j * TILE:(j + 1) * TILE] = value


def middle_kernel(s, *refs):
    mine, theirs, root, corners_in = refs[:4], refs[4], refs[5], refs[6]
    ext, self_out, end_out = refs[7:10]
    stage, root_in, corners, sems, ab, dg = refs[10:16]
    p, d, a, f, w, t, pt, dt = pairs(refs[16:])
    r = s[0]
    order = a[0].shape[0]
    own = d[0].shape[0]
    half = order // 2
    blocks = [[x for k in range(4) for x in (mine[k].at[node], theirs.at[k, node])] for node in (1, 2)]
    copies = [
        pltpu.make_async_copy(ref, stage.at[node, k], sems.at[node, k])
        for node in range(2) for k, ref in enumerate(blocks[node])
    ]
    later = [pltpu.make_async_copy(root, root_in, sems.at[2, 0]), pltpu.make_async_copy(corners_in, corners, sems.at[2, 1])]
    for one in copies[:8] + later + copies[8:]:
        one.start()
    for one in copies[:8] + later:
        one.wait()

    @pl.loop(0, 2)
    def _(node):
        start = LIST + node * (order // TILE)
        index, weight = tail_of(s, start, own, order)
        @pl.when(node == 1)
        def _():
            for one in copies[8:]:
                one.wait()

        load_panels([stage.at[node, k] for k in range(8)], r, p, d, pt, dt, half)

        def join():
            join_block(
                a, own,
                lambda i, j: corners[node, i * TILE:(i + 1) * TILE, j * TILE:(j + 1) * TILE],
                lambda i: root_in[at(index[i] * TILE, TILE), :], root_in[order:, :], index, weight,
            )

        solve(p, pt, dt, a, d, f, w, t, weights_of(s, start, order), *emitters(ab, dg), join)
        columns_out(s, ab, dg, self_out.at[node], end_out.at[node])
        ext[node, 0:half, :] = ab[0:half, :]
        ext[node, half:, :] = dg[...]


def leaf_kernel(first, skips, s, x0, x1, x2, x3, ex, ext, root, self_out, core_out, end_out, cross_out, *rest):
    stage, sems, tails, top, grand_in, ab, dg = rest[:7]
    p, d, a, dc, f, w, t, pt, dt = pairs(rest[7:])
    r, c = s[0], s[1]
    blocks = [x for k, ref in enumerate((x0, x1, x2, x3)) for x in (ref.at[skips[k] + r], ex.at[k])]
    order = a[0].shape[0]
    own = d[0].shape[0]
    half = order // 2
    far = c // 2
    node = first + r
    start = LIST + (node - 1) * (order // TILE)
    index, weight = tail_of(s, start, own, order)
    parent = s[LINKS + node - 3] - 1
    copies = [pltpu.make_async_copy(ref, stage.at[k], sems.at[k]) for k, ref in enumerate(blocks)]
    later = [
        pltpu.make_async_copy(ext.at[parent, pl.ds(half, own)], top, sems.at[8]),
        pltpu.make_async_copy(root.at[pl.ds(order, own)], grand_in, sems.at[9]),
    ]
    for j, pick in enumerate(index):
        later.append(pltpu.make_async_copy(ext.at[parent, at(pick * TILE, TILE)], tails.at[j], sems.at[10 + j]))
    for one in copies + later:
        one.start()
    for one in copies:
        one.wait()
    load_panels([stage.at[k] for k in range(8)], r, p, d, pt, dt, half)
    dc[0][...] = d[0][:, at(far * STEP, STEP)]
    dc[1][...] = d[1][:, at(far * STEP, STEP)]

    def join():
        for one in later:
            one.wait()
        join_block(
            a, own, lambda i, j: grand_in[at(index[i] * TILE, TILE), at(index[j] * TILE, TILE)], lambda i: tails[i],
            top[...], index, weight,
        )

    solve(p, pt, dt, a, dc, f, w, t, weights_of(s, start, order), *emitters(ab, dg), join)
    near_cols, end_cols = at((1 - far) * TILE, TILE), at(far * TILE, TILE)
    for out, side, cols in (
        (self_out, r, near_cols), (core_out, 1 - r, near_cols), (end_out, r, end_cols), (cross_out, 1 - r, end_cols)
    ):
        out[0:half, :] = ab[at(side * half, half), cols]
        share = out.shape[0] - half
        out[half:, :] = dg[:, cols] if share == own else dg[at(side * share, share), cols]


def shares_kernel(s, *refs):
    out, sems = refs[-2:]
    share = out.shape[0] // len(refs[:-2])
    copy_all([
        (ref.at[pl.ds(ref.shape[0] - share, share)], out.at[pl.ds(k * share, share)]) for k, ref in enumerate(refs[:-2])
    ], sems)


def upper_shares_kernel(s, root, upper, out, sems):
    shares_kernel(s, root, upper.at[0], upper.at[1], out, sems)


def output_kernel(s, *refs):
    root_self, root_end, upper_self, upper_end, upper_shares, self_34, core_34, end_34, cross_34, shares_34 = refs[:10]
    self_56, core_56, end_56, cross_56 = refs[10:14]
    ab, dg, sems = refs[-3:]
    r, c = s[0], s[1]
    half = ab.shape[1]
    share = half // 2
    middle = (c == 1) | (c == 2)
    for core in range(2):
        @pl.when((r == core) & middle)
        def _():
            pair = [self_34, core_34] if core == 0 else [core_34, self_34]
            last = [self_56, core_56] if core == 0 else [core_56, self_56]
            copies = []
            for node, ref in enumerate([root_self, upper_self.at[0], upper_self.at[1]] + pair + last):
                copies.append((ref.at[pl.ds(0, half)], ab.at[node]))
                copies.append((ref.at[pl.ds(half, half)], dg.at[node]))
            copy_all(copies, sems)

        @pl.when((r == core) & jnp.logical_not(middle))
        def _():
            same, swapped = (3, 4) if core == 0 else (4, 3)
            last = [end_56, cross_56] if core == 0 else [cross_56, end_56]
            found = [(0, root_end, upper_shares, 0)] + [(k, upper_end.at[k - 1], upper_shares, k) for k in (1, 2)]
            found += [(same, end_34, shares_34, 1), (swapped, cross_34, shares_34, 0)]
            copies = []
            for node, ref, shares, k in found:
                copies.append((ref.at[pl.ds(0, half)], ab.at[node]))
                copies.append((ref.at[pl.ds(half, share)], dg.at[node, pl.ds(core * share, share)]))
                copies.append((shares.at[pl.ds(k * share, share)], dg.at[node, pl.ds((1 - core) * share, share)]))
            for node, ref in ((5, last[0]), (6, last[1])):
                copies.append((ref.at[pl.ds(0, half)], ab.at[node]))
                copies.append((ref.at[pl.ds(half, half)], dg.at[node]))
            copy_all(copies, sems)


def after(x, earlier):
    return lax.optimization_barrier((x, earlier))[0]


def chip_body(sigma_top, panels, inverse_diag, slot_lists, parent_links):
    r = lax.axis_index("row")
    c = lax.axis_index("col")
    leaf = lax.axis_index("leaf")
    panels, inverse, lists, links = panels[0], inverse_diag[0], slot_lists[0], parent_links[0]
    half = panels.shape[1]
    order = 2 * half
    own = inverse.shape[2]
    both = ("row", "col")
    routes = (((0, 1), (3, 2)), ((1, 2), (2, 1)), ((0, 2), (3, 1)))
    middles = (1, 2)
    swap = [(row * 4 + a, (1 - row) * 4 + a) for row in range(2) for a in middles]
    swap_ends = [(row * 4 + a, (1 - row) * 4 + a) for row in range(2) for a in (0, 3)]
    home = ((1, 0), (2, 3))
    home_cross = [(row * 4 + a, (1 - row) * 4 + b) for row in range(2) for a, b in home]
    leaf_routes = [
        [((lf * 2 + row) * 4 + a, ((lf ^ m) * 2 + row) * 4 + a) for lf in range(4) for row in range(2) for a in middles]
        for m in range(4)
    ]

    def straight(x):
        return [x] + [lax.ppermute(x, "col", route) for route in routes]

    def swapped(x):
        return lax.ppermute(x, both, swap)

    here = jnp.concatenate([jnp.stack([r, c, leaf, jnp.int32(0)]).astype(jnp.int32), links, lists.reshape(-1)])
    trunk = 3
    packed = half + own // 2

    def pack(first, count, sources):
        return move(functools.partial(pack_kernel, first), here, sources, [(count, packed, TILE)], 5 * count)[0]

    sigma_parts = straight(sigma_top)
    pack_t = pack(0, trunk, [panels, inverse])
    blocks_t = straight(pack_t)
    sigma_cols = move(join_columns_kernel, here, after(sigma_parts, pack_t), [(TILE, order)], 4)[0]
    sigma_rows = [sigma_cols] + [
        lax.ppermute(sigma_cols, ("leaf", "row", "col"), leaf_routes[m]) for m in range(1, 4)
    ]
    sigma_mine = move(stack_kernel, here, sigma_rows, [(4, TILE, order)], 4)[0]
    sigma_other = swapped(sigma_mine)
    pack_l = pack(trunk, 4, after([panels, inverse], pack_t))
    gathered = after(blocks_t, (sigma_mine, pack_l))
    other_t = swapped(move(stack_kernel, here, gathered, [(4, trunk, packed, TILE)], 4)[0])
    near, between, far = routes
    queued = after(pack_l, blocks_t[1:])
    blocks_l = [pack_l, lax.ppermute(queued, "col", near), lax.ppermute(queued, "col", between)]
    far_34 = lax.ppermute(queued[:2], "col", far)
    node_scratch = scratch_pairs(
        (order, own), (own, own), (order, order), (order, own), (order, own), (own, own), (own, order), (own, own)
    )
    root, corners, root_self, root_end = call(
        root_kernel, here, blocks_t + [other_t] + sigma_rows + [sigma_other],
        [(order + own, own), (2, order - own, order - own), (half + own, TILE), (packed, TILE)],
        [pltpu.VMEM((8, packed, TILE), F32), pltpu.VMEM((8, TILE, order), F32), pltpu.SemaphoreType.DMA((2, 8))]
        + node_scratch, [ANY] * 10,
    )
    root_home = lax.ppermute(root_end, "col", home)
    ext, upper_self, upper_end = call(
        middle_kernel, here, blocks_t + [other_t, root, corners],
        [(2, half + own, own), (2, half + own, TILE), (2, packed, TILE)],
        [
            pltpu.VMEM((2, 8, packed, TILE), F32), pltpu.VMEM((order + own, own), F32),
            pltpu.VMEM((2, order - own, order - own), F32), pltpu.SemaphoreType.DMA((3, 8)),
            pltpu.VMEM((order, own), F32), pltpu.VMEM((own, own), F32),
        ] + node_scratch, [ANY] * 7,
    )
    far_56 = lax.ppermute(after(pack_l[2:], ext), "col", far)
    upper_home = lax.ppermute(upper_end, "col", home)
    tails = (order - own) // TILE
    leaf_scratch = [
        pltpu.VMEM((8, packed, TILE), F32), pltpu.SemaphoreType.DMA((10 + tails,)), pltpu.VMEM((tails, TILE, own), F32),
        pltpu.VMEM((own, own), F32), pltpu.VMEM((own, own), F32), pltpu.VMEM((order, STEP), F32),
        pltpu.VMEM((own, STEP), F32),
    ] + scratch_pairs(
        (order, own), (own, own), (order, order), (own, STEP), (order, STEP), (order, STEP), (own, STEP), (own, order),
        (own, own),
    )

    def leaves(first, last, skips, earlier, end_rows):
        blocks = after(blocks_l + [last], earlier)
        theirs = swapped(move(functools.partial(swap_kernel, skips), here, blocks, [(4, packed, TILE)], 4)[0])
        self_out, core_out, end_out, cross_out = call(
            functools.partial(leaf_kernel, first, skips), here, blocks + [theirs, ext, root],
            [(half + own, TILE)] * 2 + [(end_rows, TILE)] * 2, leaf_scratch, [ANY] * 7, micros=10,
        )
        return self_out, core_out, lax.ppermute(end_out, "col", home), lax.ppermute(cross_out, both, home_cross)

    self_34, core_34, end_34, cross_34 = leaves(3, far_34, (0, 0, 0, 0), (ext, root_home), packed)
    self_56, core_56, end_56, cross_56 = leaves(5, far_56, (2, 2, 2, 0), (self_34, upper_home), half + own)

    def shared(kernel, parts, count):
        out = move(kernel, here, parts, [(count * (own // 2), TILE)], count)[0]
        return lax.ppermute(out, both, swap_ends)

    upper_shares = shared(upper_shares_kernel, after([root_home, upper_home], self_56), 3)
    shares_34 = shared(shares_kernel, [end_34, cross_34], 2)
    count = panels.shape[0]
    ancestor_block, diagonal_block = move(
        output_kernel, here,
        [
            root_self, root_home, upper_self, upper_home, upper_shares, self_34, swapped(core_34), end_34, cross_34, shares_34, self_56,
            swapped(core_56), end_56, cross_56,
        ],
        [(count, half, TILE), (count, own, TILE)], 3 * count,
    )
    return (ancestor_block[None], diagonal_block[None])


def child_blocks(ancestors, products, diagonals, parent_ids, picks, tile):
    count_parents = ancestors.shape[0]
    slot_count = ancestors.shape[1] // tile
    own_width = diagonals.shape[1]
    own_tiles = own_width // tile
    tail = picks[:, own_tiles:]
    living = tail >= 0
    indices = jnp.maximum(tail, 0)
    child_count = tail.shape[0]
    tail_count = tail.shape[1]
    a_tiles = ancestors.reshape(count_parents, slot_count, tile, slot_count, tile)
    corner = a_tiles[parent_ids[:, None, None], indices[:, :, None], :, indices[:, None, :], :]
    corner = jnp.transpose(corner, (0, 1, 3, 2, 4))
    weights = (living[:, :, None] & living[:, None, :]).astype(jnp.float32)
    corner = corner * weights[:, :, None, :, None]
    corner = corner.reshape(child_count, tail_count * tile, tail_count * tile)
    p_tiles = products.reshape(count_parents, slot_count, tile, own_width)
    side = p_tiles[parent_ids[:, None], indices]
    side = side * living.astype(jnp.float32)[:, :, None, None]
    side = side.reshape(child_count, tail_count * tile, own_width)
    top_left = jnp.take(diagonals, parent_ids, axis=0)
    upper = jnp.concatenate([top_left, -jnp.transpose(side, (0, 2, 1))], axis=2)
    lower = jnp.concatenate([-side, corner], axis=2)
    return jnp.concatenate([upper, lower], axis=1)


def body(sigma_top, panels, inverse_diag, slot_lists, parent_links):
    highest = lax.Precision.HIGHEST
    row_count = lax.axis_size("row")
    col_count = lax.axis_size("col")
    row_index = lax.axis_index("row")
    col_index = lax.axis_index("col")
    panel_local = panels[0]
    inverse_local = inverse_diag[0]
    picks_all = slot_lists[0]
    parents = parent_links[0]
    block_rows = panel_local.shape[1]
    block_cols = panel_local.shape[2]
    diag_width = inverse_local.shape[2]
    diag_rows = diag_width // row_count
    tile = TILE
    top_rows = lax.all_gather(sigma_top, ("leaf", "row"), axis=0, tiled=True)
    top_full = lax.all_gather(top_rows, "col", axis=1, tiled=True)
    partial_factor = jnp.einsum("vrk,vkj->vrj", panel_local, inverse_local, precision=highest)
    inverse_band = lax.dynamic_slice_in_dim(inverse_local, row_index * diag_rows, diag_rows, 2)
    partial_gram = jnp.einsum("vki,vkj->vij", inverse_band, inverse_local, precision=highest)
    factor_rows = lax.psum(partial_factor, "col")
    gram_mine = lax.psum_scatter(partial_gram, "col", scatter_dimension=2, tiled=True)
    slots_here = block_rows // tile
    slot_ids = row_index * slots_here + jnp.arange(slots_here, dtype=jnp.int32)
    listed = jnp.take(picks_all, slot_ids, axis=1) >= 0
    living = jnp.concatenate([jnp.ones((1, slots_here), jnp.bool_), listed], axis=0)
    row_weight = jnp.repeat(living.astype(jnp.float32), tile, axis=1)
    factor_rows = factor_rows * row_weight[:, :, None]
    factor_mine = lax.dynamic_slice_in_dim(factor_rows, col_index * block_cols, block_cols, 2)
    factor_cols = lax.all_gather(factor_mine, "row", axis=1, tiled=True)
    ancestors = top_full[None]
    ancestor_parts = []
    diagonal_parts = []
    bounds = ((0, 1), (1, 3), (3, 7))
    for level_id, (first_node, last_node) in enumerate(bounds):
        own_rows = lax.dynamic_slice_in_dim(ancestors, row_index * block_rows, block_rows, 1)
        product_mine = jnp.einsum(
            "vra,vac->vrc", own_rows, factor_cols[first_node:last_node], precision=highest
        )
        partial_diag = jnp.einsum(
            "vrj,vrc->vjc", factor_rows[first_node:last_node], product_mine, precision=highest
        )
        diag_piece = lax.psum_scatter(partial_diag, "row", scatter_dimension=1, tiled=True)
        diag_piece = diag_piece + gram_mine[first_node:last_node]
        ancestor_parts.append(-product_mine)
        if level_id == 2:
            diag_cols = lax.all_gather(diag_piece, "row", axis=1, tiled=True)
        else:
            width_nodes = last_node - first_node
            product_all, diag_all = (
                lax.all_gather(product_mine[:, None], ("row", "col"), axis=1, tiled=True),
                lax.all_gather(diag_piece[:, None], ("row", "col"), axis=1, tiled=True),
            )
            product_full = product_all.reshape(
                width_nodes, row_count, col_count, block_rows, block_cols
            )
            product_full = product_full.transpose(0, 1, 3, 2, 4).reshape(
                width_nodes, row_count * block_rows, col_count * block_cols
            )
            diag_full = diag_all.reshape(width_nodes, row_count, col_count, diag_rows, block_cols)
            diag_full = diag_full.transpose(0, 1, 3, 2, 4).reshape(
                width_nodes, row_count * diag_rows, col_count * block_cols
            )
            diag_cols = lax.dynamic_slice_in_dim(diag_full, col_index * block_cols, block_cols, 2)
            if level_id == 0:
                parent_ids = jnp.zeros((2,), jnp.int32)
                picks_level = picks_all[0:2]
            else:
                parent_ids = parents - 1
                picks_level = picks_all[2:6]
            ancestors = child_blocks(
                ancestors, product_full, diag_full, parent_ids, picks_level, tile
            )
        diagonal_parts.append(diag_cols)
    ancestor_block = jnp.concatenate(ancestor_parts, axis=0)[None]
    diagonal_block = jnp.concatenate(diagonal_parts, axis=0)[None]
    return (ancestor_block, diagonal_block)


def solution(mesh):
    two_middles = (mesh.shape["leaf"], mesh.shape["row"], mesh.shape["col"]) == (4, 2, 4)
    return jax.shard_map(
        chip_body if two_middles else body,
        mesh=mesh,
        in_specs=(
            P(("leaf", "row"), "col"),
            P("leaf", None, "row", "col"),
            P("leaf", None, "col", None),
            P("leaf", None, None),
            P("leaf", None),
        ),
        out_specs=(P("leaf", None, "row", "col"), P("leaf", None, None, "col")),
        check_vma=False,
    )
```

```python
import functools

import jax
import jax.numpy as jnp
from jax import lax
from jax.experimental import pallas as pl
from jax.experimental.pallas import tpu as pltpu
from jax.sharding import PartitionSpec as P

TILE = 128
STEP = 2 * TILE
QUARTER = TILE // 2
F32 = jnp.float32
BF16 = jnp.bfloat16
VMEM_LIMIT = 56 * 2**20
WHOLE = pl.BlockSpec(memory_space=pltpu.VMEM)
ANY = pl.BlockSpec(memory_space=pl.ANY)


def split(x):
    high = x.astype(BF16)
    return high, (x - high.astype(F32)).astype(BF16)


def dot3(a, b):
    dot = functools.partial(jnp.dot, preferred_element_type=F32)
    return dot(a[0], b[0]) + (dot(a[0], b[1]) + dot(a[1], b[0]))


def put(pair, index, value):
    high, low = split(value)
    pair[0][index] = high
    pair[1][index] = low


def get(pair, index):
    return pair[0][index], pair[1][index]


def at(start, size, unit=TILE):
    return pl.ds(pl.multiple_of(start, unit), size)


def tiles(size, step=STEP):
    return [slice(m, m + step) for m in range(0, size, step)]


ALL = slice(None)


def load_panels(blocks, r, p, d, pt, dt, half):
    for slot in range(4):
        for turn in range(2):
            ref = blocks[2 * slot + turn]
            side = r if turn == 0 else 1 - r
            panel = ref[0:half, :]
            put(p, (at(side * half, half), slice(slot * TILE, (slot + 1) * TILE)), panel)
            put(pt, (slice(slot * TILE, (slot + 1) * TILE), at(side * half, half)), panel.T)
            for j in range(4):
                rows = at(slot * TILE + side * QUARTER, QUARTER, QUARTER)
                place = slice(j * TILE, (j + 1) * TILE)
                put(d, (rows, place), ref[half + j * QUARTER:half + (j + 1) * QUARTER, :])
    for slot in range(4):
        for j in range(4):
            rows, cols = slice(slot * TILE, (slot + 1) * TILE), slice(j * TILE, (j + 1) * TILE)
            for whole, turned in zip(d, dt):
                turned[cols, rows] = whole[rows, cols].T


def solve(p, pt, dt, a, dc, f, w, t, weights, emit_ab, emit_dg, join):
    width = dc[0].shape[1]
    for rows in tiles(p[0].shape[0]):
        k = rows.start // TILE
        for cols in tiles(width):
            value = dot3(get(p, (rows, ALL)), get(dc, (ALL, cols)))
            value = jnp.concatenate([value[:TILE] * weights[k], value[TILE:] * weights[k + 1]], axis=0)
            put(f, (rows, cols), value)
    join()
    for cols in tiles(width):
        for rows in tiles(a[0].shape[0]):
            value = dot3(get(a, (rows, ALL)), get(f, (ALL, cols)))
            emit_ab(rows, cols, -value)
            put(w, (rows, cols), value)
        for rows in tiles(pt[0].shape[0]):
            value = dot3(get(pt, (rows, ALL)), get(w, (ALL, cols)))
            put(t, (rows, cols), value + dc[0][rows, cols].astype(F32) + dc[1][rows, cols].astype(F32))
        for rows in tiles(dt[0].shape[0]):
            emit_dg(rows, cols, dot3(get(dt, (rows, ALL)), get(t, (ALL, cols))))


def scratch_pairs(*shapes):
    return [pltpu.VMEM(shape, BF16) for shape in shapes for _ in range(2)]


def pairs(refs):
    return [(refs[i], refs[i + 1]) for i in range(0, len(refs), 2)]


def call(kernel, scalars, operands, outs, scratch, places=None, micros=1):
    return pl.pallas_call(
        kernel,
        out_shape=[jax.ShapeDtypeStruct(o, F32) for o in outs],
        in_specs=[pl.BlockSpec(memory_space=pltpu.SMEM)] + (places or [WHOLE] * len(operands)),
        out_specs=[WHOLE] * len(outs),
        scratch_shapes=scratch,
        compiler_params=pltpu.CompilerParams(vmem_limit_bytes=VMEM_LIMIT),
        cost_estimate=pl.CostEstimate(flops=micros * 10**9, bytes_accessed=1, transcendentals=0),
    )(scalars, *operands)


def copy_all(copies, sems):
    started = [pltpu.make_async_copy(src, dst, sems.at[i]) for i, (src, dst) in enumerate(copies)]
    for one in started:
        one.start()
    for one in started:
        one.wait()


def move(kernel, scalars, operands, outs, count, micros=1):
    return call(
        kernel, scalars, operands, outs, [pltpu.SemaphoreType.DMA((count,))], [ANY] * len(operands), micros
    )


LINKS, LIST = 4, 8


def tail_of(s, start, own, order):
    spots = [start + k for k in range(own // TILE, order // TILE)]
    return [jnp.maximum(s[k], 0) for k in spots], [(s[k] >= 0).astype(F32) for k in spots]


def weights_of(s, start, order):
    return [(s[start + j] >= 0).astype(F32) for j in range(order // TILE)]


def pack_kernel(first, s, panels, inverse, *rest):
    outs, sems = rest[:-1], rest[-1]
    half = panels.shape[1]
    copies = []
    node = first
    for out in outs:
        for i in range(out.shape[0]):
            copies.append((panels.at[node], out.at[i, pl.ds(0, half)]))
            for j in range(inverse.shape[2] // TILE):
                copies.append((
                    inverse.at[node, at(s[0] * QUARTER, QUARTER, QUARTER), pl.ds(j * TILE, TILE)],
                    out.at[i, pl.ds(half + j * QUARTER, QUARTER)],
                ))
            node += 1
    copy_all(copies, sems)


def stack_kernel(s, *refs):
    out, sems = refs[-2:]
    copy_all([(ref, out.at[k]) for k, ref in enumerate(refs[:-2])], sems)


def swap_kernel(skips, s, *refs):
    out, sems = refs[-2:]
    copy_all([(ref.at[skips[k] + 1 - s[0]], out.at[k]) for k, ref in enumerate(refs[:-2])], sems)


def join_block(a, own, corner, rows_of, top, index, weight):
    put(a, (slice(0, own), slice(0, own)), top)
    for i in range(len(index)):
        place = slice(own + i * TILE, own + (i + 1) * TILE)
        value = rows_of(i) * weight[i]
        put(a, (place, slice(0, own)), value)
        put(a, (slice(0, own), place), value.T)
        for j in range(len(index)):
            put(a, (place, slice(own + j * TILE, own + (j + 1) * TILE)), corner(i, j) * (weight[i] * weight[j]))


def emitters(ab, dg):
    def emit_ab(rows, cols, value):
        ab[rows, cols] = value

    def emit_dg(rows, cols, value):
        dg[rows, cols] = value

    return emit_ab, emit_dg


def columns_out(s, ab, dg, self_out, end_out):
    r, c = s[0], s[1]
    half = ab.shape[0] // 2
    own = dg.shape[0]
    share = own // 2
    end_cols = at(3 * (c // 2) * TILE, TILE)
    self_out[0:half, :] = ab[at(r * half, half), at(c * TILE, TILE)]
    self_out[half:, :] = dg[:, at(c * TILE, TILE)]
    end_out[0:half, :] = ab[at(r * half, half), end_cols]
    end_out[half:, :] = dg[at(r * share, share), end_cols]


def root_kernel(s, *refs):
    mine, theirs, sigmas = refs[:4], refs[4], refs[5:10]
    ext, corners, self_out, end_out = refs[10:14]
    stage, sigma, sems = refs[14:17]
    p, d, a, f, w, t, pt, dt = pairs(refs[17:])
    r, leaf = s[0], s[2]
    order = a[0].shape[0]
    own = d[0].shape[0]
    half = order // 2
    blocks = [x for k in range(4) for x in (mine[k].at[0], theirs.at[k, 0])]
    copies = [pltpu.make_async_copy(ref, stage.at[k], sems.at[0, k]) for k, ref in enumerate(blocks)]
    pieces = list(sigmas[:4]) + [sigmas[4].at[m] for m in range(4)]
    later = [pltpu.make_async_copy(ref, sigma.at[k], sems.at[1, k]) for k, ref in enumerate(pieces)]
    for one in copies + later:
        one.start()
    for one in copies:
        one.wait()
    load_panels([stage.at[k] for k in range(8)], r, p, d, pt, dt, half)

    def join():
        for one in later:
            one.wait()
        for m in range(4):
            for turn in range(2):
                side = r if turn == 0 else 1 - r
                rows = at(((leaf ^ m) * 2 + side) * TILE, TILE)
                put(a, (rows, ALL), sigma[4 * turn + m])

    ab, dg = ext.at[pl.ds(0, order)], ext.at[pl.ds(order, own)]
    solve(p, pt, dt, a, d, f, w, t, [1.0] * (order // TILE), *emitters(ab, dg), join)
    columns_out(s, ab, dg, self_out, end_out)
    for node in range(2):
        index, weight = tail_of(s, LIST + node * (order // TILE), own, order)
        for i in range(len(index)):
            for j in range(len(index)):
                high, low = get(a, (at(index[i] * TILE, TILE), at(index[j] * TILE, TILE)))
                value = high.astype(F32) + low.astype(F32)
                corners[node, i * TILE:(i + 1) * TILE, j * TILE:(j + 1) * TILE] = value


def middle_kernel(s, *refs):
    mine, theirs, root, corners_in = refs[:4], refs[4], refs[5], refs[6]
    ext, self_out, end_out = refs[7:10]
    stage, root_in, corners, sems, ab, dg = refs[10:16]
    p, d, a, f, w, t, pt, dt = pairs(refs[16:])
    r = s[0]
    order = a[0].shape[0]
    own = d[0].shape[0]
    half = order // 2
    blocks = [[x for k in range(4) for x in (mine[k].at[node], theirs.at[k, node])] for node in (1, 2)]
    copies = [
        pltpu.make_async_copy(ref, stage.at[node, k], sems.at[node, k])
        for node in range(2) for k, ref in enumerate(blocks[node])
    ]
    later = [pltpu.make_async_copy(root, root_in, sems.at[2, 0]), pltpu.make_async_copy(corners_in, corners, sems.at[2, 1])]
    for one in copies[:8] + later + copies[8:]:
        one.start()
    for one in copies[:8] + later:
        one.wait()

    @pl.loop(0, 2)
    def _(node):
        start = LIST + node * (order // TILE)
        index, weight = tail_of(s, start, own, order)
        @pl.when(node == 1)
        def _():
            for one in copies[8:]:
                one.wait()

        load_panels([stage.at[node, k] for k in range(8)], r, p, d, pt, dt, half)

        def join():
            join_block(
                a, own,
                lambda i, j: corners[node, i * TILE:(i + 1) * TILE, j * TILE:(j + 1) * TILE],
                lambda i: root_in[at(index[i] * TILE, TILE), :], root_in[order:, :], index, weight,
            )

        solve(p, pt, dt, a, d, f, w, t, weights_of(s, start, order), *emitters(ab, dg), join)
        columns_out(s, ab, dg, self_out.at[node], end_out.at[node])
        ext[node, 0:half, :] = ab[0:half, :]
        ext[node, half:, :] = dg[...]


def leaf_kernel(first, skips, s, x0, x1, x2, x3, ex, ext, root, self_out, core_out, end_out, cross_out, *rest):
    stage, sems, tails, top, grand_in, ab, dg = rest[:7]
    p, d, a, dc, f, w, t, pt, dt = pairs(rest[7:])
    r, c = s[0], s[1]
    blocks = [x for k, ref in enumerate((x0, x1, x2, x3)) for x in (ref.at[skips[k] + r], ex.at[k])]
    order = a[0].shape[0]
    own = d[0].shape[0]
    half = order // 2
    far = c // 2
    node = first + r
    start = LIST + (node - 1) * (order // TILE)
    index, weight = tail_of(s, start, own, order)
    parent = s[LINKS + node - 3] - 1
    copies = [pltpu.make_async_copy(ref, stage.at[k], sems.at[k]) for k, ref in enumerate(blocks)]
    later = [
        pltpu.make_async_copy(ext.at[parent, pl.ds(half, own)], top, sems.at[8]),
        pltpu.make_async_copy(root.at[pl.ds(order, own)], grand_in, sems.at[9]),
    ]
    for j, pick in enumerate(index):
        later.append(pltpu.make_async_copy(ext.at[parent, at(pick * TILE, TILE)], tails.at[j], sems.at[10 + j]))
    for one in copies + later:
        one.start()
    for one in copies:
        one.wait()
    load_panels([stage.at[k] for k in range(8)], r, p, d, pt, dt, half)
    dc[0][...] = d[0][:, at(far * STEP, STEP)]
    dc[1][...] = d[1][:, at(far * STEP, STEP)]

    def join():
        for one in later:
            one.wait()
        join_block(
            a, own, lambda i, j: grand_in[at(index[i] * TILE, TILE), at(index[j] * TILE, TILE)], lambda i: tails[i],
            top[...], index, weight,
        )

    solve(p, pt, dt, a, dc, f, w, t, weights_of(s, start, order), *emitters(ab, dg), join)
    near_cols, end_cols = at((1 - far) * TILE, TILE), at(far * TILE, TILE)
    for out, side, cols in (
        (self_out, r, near_cols), (core_out, 1 - r, near_cols), (end_out, r, end_cols), (cross_out, 1 - r, end_cols)
    ):
        out[0:half, :] = ab[at(side * half, half), cols]
        share = out.shape[0] - half
        out[half:, :] = dg[:, cols] if share == own else dg[at(side * share, share), cols]


def shares_kernel(s, *refs):
    out, sems = refs[-2:]
    share = out.shape[0] // len(refs[:-2])
    copy_all([
        (ref.at[pl.ds(ref.shape[0] - share, share)], out.at[pl.ds(k * share, share)]) for k, ref in enumerate(refs[:-2])
    ], sems)


def upper_shares_kernel(s, root, upper, out, sems):
    shares_kernel(s, root, upper.at[0], upper.at[1], out, sems)


def first_output_kernel(s, *refs):
    root_self, root_end, upper_self, upper_end, upper_shares, self_34, core_34, end_34, cross_34, shares_34 = refs[:10]
    ab, dg, sems = refs[-3:]
    r, c = s[0], s[1]
    half = ab.shape[1]
    share = half // 2
    middle = (c == 1) | (c == 2)
    for core in range(2):
        @pl.when((r == core) & middle)
        def _():
            pair = [self_34, core_34] if core == 0 else [core_34, self_34]
            copies = []
            for node, ref in enumerate([root_self, upper_self.at[0], upper_self.at[1]] + pair):
                copies.append((ref.at[pl.ds(0, half)], ab.at[node]))
                copies.append((ref.at[pl.ds(half, half)], dg.at[node]))
            copy_all(copies, sems)

        @pl.when((r == core) & jnp.logical_not(middle))
        def _():
            same, swapped = (3, 4) if core == 0 else (4, 3)
            found = [(0, root_end, upper_shares, 0)] + [(k, upper_end.at[k - 1], upper_shares, k) for k in (1, 2)]
            found += [(same, end_34, shares_34, 1), (swapped, cross_34, shares_34, 0)]
            copies = []
            for node, ref, shares, k in found:
                copies.append((ref.at[pl.ds(0, half)], ab.at[node]))
                copies.append((ref.at[pl.ds(half, share)], dg.at[node, pl.ds(core * share, share)]))
                copies.append((shares.at[pl.ds(k * share, share)], dg.at[node, pl.ds((1 - core) * share, share)]))
            copy_all(copies, sems)


def last_output_kernel(s, ab_in, dg_in, self_56, core_56, end_56, cross_56, ab, dg, stage, sems):
    r, c = s[0], s[1]
    half = ab.shape[1]
    middle = (c == 1) | (c == 2)
    for core in range(2):
        for inner in range(2):
            @pl.when((r == core) & (middle == (inner == 1)))
            def _():
                pair = [self_56, core_56] if inner else [end_56, cross_56]
                if core == 1:
                    pair = pair[::-1]
                copy_all([(ref, stage.at[k]) for k, ref in enumerate(pair)], sems)
    copies = []
    for k in range(2):
        copies.append((stage.at[k, pl.ds(0, half)], ab.at[5 + k]))
        copies.append((stage.at[k, pl.ds(half, half)], dg.at[5 + k]))
    copy_all(copies, sems)


def after(x, earlier):
    return lax.optimization_barrier((x, earlier))[0]


def chip_body(sigma_top, panels, inverse_diag, slot_lists, parent_links):
    r = lax.axis_index("row")
    c = lax.axis_index("col")
    leaf = lax.axis_index("leaf")
    panels, inverse, lists, links = panels[0], inverse_diag[0], slot_lists[0], parent_links[0]
    half = panels.shape[1]
    order = 2 * half
    own = inverse.shape[2]
    both = ("row", "col")
    routes = (((0, 1), (3, 2)), ((1, 2), (2, 1)), ((0, 2), (3, 1)))
    middles = (1, 2)
    swap = [(row * 4 + a, (1 - row) * 4 + a) for row in range(2) for a in middles]
    swap_ends = [(row * 4 + a, (1 - row) * 4 + a) for row in range(2) for a in (0, 3)]
    home = ((1, 0), (2, 3))
    home_cross = [(row * 4 + a, (1 - row) * 4 + b) for row in range(2) for a, b in home]
    leaf_routes = [
        [((lf * 2 + row) * 4 + a, ((lf ^ m) * 2 + row) * 4 + a) for lf in range(4) for row in range(2) for a in middles]
        for m in range(4)
    ]

    def straight(x):
        return [x] + [lax.ppermute(x, "col", route) for route in routes]

    def swapped(x):
        return lax.ppermute(x, both, swap)

    here = jnp.concatenate([jnp.stack([r, c, leaf, jnp.int32(0)]).astype(jnp.int32), links, lists.reshape(-1)])
    trunk = 3
    packed = half + own // 2

    def pack(first, count, sources):
        return move(functools.partial(pack_kernel, first), here, sources, [(count, packed, TILE)], 5 * count)[0]

    sigma_cols = lax.all_gather(sigma_top, "col", axis=1, tiled=True)
    pack_t = pack(0, trunk, [panels, inverse])
    blocks_t = straight(pack_t)
    sigma_rows = [sigma_cols] + [
        lax.ppermute(sigma_cols, ("leaf", "row", "col"), leaf_routes[m]) for m in range(1, 4)
    ]
    sigma_mine = move(stack_kernel, here, sigma_rows, [(4, TILE, order)], 4)[0]
    sigma_other = swapped(sigma_mine)
    pack_l = pack(trunk, 4, after([panels, inverse], pack_t))
    gathered = after(blocks_t, (sigma_mine, pack_l))
    other_t = swapped(move(stack_kernel, here, gathered, [(4, trunk, packed, TILE)], 4)[0])
    near, between, far = routes
    queued = after(pack_l, blocks_t[1:])
    blocks_l = [pack_l, lax.ppermute(queued, "col", near), lax.ppermute(queued, "col", between)]
    far_34 = lax.ppermute(queued[:2], "col", far)
    node_scratch = scratch_pairs(
        (order, own), (own, own), (order, order), (order, own), (order, own), (own, own), (own, order), (own, own)
    )
    root, corners, root_self, root_end = call(
        root_kernel, here, blocks_t + [other_t] + sigma_rows + [sigma_other],
        [(order + own, own), (2, order - own, order - own), (half + own, TILE), (packed, TILE)],
        [pltpu.VMEM((8, packed, TILE), F32), pltpu.VMEM((8, TILE, order), F32), pltpu.SemaphoreType.DMA((2, 8))]
        + node_scratch, [ANY] * 10,
    )
    root_home = lax.ppermute(root_end, "col", home)
    ext, upper_self, upper_end = call(
        middle_kernel, here, blocks_t + [other_t, root, corners],
        [(2, half + own, own), (2, half + own, TILE), (2, packed, TILE)],
        [
            pltpu.VMEM((2, 8, packed, TILE), F32), pltpu.VMEM((order + own, own), F32),
            pltpu.VMEM((2, order - own, order - own), F32), pltpu.SemaphoreType.DMA((3, 8)),
            pltpu.VMEM((order, own), F32), pltpu.VMEM((own, own), F32),
        ] + node_scratch, [ANY] * 7,
    )
    far_56 = lax.ppermute(after(pack_l[2:], ext), "col", far)
    upper_home = lax.ppermute(upper_end, "col", home)
    tails = (order - own) // TILE
    leaf_scratch = [
        pltpu.VMEM((8, packed, TILE), F32), pltpu.SemaphoreType.DMA((10 + tails,)), pltpu.VMEM((tails, TILE, own), F32),
        pltpu.VMEM((own, own), F32), pltpu.VMEM((own, own), F32), pltpu.VMEM((order, STEP), F32),
        pltpu.VMEM((own, STEP), F32),
    ] + scratch_pairs(
        (order, own), (own, own), (order, order), (own, STEP), (order, STEP), (order, STEP), (own, STEP), (own, order),
        (own, own),
    )

    def leaves(first, last, skips, earlier, end_rows):
        blocks = after(blocks_l + [last], earlier)
        theirs = swapped(move(functools.partial(swap_kernel, skips), here, blocks, [(4, packed, TILE)], 4)[0])
        self_out, core_out, end_out, cross_out = call(
            functools.partial(leaf_kernel, first, skips), here, blocks + [theirs, ext, root],
            [(half + own, TILE)] * 2 + [(end_rows, TILE)] * 2, leaf_scratch, [ANY] * 7, micros=10,
        )
        return self_out, core_out, lax.ppermute(end_out, "col", home), lax.ppermute(cross_out, both, home_cross)

    self_34, core_34, end_34, cross_34 = leaves(3, far_34, (0, 0, 0, 0), (ext, root_home), packed)
    self_56, core_56, end_56, cross_56 = leaves(5, far_56, (2, 2, 2, 0), (self_34, upper_home, end_34), half + own)

    def shared(kernel, parts, count):
        out = move(kernel, here, parts, [(count * (own // 2), TILE)], count)[0]
        return lax.ppermute(out, both, swap_ends)

    upper_shares = shared(upper_shares_kernel, after([root_home, upper_home], self_56), 3)
    shares_34 = shared(shares_kernel, [end_34, cross_34], 2)
    count = panels.shape[0]
    shapes = [(count, half, TILE), (count, own, TILE)]
    first_outputs = move(
        first_output_kernel, here,
        [
            root_self, root_home, upper_self, upper_home, upper_shares, self_34, swapped(core_34), end_34, cross_34,
            shares_34,
        ],
        shapes, 15,
    )
    ancestor_block, diagonal_block = pl.pallas_call(
        last_output_kernel,
        out_shape=[jax.ShapeDtypeStruct(shape, F32) for shape in shapes],
        in_specs=[pl.BlockSpec(memory_space=pltpu.SMEM)] + [ANY] * 6,
        out_specs=[ANY] * 2,
        scratch_shapes=[pltpu.VMEM((2, half + own, TILE), F32), pltpu.SemaphoreType.DMA((4,))],
        input_output_aliases={1: 0, 2: 1},
        compiler_params=pltpu.CompilerParams(vmem_limit_bytes=VMEM_LIMIT),
    )(here, *first_outputs, self_56, swapped(core_56), end_56, cross_56)
    return (ancestor_block[None], diagonal_block[None])


def child_blocks(ancestors, products, diagonals, parent_ids, picks, tile):
    count_parents = ancestors.shape[0]
    slot_count = ancestors.shape[1] // tile
    own_width = diagonals.shape[1]
    own_tiles = own_width // tile
    tail = picks[:, own_tiles:]
    living = tail >= 0
    indices = jnp.maximum(tail, 0)
    child_count = tail.shape[0]
    tail_count = tail.shape[1]
    a_tiles = ancestors.reshape(count_parents, slot_count, tile, slot_count, tile)
    corner = a_tiles[parent_ids[:, None, None], indices[:, :, None], :, indices[:, None, :], :]
    corner = jnp.transpose(corner, (0, 1, 3, 2, 4))
    weights = (living[:, :, None] & living[:, None, :]).astype(jnp.float32)
    corner = corner * weights[:, :, None, :, None]
    corner = corner.reshape(child_count, tail_count * tile, tail_count * tile)
    p_tiles = products.reshape(count_parents, slot_count, tile, own_width)
    side = p_tiles[parent_ids[:, None], indices]
    side = side * living.astype(jnp.float32)[:, :, None, None]
    side = side.reshape(child_count, tail_count * tile, own_width)
    top_left = jnp.take(diagonals, parent_ids, axis=0)
    upper = jnp.concatenate([top_left, -jnp.transpose(side, (0, 2, 1))], axis=2)
    lower = jnp.concatenate([-side, corner], axis=2)
    return jnp.concatenate([upper, lower], axis=1)


def body(sigma_top, panels, inverse_diag, slot_lists, parent_links):
    highest = lax.Precision.HIGHEST
    row_count = lax.axis_size("row")
    col_count = lax.axis_size("col")
    row_index = lax.axis_index("row")
    col_index = lax.axis_index("col")
    panel_local = panels[0]
    inverse_local = inverse_diag[0]
    picks_all = slot_lists[0]
    parents = parent_links[0]
    block_rows = panel_local.shape[1]
    block_cols = panel_local.shape[2]
    diag_width = inverse_local.shape[2]
    diag_rows = diag_width // row_count
    tile = TILE
    top_rows = lax.all_gather(sigma_top, ("leaf", "row"), axis=0, tiled=True)
    top_full = lax.all_gather(top_rows, "col", axis=1, tiled=True)
    partial_factor = jnp.einsum("vrk,vkj->vrj", panel_local, inverse_local, precision=highest)
    inverse_band = lax.dynamic_slice_in_dim(inverse_local, row_index * diag_rows, diag_rows, 2)
    partial_gram = jnp.einsum("vki,vkj->vij", inverse_band, inverse_local, precision=highest)
    factor_rows = lax.psum(partial_factor, "col")
    gram_mine = lax.psum_scatter(partial_gram, "col", scatter_dimension=2, tiled=True)
    slots_here = block_rows // tile
    slot_ids = row_index * slots_here + jnp.arange(slots_here, dtype=jnp.int32)
    listed = jnp.take(picks_all, slot_ids, axis=1) >= 0
    living = jnp.concatenate([jnp.ones((1, slots_here), jnp.bool_), listed], axis=0)
    row_weight = jnp.repeat(living.astype(jnp.float32), tile, axis=1)
    factor_rows = factor_rows * row_weight[:, :, None]
    factor_mine = lax.dynamic_slice_in_dim(factor_rows, col_index * block_cols, block_cols, 2)
    factor_cols = lax.all_gather(factor_mine, "row", axis=1, tiled=True)
    ancestors = top_full[None]
    ancestor_parts = []
    diagonal_parts = []
    bounds = ((0, 1), (1, 3), (3, 7))
    for level_id, (first_node, last_node) in enumerate(bounds):
        own_rows = lax.dynamic_slice_in_dim(ancestors, row_index * block_rows, block_rows, 1)
        product_mine = jnp.einsum(
            "vra,vac->vrc", own_rows, factor_cols[first_node:last_node], precision=highest
        )
        partial_diag = jnp.einsum(
            "vrj,vrc->vjc", factor_rows[first_node:last_node], product_mine, precision=highest
        )
        diag_piece = lax.psum_scatter(partial_diag, "row", scatter_dimension=1, tiled=True)
        diag_piece = diag_piece + gram_mine[first_node:last_node]
        ancestor_parts.append(-product_mine)
        if level_id == 2:
            diag_cols = lax.all_gather(diag_piece, "row", axis=1, tiled=True)
        else:
            width_nodes = last_node - first_node
            product_all, diag_all = (
                lax.all_gather(product_mine[:, None], ("row", "col"), axis=1, tiled=True),
                lax.all_gather(diag_piece[:, None], ("row", "col"), axis=1, tiled=True),
            )
            product_full = product_all.reshape(
                width_nodes, row_count, col_count, block_rows, block_cols
            )
            product_full = product_full.transpose(0, 1, 3, 2, 4).reshape(
                width_nodes, row_count * block_rows, col_count * block_cols
            )
            diag_full = diag_all.reshape(width_nodes, row_count, col_count, diag_rows, block_cols)
            diag_full = diag_full.transpose(0, 1, 3, 2, 4).reshape(
                width_nodes, row_count * diag_rows, col_count * block_cols
            )
            diag_cols = lax.dynamic_slice_in_dim(diag_full, col_index * block_cols, block_cols, 2)
            if level_id == 0:
                parent_ids = jnp.zeros((2,), jnp.int32)
                picks_level = picks_all[0:2]
            else:
                parent_ids = parents - 1
                picks_level = picks_all[2:6]
            ancestors = child_blocks(
                ancestors, product_full, diag_full, parent_ids, picks_level, tile
            )
        diagonal_parts.append(diag_cols)
    ancestor_block = jnp.concatenate(ancestor_parts, axis=0)[None]
    diagonal_block = jnp.concatenate(diagonal_parts, axis=0)[None]
    return (ancestor_block, diagonal_block)


def solution(mesh):
    two_middles = (mesh.shape["leaf"], mesh.shape["row"], mesh.shape["col"]) == (4, 2, 4)
    return jax.shard_map(
        chip_body if two_middles else body,
        mesh=mesh,
        in_specs=(
            P(("leaf", "row"), "col"),
            P("leaf", None, "row", "col"),
            P("leaf", None, "col", None),
            P("leaf", None, None),
            P("leaf", None),
        ),
        out_specs=(P("leaf", None, "row", "col"), P("leaf", None, None, "col")),
        check_vma=False,
    )
```

```python
import functools

import jax
import jax.numpy as jnp
from jax import lax
from jax.experimental import pallas as pl
from jax.experimental.pallas import tpu as pltpu
from jax.sharding import PartitionSpec as P

TILE = 128
STEP = 2 * TILE
QUARTER = TILE // 2
F32 = jnp.float32
BF16 = jnp.bfloat16
VMEM_LIMIT = 56 * 2**20
WHOLE = pl.BlockSpec(memory_space=pltpu.VMEM)
ANY = pl.BlockSpec(memory_space=pl.ANY)


def split(x):
    high = x.astype(BF16)
    return high, (x - high.astype(F32)).astype(BF16)


def dot3(a, b):
    dot = functools.partial(jnp.dot, preferred_element_type=F32)
    return dot(a[0], b[0]) + (dot(a[0], b[1]) + dot(a[1], b[0]))


def put(pair, index, value):
    high, low = split(value)
    pair[0][index] = high
    pair[1][index] = low


def get(pair, index):
    return pair[0][index], pair[1][index]


def at(start, size, unit=TILE):
    return pl.ds(pl.multiple_of(start, unit), size)


def tiles(size, step=STEP):
    return [slice(m, m + step) for m in range(0, size, step)]


ALL = slice(None)


def load_panels(blocks, r, p, d, pt, dt, half):
    for slot in range(4):
        for turn in range(2):
            ref = blocks[2 * slot + turn]
            side = r if turn == 0 else 1 - r
            panel = ref[0:half, :]
            put(p, (at(side * half, half), slice(slot * TILE, (slot + 1) * TILE)), panel)
            put(pt, (slice(slot * TILE, (slot + 1) * TILE), at(side * half, half)), panel.T)
            for j in range(4):
                rows = at(slot * TILE + side * QUARTER, QUARTER, QUARTER)
                place = slice(j * TILE, (j + 1) * TILE)
                put(d, (rows, place), ref[half + j * QUARTER:half + (j + 1) * QUARTER, :])
    for slot in range(4):
        for j in range(4):
            rows, cols = slice(slot * TILE, (slot + 1) * TILE), slice(j * TILE, (j + 1) * TILE)
            for whole, turned in zip(d, dt):
                turned[cols, rows] = whole[rows, cols].T


def solve(p, pt, dt, a, dc, f, w, t, weights, emit_ab, emit_dg, join):
    width = dc[0].shape[1]
    for rows in tiles(p[0].shape[0]):
        k = rows.start // TILE
        for cols in tiles(width):
            value = dot3(get(p, (rows, ALL)), get(dc, (ALL, cols)))
            value = jnp.concatenate([value[:TILE] * weights[k], value[TILE:] * weights[k + 1]], axis=0)
            put(f, (rows, cols), value)
    join()
    for cols in tiles(width):
        for rows in tiles(a[0].shape[0]):
            value = dot3(get(a, (rows, ALL)), get(f, (ALL, cols)))
            emit_ab(rows, cols, -value)
            put(w, (rows, cols), value)
        for rows in tiles(pt[0].shape[0]):
            value = dot3(get(pt, (rows, ALL)), get(w, (ALL, cols)))
            put(t, (rows, cols), value + dc[0][rows, cols].astype(F32) + dc[1][rows, cols].astype(F32))
        for rows in tiles(dt[0].shape[0]):
            emit_dg(rows, cols, dot3(get(dt, (rows, ALL)), get(t, (ALL, cols))))


def scratch_pairs(*shapes):
    return [pltpu.VMEM(shape, BF16) for shape in shapes for _ in range(2)]


def pairs(refs):
    return [(refs[i], refs[i + 1]) for i in range(0, len(refs), 2)]


def call(kernel, scalars, operands, outs, scratch, places=None, micros=1):
    return pl.pallas_call(
        kernel,
        out_shape=[jax.ShapeDtypeStruct(o, F32) for o in outs],
        in_specs=[pl.BlockSpec(memory_space=pltpu.SMEM)] + (places or [WHOLE] * len(operands)),
        out_specs=[WHOLE] * len(outs),
        scratch_shapes=scratch,
        compiler_params=pltpu.CompilerParams(vmem_limit_bytes=VMEM_LIMIT),
        cost_estimate=pl.CostEstimate(flops=micros * 10**9, bytes_accessed=1, transcendentals=0),
    )(scalars, *operands)


def copy_all(copies, sems):
    started = [pltpu.make_async_copy(src, dst, sems.at[i]) for i, (src, dst) in enumerate(copies)]
    for one in started:
        one.start()
    for one in started:
        one.wait()


def move(kernel, scalars, operands, outs, count, micros=1):
    return call(
        kernel, scalars, operands, outs, [pltpu.SemaphoreType.DMA((count,))], [ANY] * len(operands), micros
    )


LINKS, LIST = 4, 8


def tail_of(s, start, own, order):
    spots = [start + k for k in range(own // TILE, order // TILE)]
    return [jnp.maximum(s[k], 0) for k in spots], [(s[k] >= 0).astype(F32) for k in spots]


def weights_of(s, start, order):
    return [(s[start + j] >= 0).astype(F32) for j in range(order // TILE)]


def pack_kernel(first, s, panels, inverse, *rest):
    outs, sems = rest[:-1], rest[-1]
    half = panels.shape[1]
    copies = []
    node = first
    for out in outs:
        for i in range(out.shape[0]):
            copies.append((panels.at[node], out.at[i, pl.ds(0, half)]))
            for j in range(inverse.shape[2] // TILE):
                copies.append((
                    inverse.at[node, at(s[0] * QUARTER, QUARTER, QUARTER), pl.ds(j * TILE, TILE)],
                    out.at[i, pl.ds(half + j * QUARTER, QUARTER)],
                ))
            node += 1
    copy_all(copies, sems)


def join_columns_kernel(s, *refs):
    out, sems = refs[-2:]
    width = refs[0].shape[1]
    copy_all([(ref, out.at[:, pl.ds(k * width, width)]) for k, ref in enumerate(refs[:-2])], sems)


def stack_kernel(s, *refs):
    out, sems = refs[-2:]
    copy_all([(ref, out.at[k]) for k, ref in enumerate(refs[:-2])], sems)


def swap_kernel(skips, s, *refs):
    blocks, outs, sems = refs[:4], refs[4:6], refs[6]
    copies = []
    for k, ref in enumerate(blocks):
        copies.append((ref.at[skips[k] + 1 - s[0], pl.ds(0, outs[0].shape[1])], outs[k // 2].at[k % 2]))
    copy_all(copies, sems)


def join_block(a, own, corner, rows_of, top, index, weight):
    put(a, (slice(0, own), slice(0, own)), top)
    for i in range(len(index)):
        place = slice(own + i * TILE, own + (i + 1) * TILE)
        value = rows_of(i) * weight[i]
        put(a, (place, slice(0, own)), value)
        put(a, (slice(0, own), place), value.T)
        for j in range(len(index)):
            put(a, (place, slice(own + j * TILE, own + (j + 1) * TILE)), corner(i, j) * (weight[i] * weight[j]))


def emitters(ab, dg):
    def emit_ab(rows, cols, value):
        ab[rows, cols] = value

    def emit_dg(rows, cols, value):
        dg[rows, cols] = value

    return emit_ab, emit_dg


def columns_out(s, ab, dg, self_out, end_out):
    r, c = s[0], s[1]
    half = ab.shape[0] // 2
    own = dg.shape[0]
    share = own // 2
    end_cols = at(3 * (c // 2) * TILE, TILE)
    self_out[0:half, :] = ab[at(r * half, half), at(c * TILE, TILE)]
    self_out[half:, :] = dg[:, at(c * TILE, TILE)]
    end_out[0:half, :] = ab[at(r * half, half), end_cols]
    end_out[half:, :] = dg[at(r * share, share), end_cols]


def root_kernel(s, *refs):
    mine, theirs, sigmas, leaves = refs[:4], refs[4], refs[5:10], refs[10]
    ext, corners, self_out, sent = refs[11:15]
    stage, sigma, end_out, sems = refs[15:19]
    p, d, a, f, w, t, pt, dt = pairs(refs[19:])
    r, c, leaf = s[0], s[1], s[2]
    far = c // 2
    middle = (c == 1) | (c == 2)
    order = a[0].shape[0]
    own = d[0].shape[0]
    half = order // 2
    blocks = [x for k in range(4) for x in (mine[k].at[0], theirs.at[k, 0])]
    copies = [pltpu.make_async_copy(ref, stage.at[k], sems.at[0, k]) for k, ref in enumerate(blocks)]
    pieces = list(sigmas[:4]) + [sigmas[4].at[m] for m in range(4)]
    later = [pltpu.make_async_copy(ref, sigma.at[k], sems.at[1, k]) for k, ref in enumerate(pieces)]
    for one in copies + later:
        one.start()
    for one in copies:
        one.wait()
    load_panels([stage.at[k] for k in range(8)], r, p, d, pt, dt, half)

    def join():
        places = (c, 3 * far, 3 - c, 3 - 3 * far)
        span = order // 4
        for one in later:
            one.wait()
        for m in range(4):
            for turn in range(2):
                side = r if turn == 0 else 1 - r
                rows = at(((leaf ^ m) * 2 + side) * TILE, TILE)
                for k in range(4):
                    put(a, (rows, at(places[k] * span, span)), sigma[4 * turn + m, :, k * span:(k + 1) * span])

    ab, dg = ext.at[pl.ds(0, order)], ext.at[pl.ds(order, own)]
    solve(p, pt, dt, a, d, f, w, t, [1.0] * (order // TILE), *emitters(ab, dg), join)
    columns_out(s, ab, dg, self_out, end_out)
    packed = end_out.shape[0]

    @pl.when(middle)
    def _():
        sent[0, 0:packed, :] = end_out[...]

    @pl.when(jnp.logical_not(middle))
    def _():
        copy_all([(leaves.at[2 + i], sent.at[i, pl.ds(0, packed)]) for i in range(2)], sems.at[2])

    for node in range(2):
        index, weight = tail_of(s, LIST + node * (order // TILE), own, order)
        for i in range(len(index)):
            for j in range(len(index)):
                high, low = get(a, (at(index[i] * TILE, TILE), at(index[j] * TILE, TILE)))
                value = high.astype(F32) + low.astype(F32)
                corners[node, i * TILE:(i + 1) * TILE, j * TILE:(j + 1) * TILE] = value


def middle_kernel(s, *refs):
    mine, theirs, root, corners_in = refs[:4], refs[4], refs[5], refs[6]
    ext, self_out, end_out = refs[7:10]
    stage, root_in, corners, sems, ab, dg = refs[10:16]
    p, d, a, f, w, t, pt, dt = pairs(refs[16:])
    r = s[0]
    order = a[0].shape[0]
    own = d[0].shape[0]
    half = order // 2
    blocks = [[x for k in range(4) for x in (mine[k].at[node], theirs.at[k, node])] for node in (1, 2)]
    copies = [
        pltpu.make_async_copy(ref, stage.at[node, k], sems.at[node, k])
        for node in range(2) for k, ref in enumerate(blocks[node])
    ]
    later = [pltpu.make_async_copy(root, root_in, sems.at[2, 0]), pltpu.make_async_copy(corners_in, corners, sems.at[2, 1])]
    for one in copies[:8] + later + copies[8:]:
        one.start()
    for one in copies[:8] + later:
        one.wait()

    @pl.loop(0, 2)
    def _(node):
        start = LIST + node * (order // TILE)
        index, weight = tail_of(s, start, own, order)
        @pl.when(node == 1)
        def _():
            for one in copies[8:]:
                one.wait()

        load_panels([stage.at[node, k] for k in range(8)], r, p, d, pt, dt, half)

        def join():
            join_block(
                a, own,
                lambda i, j: corners[node, i * TILE:(i + 1) * TILE, j * TILE:(j + 1) * TILE],
                lambda i: root_in[at(index[i] * TILE, TILE), :], root_in[order:, :], index, weight,
            )

        solve(p, pt, dt, a, d, f, w, t, weights_of(s, start, order), *emitters(ab, dg), join)
        columns_out(s, ab, dg, self_out.at[node], end_out.at[node])
        ext[node, 0:half, :] = ab[0:half, :]
        ext[node, half:, :] = dg[...]


def leaf_kernel(first, skips, s, x0, x1, x2, x3, ex0, ex1, ext, root, self_out, core_out, end_out, cross_out, *rest):
    stage, sems, tails, top, grand_in, ab, dg = rest[:7]
    p, d, a, dc, f, w, t, pt, dt = pairs(rest[7:])
    r, c = s[0], s[1]
    packed = stage.shape[1]
    blocks = [x for k, ref in enumerate((x0, x1, x2, x3)) for x in (ref.at[skips[k] + r, pl.ds(0, packed)], (ex0, ex1)[k // 2].at[k % 2])]
    order = a[0].shape[0]
    own = d[0].shape[0]
    half = order // 2
    far = c // 2
    node = first + r
    start = LIST + (node - 1) * (order // TILE)
    index, weight = tail_of(s, start, own, order)
    parent = s[LINKS + node - 3] - 1
    copies = [pltpu.make_async_copy(ref, stage.at[k], sems.at[k]) for k, ref in enumerate(blocks)]
    later = [
        pltpu.make_async_copy(ext.at[parent, pl.ds(half, own)], top, sems.at[8]),
        pltpu.make_async_copy(root.at[pl.ds(order, own)], grand_in, sems.at[9]),
    ]
    for j, pick in enumerate(index):
        later.append(pltpu.make_async_copy(ext.at[parent, at(pick * TILE, TILE)], tails.at[j], sems.at[10 + j]))
    for one in copies + later:
        one.start()
    for one in copies:
        one.wait()
    load_panels([stage.at[k] for k in range(8)], r, p, d, pt, dt, half)
    dc[0][...] = d[0][:, at(far * STEP, STEP)]
    dc[1][...] = d[1][:, at(far * STEP, STEP)]

    def join():
        for one in later:
            one.wait()
        join_block(
            a, own, lambda i, j: grand_in[at(index[i] * TILE, TILE), at(index[j] * TILE, TILE)], lambda i: tails[i],
            top[...], index, weight,
        )

    solve(p, pt, dt, a, dc, f, w, t, weights_of(s, start, order), *emitters(ab, dg), join)
    near_cols, end_cols = at((1 - far) * TILE, TILE), at(far * TILE, TILE)
    for out, side, cols in (
        (self_out, r, near_cols), (core_out, 1 - r, near_cols), (end_out, r, end_cols), (cross_out, 1 - r, end_cols)
    ):
        out[0:half, :] = ab[at(side * half, half), cols]
        share = out.shape[0] - half
        out[half:, :] = dg[:, cols] if share == own else dg[at(side * share, share), cols]


def shares_kernel(s, *refs):
    out, sems = refs[-2:]
    share = out.shape[0] // len(refs[:-2])
    copy_all([
        (ref.at[pl.ds(2 * share, share)], out.at[pl.ds(k * share, share)]) for k, ref in enumerate(refs[:-2])
    ], sems)


def upper_shares_kernel(s, root, upper, out, sems):
    shares_kernel(s, root.at[0], upper.at[0], upper.at[1], out, sems)


def first_output_kernel(s, *refs):
    root_self, root_end, upper_self, upper_end, upper_shares, self_34, core_34, end_34, cross_34, shares_34 = refs[:10]
    ab, dg, sems = refs[-3:]
    r, c = s[0], s[1]
    half = ab.shape[1]
    share = half // 2
    middle = (c == 1) | (c == 2)
    for core in range(2):
        @pl.when((r == core) & middle)
        def _():
            pair = [self_34, core_34] if core == 0 else [core_34, self_34]
            copies = []
            for node, ref in enumerate([root_self, upper_self.at[0], upper_self.at[1]] + pair):
                copies.append((ref.at[pl.ds(0, half)], ab.at[node]))
                copies.append((ref.at[pl.ds(half, half)], dg.at[node]))
            copy_all(copies, sems)

        @pl.when((r == core) & jnp.logical_not(middle))
        def _():
            same, swapped = (3, 4) if core == 0 else (4, 3)
            found = [(0, root_end.at[0], upper_shares, 0)] + [(k, upper_end.at[k - 1], upper_shares, k) for k in (1, 2)]
            found += [(same, end_34, shares_34, 1), (swapped, cross_34, shares_34, 0)]
            copies = []
            for node, ref, shares, k in found:
                copies.append((ref.at[pl.ds(0, half)], ab.at[node]))
                copies.append((ref.at[pl.ds(half, share)], dg.at[node, pl.ds(core * share, share)]))
                copies.append((shares.at[pl.ds(k * share, share)], dg.at[node, pl.ds((1 - core) * share, share)]))
            copy_all(copies, sems)


def last_output_kernel(s, ab_in, dg_in, self_56, core_56, end_56, cross_56, ab, dg, stage, sems):
    r, c = s[0], s[1]
    half = ab.shape[1]
    middle = (c == 1) | (c == 2)
    for core in range(2):
        for inner in range(2):
            @pl.when((r == core) & (middle == (inner == 1)))
            def _():
                pair = [self_56, core_56] if inner else [end_56, cross_56]
                if core == 1:
                    pair = pair[::-1]
                copy_all([(ref, stage.at[k]) for k, ref in enumerate(pair)], sems)
    copies = []
    for k in range(2):
        copies.append((stage.at[k, pl.ds(0, half)], ab.at[5 + k]))
        copies.append((stage.at[k, pl.ds(half, half)], dg.at[5 + k]))
    copy_all(copies, sems)


def after(x, earlier):
    return lax.optimization_barrier((x, earlier))[0]


def chip_body(sigma_top, panels, inverse_diag, slot_lists, parent_links):
    r = lax.axis_index("row")
    c = lax.axis_index("col")
    leaf = lax.axis_index("leaf")
    panels, inverse, lists, links = panels[0], inverse_diag[0], slot_lists[0], parent_links[0]
    half = panels.shape[1]
    order = 2 * half
    own = inverse.shape[2]
    both = ("row", "col")
    routes = (((0, 1), (3, 2)), ((1, 2), (2, 1)), ((0, 2), (3, 1)))
    middles = (1, 2)
    swap = [(row * 4 + a, (1 - row) * 4 + a) for row in range(2) for a in middles]
    swap_ends = [(row * 4 + a, (1 - row) * 4 + a) for row in range(2) for a in (0, 3)]
    home = ((1, 0), (2, 3))
    home_cross = [(row * 4 + a, (1 - row) * 4 + b) for row in range(2) for a, b in home]
    leaf_routes = [
        [((lf * 2 + row) * 4 + a, ((lf ^ m) * 2 + row) * 4 + a) for lf in range(4) for row in range(2) for a in middles]
        for m in range(4)
    ]

    def straight(x):
        return [x] + [lax.ppermute(x, "col", route) for route in routes]

    def swapped(x):
        return lax.ppermute(x, both, swap)

    here = jnp.concatenate([jnp.stack([r, c, leaf, jnp.int32(0)]).astype(jnp.int32), links, lists.reshape(-1)])
    trunk = 3
    packed = half + own // 2

    def pack(first, count, sources):
        return move(functools.partial(pack_kernel, first), here, sources, [(count, packed, TILE)], 5 * count)[0]

    sigma_parts = straight(sigma_top)
    pack_t = pack(0, trunk, [panels, inverse])
    blocks_t = straight(pack_t)
    sigma_cols = move(join_columns_kernel, here, after(sigma_parts, pack_t), [(TILE, order)], 4)[0]
    sigma_rows = [sigma_cols] + [
        lax.ppermute(sigma_cols, ("leaf", "row", "col"), leaf_routes[m]) for m in range(1, 4)
    ]
    sigma_mine = move(stack_kernel, here, sigma_rows, [(4, TILE, order)], 4)[0]
    sigma_other = swapped(sigma_mine)
    pack_l = pack(trunk, 4, after([panels, inverse], pack_t))
    gathered = after(blocks_t, (sigma_mine, pack_l))
    other_t = swapped(move(stack_kernel, here, gathered, [(4, trunk, packed, TILE)], 4)[0])
    near, between, far = routes
    queued = after(pack_l, blocks_t[1:])
    blocks_l = [pack_l, lax.ppermute(queued, "col", near), lax.ppermute(queued, "col", between)]
    far_34 = lax.ppermute(queued[:2], "col", far)
    node_scratch = scratch_pairs(
        (order, own), (own, own), (order, order), (order, own), (order, own), (own, own), (own, order), (own, own)
    )
    root, corners, root_self, sent = call(
        root_kernel, here, blocks_t + [other_t] + sigma_rows + [sigma_other, pack_l],
        [(order + own, own), (2, order - own, order - own), (half + own, TILE), (2, packed + QUARTER, TILE)],
        [
            pltpu.VMEM((8, packed, TILE), F32), pltpu.VMEM((8, TILE, order), F32), pltpu.VMEM((packed, TILE), F32),
            pltpu.SemaphoreType.DMA((3, 8)),
        ] + node_scratch, [ANY] * 11,
    )
    mixed = lax.ppermute(sent, "col", home + far)
    ext, upper_self, upper_end = call(
        middle_kernel, here, blocks_t + [other_t, root, corners],
        [(2, half + own, own), (2, half + own, TILE), (2, packed, TILE)],
        [
            pltpu.VMEM((2, 8, packed, TILE), F32), pltpu.VMEM((order + own, own), F32),
            pltpu.VMEM((2, order - own, order - own), F32), pltpu.SemaphoreType.DMA((3, 8)),
            pltpu.VMEM((order, own), F32), pltpu.VMEM((own, own), F32),
        ] + node_scratch, [ANY] * 7,
    )
    upper_home = lax.ppermute(upper_end, "col", home)
    tails = (order - own) // TILE
    leaf_scratch = [
        pltpu.VMEM((8, packed, TILE), F32), pltpu.SemaphoreType.DMA((10 + tails,)), pltpu.VMEM((tails, TILE, own), F32),
        pltpu.VMEM((own, own), F32), pltpu.VMEM((own, own), F32), pltpu.VMEM((order, STEP), F32),
        pltpu.VMEM((own, STEP), F32),
    ] + scratch_pairs(
        (order, own), (own, own), (order, order), (own, STEP), (order, STEP), (order, STEP), (own, STEP), (own, order),
        (own, own),
    )

    def leaves(first, last, skips, earlier, latest, end_rows):
        blocks = after(blocks_l, earlier) + [last]
        picked = move(functools.partial(swap_kernel, skips), here, blocks, [(2, packed, TILE)] * 2, 4)
        theirs = after([swapped(x) for x in picked], latest)
        self_out, core_out, end_out, cross_out = call(
            functools.partial(leaf_kernel, first, skips), here, blocks + theirs + [ext, root],
            [(half + own, TILE)] * 2 + [(end_rows, TILE)] * 2, leaf_scratch, [ANY] * 8, micros=10,
        )
        return self_out, core_out, lax.ppermute(end_out, "col", home), lax.ppermute(cross_out, both, home_cross)

    self_34, core_34, end_34, cross_34 = leaves(3, far_34, (0, 0, 0, 0), ext, mixed, packed)
    self_56, core_56, end_56, cross_56 = leaves(5, mixed, (2, 2, 2, 0), (self_34, upper_home), ext, half + own)

    def shared(kernel, parts, count):
        out = move(kernel, here, parts, [(count * (own // 2), TILE)], count)[0]
        return lax.ppermute(out, both, swap_ends)

    upper_shares = shared(upper_shares_kernel, after([mixed, upper_home], self_56), 3)
    shares_34 = shared(shares_kernel, [end_34, cross_34], 2)
    count = panels.shape[0]
    shapes = [(count, half, TILE), (count, own, TILE)]
    first_outputs = move(
        first_output_kernel, here,
        [
            root_self, mixed, upper_self, upper_home, upper_shares, self_34, swapped(core_34), end_34, cross_34,
            shares_34,
        ],
        shapes, 15,
    )
    ancestor_block, diagonal_block = pl.pallas_call(
        last_output_kernel,
        out_shape=[jax.ShapeDtypeStruct(shape, F32) for shape in shapes],
        in_specs=[pl.BlockSpec(memory_space=pltpu.SMEM)] + [ANY] * 6,
        out_specs=[ANY] * 2,
        scratch_shapes=[pltpu.VMEM((2, half + own, TILE), F32), pltpu.SemaphoreType.DMA((4,))],
        input_output_aliases={1: 0, 2: 1},
        compiler_params=pltpu.CompilerParams(vmem_limit_bytes=VMEM_LIMIT),
    )(here, *first_outputs, self_56, swapped(core_56), end_56, cross_56)
    return (ancestor_block[None], diagonal_block[None])


def child_blocks(ancestors, products, diagonals, parent_ids, picks, tile):
    count_parents = ancestors.shape[0]
    slot_count = ancestors.shape[1] // tile
    own_width = diagonals.shape[1]
    own_tiles = own_width // tile
    tail = picks[:, own_tiles:]
    living = tail >= 0
    indices = jnp.maximum(tail, 0)
    child_count = tail.shape[0]
    tail_count = tail.shape[1]
    a_tiles = ancestors.reshape(count_parents, slot_count, tile, slot_count, tile)
    corner = a_tiles[parent_ids[:, None, None], indices[:, :, None], :, indices[:, None, :], :]
    corner = jnp.transpose(corner, (0, 1, 3, 2, 4))
    weights = (living[:, :, None] & living[:, None, :]).astype(jnp.float32)
    corner = corner * weights[:, :, None, :, None]
    corner = corner.reshape(child_count, tail_count * tile, tail_count * tile)
    p_tiles = products.reshape(count_parents, slot_count, tile, own_width)
    side = p_tiles[parent_ids[:, None], indices]
    side = side * living.astype(jnp.float32)[:, :, None, None]
    side = side.reshape(child_count, tail_count * tile, own_width)
    top_left = jnp.take(diagonals, parent_ids, axis=0)
    upper = jnp.concatenate([top_left, -jnp.transpose(side, (0, 2, 1))], axis=2)
    lower = jnp.concatenate([-side, corner], axis=2)
    return jnp.concatenate([upper, lower], axis=1)


def body(sigma_top, panels, inverse_diag, slot_lists, parent_links):
    highest = lax.Precision.HIGHEST
    row_count = lax.axis_size("row")
    col_count = lax.axis_size("col")
    row_index = lax.axis_index("row")
    col_index = lax.axis_index("col")
    panel_local = panels[0]
    inverse_local = inverse_diag[0]
    picks_all = slot_lists[0]
    parents = parent_links[0]
    block_rows = panel_local.shape[1]
    block_cols = panel_local.shape[2]
    diag_width = inverse_local.shape[2]
    diag_rows = diag_width // row_count
    tile = TILE
    top_rows = lax.all_gather(sigma_top, ("leaf", "row"), axis=0, tiled=True)
    top_full = lax.all_gather(top_rows, "col", axis=1, tiled=True)
    partial_factor = jnp.einsum("vrk,vkj->vrj", panel_local, inverse_local, precision=highest)
    inverse_band = lax.dynamic_slice_in_dim(inverse_local, row_index * diag_rows, diag_rows, 2)
    partial_gram = jnp.einsum("vki,vkj->vij", inverse_band, inverse_local, precision=highest)
    factor_rows = lax.psum(partial_factor, "col")
    gram_mine = lax.psum_scatter(partial_gram, "col", scatter_dimension=2, tiled=True)
    slots_here = block_rows // tile
    slot_ids = row_index * slots_here + jnp.arange(slots_here, dtype=jnp.int32)
    listed = jnp.take(picks_all, slot_ids, axis=1) >= 0
    living = jnp.concatenate([jnp.ones((1, slots_here), jnp.bool_), listed], axis=0)
    row_weight = jnp.repeat(living.astype(jnp.float32), tile, axis=1)
    factor_rows = factor_rows * row_weight[:, :, None]
    factor_mine = lax.dynamic_slice_in_dim(factor_rows, col_index * block_cols, block_cols, 2)
    factor_cols = lax.all_gather(factor_mine, "row", axis=1, tiled=True)
    ancestors = top_full[None]
    ancestor_parts = []
    diagonal_parts = []
    bounds = ((0, 1), (1, 3), (3, 7))
    for level_id, (first_node, last_node) in enumerate(bounds):
        own_rows = lax.dynamic_slice_in_dim(ancestors, row_index * block_rows, block_rows, 1)
        product_mine = jnp.einsum(
            "vra,vac->vrc", own_rows, factor_cols[first_node:last_node], precision=highest
        )
        partial_diag = jnp.einsum(
            "vrj,vrc->vjc", factor_rows[first_node:last_node], product_mine, precision=highest
        )
        diag_piece = lax.psum_scatter(partial_diag, "row", scatter_dimension=1, tiled=True)
        diag_piece = diag_piece + gram_mine[first_node:last_node]
        ancestor_parts.append(-product_mine)
        if level_id == 2:
            diag_cols = lax.all_gather(diag_piece, "row", axis=1, tiled=True)
        else:
            width_nodes = last_node - first_node
            product_all, diag_all = (
                lax.all_gather(product_mine[:, None], ("row", "col"), axis=1, tiled=True),
                lax.all_gather(diag_piece[:, None], ("row", "col"), axis=1, tiled=True),
            )
            product_full = product_all.reshape(
                width_nodes, row_count, col_count, block_rows, block_cols
            )
            product_full = product_full.transpose(0, 1, 3, 2, 4).reshape(
                width_nodes, row_count * block_rows, col_count * block_cols
            )
            diag_full = diag_all.reshape(width_nodes, row_count, col_count, diag_rows, block_cols)
            diag_full = diag_full.transpose(0, 1, 3, 2, 4).reshape(
                width_nodes, row_count * diag_rows, col_count * block_cols
            )
            diag_cols = lax.dynamic_slice_in_dim(diag_full, col_index * block_cols, block_cols, 2)
            if level_id == 0:
                parent_ids = jnp.zeros((2,), jnp.int32)
                picks_level = picks_all[0:2]
            else:
                parent_ids = parents - 1
                picks_level = picks_all[2:6]
            ancestors = child_blocks(
                ancestors, product_full, diag_full, parent_ids, picks_level, tile
            )
        diagonal_parts.append(diag_cols)
    ancestor_block = jnp.concatenate(ancestor_parts, axis=0)[None]
    diagonal_block = jnp.concatenate(diagonal_parts, axis=0)[None]
    return (ancestor_block, diagonal_block)


def solution(mesh):
    two_middles = (mesh.shape["leaf"], mesh.shape["row"], mesh.shape["col"]) == (4, 2, 4)
    return jax.shard_map(
        chip_body if two_middles else body,
        mesh=mesh,
        in_specs=(
            P(("leaf", "row"), "col"),
            P("leaf", None, "row", "col"),
            P("leaf", None, "col", None),
            P("leaf", None, None),
            P("leaf", None),
        ),
        out_specs=(P("leaf", None, "row", "col"), P("leaf", None, None, "col")),
        check_vma=False,
    )
```

```python
import functools

import jax
import jax.numpy as jnp
from jax import lax
from jax.experimental import pallas as pl
from jax.experimental.pallas import tpu as pltpu
from jax.sharding import PartitionSpec as P

TILE = 128
STEP = 2 * TILE
QUARTER = TILE // 2
F32 = jnp.float32
BF16 = jnp.bfloat16
VMEM_LIMIT = 56 * 2**20
WHOLE = pl.BlockSpec(memory_space=pltpu.VMEM)
ANY = pl.BlockSpec(memory_space=pl.ANY)


def split(x):
    high = x.astype(BF16)
    return high, (x - high.astype(F32)).astype(BF16)


def dot3(a, b):
    dot = functools.partial(jnp.dot, preferred_element_type=F32)
    return dot(a[0], b[0]) + (dot(a[0], b[1]) + dot(a[1], b[0]))


def put(pair, index, value):
    high, low = split(value)
    pair[0][index] = high
    pair[1][index] = low


def get(pair, index):
    return pair[0][index], pair[1][index]


def at(start, size, unit=TILE):
    return pl.ds(pl.multiple_of(start, unit), size)


def tiles(size, step=STEP):
    return [slice(m, m + step) for m in range(0, size, step)]


ALL = slice(None)


def load_panels(blocks, r, p, d, pt, dt, half):
    for slot in range(4):
        for turn in range(2):
            ref = blocks[2 * slot + turn]
            side = r if turn == 0 else 1 - r
            panel = ref[0:half, :]
            put(p, (at(side * half, half), slice(slot * TILE, (slot + 1) * TILE)), panel)
            put(pt, (slice(slot * TILE, (slot + 1) * TILE), at(side * half, half)), panel.T)
            for j in range(4):
                rows = at(slot * TILE + side * QUARTER, QUARTER, QUARTER)
                place = slice(j * TILE, (j + 1) * TILE)
                put(d, (rows, place), ref[half + j * QUARTER:half + (j + 1) * QUARTER, :])
    for slot in range(4):
        for j in range(4):
            rows, cols = slice(slot * TILE, (slot + 1) * TILE), slice(j * TILE, (j + 1) * TILE)
            for whole, turned in zip(d, dt):
                turned[cols, rows] = whole[rows, cols].T


def solve(p, pt, dt, a, dc, f, w, t, weights, emit_ab, emit_dg, join):
    width = dc[0].shape[1]
    for rows in tiles(p[0].shape[0]):
        k = rows.start // TILE
        for cols in tiles(width):
            value = dot3(get(p, (rows, ALL)), get(dc, (ALL, cols)))
            value = jnp.concatenate([value[:TILE] * weights[k], value[TILE:] * weights[k + 1]], axis=0)
            put(f, (rows, cols), value)
    join()
    for cols in tiles(width):
        for rows in tiles(a[0].shape[0]):
            value = dot3(get(a, (rows, ALL)), get(f, (ALL, cols)))
            emit_ab(rows, cols, -value)
            put(w, (rows, cols), value)
        for rows in tiles(pt[0].shape[0]):
            value = dot3(get(pt, (rows, ALL)), get(w, (ALL, cols)))
            put(t, (rows, cols), value + dc[0][rows, cols].astype(F32) + dc[1][rows, cols].astype(F32))
        for rows in tiles(dt[0].shape[0]):
            emit_dg(rows, cols, dot3(get(dt, (rows, ALL)), get(t, (ALL, cols))))


def scratch_pairs(*shapes):
    return [pltpu.VMEM(shape, BF16) for shape in shapes for _ in range(2)]


def pairs(refs):
    return [(refs[i], refs[i + 1]) for i in range(0, len(refs), 2)]


def call(kernel, scalars, operands, outs, scratch, places=None, micros=1):
    return pl.pallas_call(
        kernel,
        out_shape=[jax.ShapeDtypeStruct(o, F32) for o in outs],
        in_specs=[pl.BlockSpec(memory_space=pltpu.SMEM)] + (places or [WHOLE] * len(operands)),
        out_specs=[WHOLE] * len(outs),
        scratch_shapes=scratch,
        compiler_params=pltpu.CompilerParams(vmem_limit_bytes=VMEM_LIMIT),
        cost_estimate=pl.CostEstimate(flops=micros * 10**9, bytes_accessed=1, transcendentals=0),
    )(scalars, *operands)


def copy_all(copies, sems):
    started = [pltpu.make_async_copy(src, dst, sems.at[i]) for i, (src, dst) in enumerate(copies)]
    for one in started:
        one.start()
    for one in started:
        one.wait()


def move(kernel, scalars, operands, outs, count, micros=1):
    return call(
        kernel, scalars, operands, outs, [pltpu.SemaphoreType.DMA((count,))], [ANY] * len(operands), micros
    )


LINKS, LIST = 4, 8


def tail_of(s, start, own, order):
    spots = [start + k for k in range(own // TILE, order // TILE)]
    return [jnp.maximum(s[k], 0) for k in spots], [(s[k] >= 0).astype(F32) for k in spots]


def weights_of(s, start, order):
    return [(s[start + j] >= 0).astype(F32) for j in range(order // TILE)]


def pack_kernel(first, s, panels, inverse, *rest):
    outs, sems = rest[:-1], rest[-1]
    half = panels.shape[1]
    copies = []
    node = first
    for out in outs:
        for i in range(out.shape[0]):
            copies.append((panels.at[node], out.at[i, pl.ds(0, half)]))
            for j in range(inverse.shape[2] // TILE):
                copies.append((
                    inverse.at[node, at(s[0] * QUARTER, QUARTER, QUARTER), pl.ds(j * TILE, TILE)],
                    out.at[i, pl.ds(half + j * QUARTER, QUARTER)],
                ))
            node += 1
    copy_all(copies, sems)


def join_columns_kernel(s, *refs):
    out, sems = refs[-2:]
    width = refs[0].shape[1]
    copy_all([(ref, out.at[:, pl.ds(k * width, width)]) for k, ref in enumerate(refs[:-2])], sems)


def stack_kernel(s, *refs):
    out, sems = refs[-2:]
    copy_all([(ref, out.at[k]) for k, ref in enumerate(refs[:-2])], sems)


def swap_kernel(s, *refs):
    blocks, outs, sems = refs[:4], refs[4:6], refs[6]
    copy_all([
        (ref.at[2 * pair + 1 - s[0]], out.at[k]) for pair, out in enumerate(outs) for k, ref in enumerate(blocks)
    ], sems)


def join_block(a, own, corner, rows_of, top, index, weight):
    put(a, (slice(0, own), slice(0, own)), top)
    for i in range(len(index)):
        place = slice(own + i * TILE, own + (i + 1) * TILE)
        value = rows_of(i) * weight[i]
        put(a, (place, slice(0, own)), value)
        put(a, (slice(0, own), place), value.T)
        for j in range(len(index)):
            put(a, (place, slice(own + j * TILE, own + (j + 1) * TILE)), corner(i, j) * (weight[i] * weight[j]))


def trunk_kernel(s, *refs):
    mine, theirs, sigmas = refs[:4], refs[4], refs[5:10]
    ext, grand, self_out, end_out = refs[10:14]
    stage, sigma, sems, corners, ab, dg = refs[14:20]
    p, d, a, f, w, t, pt, dt = pairs(refs[20:-1])
    r, c, leaf = s[0], s[1], s[2]
    order = a[0].shape[0]
    own = d[0].shape[0]
    half = order // 2
    far = c // 2
    count = 3

    def fetch(node, slot):
        found = []
        for k in range(4):
            found.append(pltpu.make_async_copy(mine[k].at[node], stage.at[slot, 2 * k], sems.at[slot, 2 * k]))
            found.append(pltpu.make_async_copy(theirs.at[k, node], stage.at[slot, 2 * k + 1], sems.at[slot, 2 * k + 1]))
        return found

    sigma_copies = [
        pltpu.make_async_copy(ref, sigma.at[k], sems.at[2, k])
        for k, ref in enumerate(list(sigmas[:4]) + [sigmas[4].at[m] for m in range(4)])
    ]
    for one in fetch(0, 0) + sigma_copies:
        one.start()

    def panels_of(node, slot):
        for one in fetch(node, slot):
            one.wait()
        load_panels([stage.at[slot, k] for k in range(8)], r, p, d, pt, dt, half)

    def emit_ab(rows, cols, value):
        ab[rows, cols] = value

    def emit_dg(rows, cols, value):
        dg[rows, cols] = value

    def columns_out(node):
        for out, col in ((self_out, c), (end_out, 3 * far)):
            out[node, 0:half, :] = ab[at(r * half, half), at(col * TILE, TILE)]
        self_out[node, half:, :] = dg[:, at(c * TILE, TILE)]
        end_out[node, half:, :] = dg[at(r * (own // 2), own // 2), at(3 * far * TILE, TILE)]

    panels_of(0, 0)
    for one in fetch(1, 1):
        one.start()

    def join_root():
        places = (c, 3 * far, 3 - c, 3 - 3 * far)
        span = order // 4
        for one in sigma_copies:
            one.wait()
        for m in range(4):
            for turn in range(2):
                side = r if turn == 0 else 1 - r
                rows = at(((leaf ^ m) * 2 + side) * TILE, TILE)
                for k in range(4):
                    value = sigma[4 * turn + m, :, k * span:(k + 1) * span]
                    put(a, (rows, at(places[k] * span, span)), value)

    solve(p, pt, dt, a, d, f, w, t, [1.0] * (order // TILE), emit_ab, emit_dg, join_root)
    columns_out(0)
    grand[...] = dg[...]
    for node in (1, 2):
        index, weight = tail_of(s, LIST + (node - 1) * (order // TILE), own, order)
        for i in range(len(index)):
            for j in range(len(index)):
                high, low = get(a, (at(index[i] * TILE, TILE), at(index[j] * TILE, TILE)))
                value = high.astype(F32) + low.astype(F32)
                corners[node - 1, i * TILE:(i + 1) * TILE, j * TILE:(j + 1) * TILE] = value
    for one in fetch(2, 0):
        one.start()
    root_ab = refs[-1]
    root_ab[...] = ab[...]

    @pl.loop(1, count)
    def _(node):
        start = LIST + (node - 1) * (order // TILE)
        index, weight = tail_of(s, start, own, order)
        panels_of(node, node % 2)

        def join():
            join_block(
                a, own,
                lambda i, j: corners[node - 1, i * TILE:(i + 1) * TILE, j * TILE:(j + 1) * TILE],
                lambda i: root_ab[at(index[i] * TILE, TILE), :], grand[...], index, weight,
            )

        solve(p, pt, dt, a, d, f, w, t, weights_of(s, start, order), emit_ab, emit_dg, join)
        columns_out(node)
        ext[node - 1, 0:half, :] = ab[0:half, :]
        ext[node - 1, half:, :] = dg[...]


def leaf_kernel(first, s, x0, x1, x2, x3, ex, ext, grand, self_out, core_out, end_out, cross_out, *rest):
    stage, sems, tails, top, grand_in, ab, dg = rest[:7]
    p, d, a, dc, f, w, t, pt, dt = pairs(rest[7:])
    r, c = s[0], s[1]
    blocks = [x for k, ref in enumerate((x0, x1, x2, x3)) for x in (ref.at[first - 3 + r], ex.at[k])]
    order = a[0].shape[0]
    own = d[0].shape[0]
    half = order // 2
    far = c // 2
    node = first + r
    start = LIST + (node - 1) * (order // TILE)
    index, weight = tail_of(s, start, own, order)
    parent = s[LINKS + node - 3] - 1
    copies = [pltpu.make_async_copy(ref, stage.at[k], sems.at[k]) for k, ref in enumerate(blocks)]
    later = [
        pltpu.make_async_copy(ext.at[parent, pl.ds(half, own)], top, sems.at[8]),
        pltpu.make_async_copy(grand, grand_in, sems.at[9]),
    ]
    for j, pick in enumerate(index):
        later.append(pltpu.make_async_copy(ext.at[parent, at(pick * TILE, TILE)], tails.at[j], sems.at[10 + j]))
    for one in copies + later:
        one.start()
    for one in copies:
        one.wait()
    load_panels([stage.at[k] for k in range(8)], r, p, d, pt, dt, half)
    dc[0][...] = d[0][:, at(far * STEP, STEP)]
    dc[1][...] = d[1][:, at(far * STEP, STEP)]

    def join():
        for one in later:
            one.wait()
        join_block(
            a, own, lambda i, j: grand_in[at(index[i] * TILE, TILE), at(index[j] * TILE, TILE)], lambda i: tails[i],
            top[...], index, weight,
        )

    def emit_ab(rows, cols, value):
        ab[rows, cols] = value

    def emit_dg(rows, cols, value):
        dg[rows, cols] = value

    solve(p, pt, dt, a, dc, f, w, t, weights_of(s, start, order), emit_ab, emit_dg, join)
    near_cols, end_cols = at((1 - far) * TILE, TILE), at(far * TILE, TILE)
    for out, side, cols in (
        (self_out, r, near_cols), (core_out, 1 - r, near_cols), (end_out, r, end_cols), (cross_out, 1 - r, end_cols)
    ):
        out[0:half, :] = ab[at(side * half, half), cols]
        share = out.shape[0] - half
        out[half:, :] = dg[:, cols] if share == own else dg[at(side * share, share), cols]


def shares_kernel(s, *refs):
    out, sems = refs[-2:]
    share = out.shape[0] // len(refs[:-2])
    copy_all([
        (ref.at[pl.ds(ref.shape[0] - share, share)], out.at[pl.ds(k * share, share)]) for k, ref in enumerate(refs[:-2])
    ], sems)


def upper_shares_kernel(s, upper, out, sems):
    shares_kernel(s, upper.at[0], upper.at[1], upper.at[2], out, sems)


def first_output_kernel(s, *refs):
    upper_self, upper_end, upper_shares, self_34, core_34, end_34, cross_34, shares_34 = refs[:8]
    ab, dg, sems = refs[-3:]
    r, c = s[0], s[1]
    half = ab.shape[1]
    share = half // 2
    middle = (c == 1) | (c == 2)
    for core in range(2):
        @pl.when((r == core) & middle)
        def _():
            pair = [self_34, core_34] if core == 0 else [core_34, self_34]
            copies = []
            for node, ref in enumerate([upper_self.at[k] for k in range(3)] + pair):
                copies.append((ref.at[pl.ds(0, half)], ab.at[node]))
                copies.append((ref.at[pl.ds(half, half)], dg.at[node]))
            copy_all(copies, sems)

        @pl.when((r == core) & jnp.logical_not(middle))
        def _():
            same, swapped = (3, 4) if core == 0 else (4, 3)
            found = [(k, upper_end.at[k], upper_shares, k) for k in range(3)]
            found += [(same, end_34, shares_34, 1), (swapped, cross_34, shares_34, 0)]
            copies = []
            for node, ref, shares, k in found:
                copies.append((ref.at[pl.ds(0, half)], ab.at[node]))
                copies.append((ref.at[pl.ds(half, share)], dg.at[node, pl.ds(core * share, share)]))
                copies.append((shares.at[pl.ds(k * share, share)], dg.at[node, pl.ds((1 - core) * share, share)]))
            copy_all(copies, sems)


def last_output_kernel(s, ab_in, dg_in, self_56, core_56, end_56, cross_56, ab, dg, stage, sems):
    r, c = s[0], s[1]
    half = ab.shape[1]
    middle = (c == 1) | (c == 2)
    for core in range(2):
        for inner in range(2):
            @pl.when((r == core) & (middle == (inner == 1)))
            def _():
                pair = [self_56, core_56] if inner else [end_56, cross_56]
                if core == 1:
                    pair = pair[::-1]
                copy_all([(ref, stage.at[k]) for k, ref in enumerate(pair)], sems)
    copies = []
    for k in range(2):
        copies.append((stage.at[k, pl.ds(0, half)], ab.at[5 + k]))
        copies.append((stage.at[k, pl.ds(half, half)], dg.at[5 + k]))
    copy_all(copies, sems)


def after(x, earlier):
    return lax.optimization_barrier((x, earlier))[0]


def chip_body(sigma_top, panels, inverse_diag, slot_lists, parent_links):
    r = lax.axis_index("row")
    c = lax.axis_index("col")
    leaf = lax.axis_index("leaf")
    panels, inverse, lists, links = panels[0], inverse_diag[0], slot_lists[0], parent_links[0]
    half = panels.shape[1]
    order = 2 * half
    own = inverse.shape[2]
    both = ("row", "col")
    routes = (((0, 1), (3, 2)), ((1, 2), (2, 1)), ((0, 2), (3, 1)))
    middles = (1, 2)
    swap = [(row * 4 + a, (1 - row) * 4 + a) for row in range(2) for a in middles]
    swap_ends = [(row * 4 + a, (1 - row) * 4 + a) for row in range(2) for a in (0, 3)]
    home = ((1, 0), (2, 3))
    home_cross = [(row * 4 + a, (1 - row) * 4 + b) for row in range(2) for a, b in home]
    leaf_routes = [
        [((lf * 2 + row) * 4 + a, ((lf ^ m) * 2 + row) * 4 + a) for lf in range(4) for row in range(2) for a in middles]
        for m in range(4)
    ]

    def straight(x):
        return [x] + [lax.ppermute(x, "col", route) for route in routes]

    def swapped(x):
        return lax.ppermute(x, both, swap)

    here = jnp.concatenate([jnp.stack([r, c, leaf, jnp.int32(0)]).astype(jnp.int32), links, lists.reshape(-1)])
    trunk = 3
    packed = half + own // 2

    def pack(first, count, sources):
        return move(functools.partial(pack_kernel, first), here, sources, [(count, packed, TILE)], 5 * count)[0]

    sigma_parts = straight(sigma_top)
    pack_t = pack(0, trunk, [panels, inverse])
    blocks_t = straight(pack_t)
    sigma_cols = move(join_columns_kernel, here, after(sigma_parts, pack_t), [(TILE, order)], 4)[0]
    sigma_rows = [sigma_cols] + [
        lax.ppermute(sigma_cols, ("leaf", "row", "col"), leaf_routes[m]) for m in range(1, 4)
    ]
    sigma_mine = move(stack_kernel, here, sigma_rows, [(4, TILE, order)], 4)[0]
    sigma_other = swapped(sigma_mine)
    pack_l = pack(trunk, 4, after([panels, inverse], pack_t))
    gathered = after(blocks_t, (sigma_mine, pack_l))
    other_t = swapped(move(stack_kernel, here, gathered, [(4, trunk, packed, TILE)], 4)[0])
    blocks_l = straight(after(pack_l, blocks_t[1:]))
    ext, grand, upper_self, upper_end = call(
        trunk_kernel, here, blocks_t + [other_t] + sigma_rows + [sigma_other],
        [(2, half + own, own), (own, own), (trunk, half + own, TILE), (trunk, packed, TILE)],
        [
            pltpu.VMEM((2, 8, packed, TILE), F32), pltpu.VMEM((8, TILE, order), F32), pltpu.SemaphoreType.DMA((3, 8)),
            pltpu.VMEM((2, order - own, order - own), F32), pltpu.VMEM((order, own), F32), pltpu.VMEM((own, own), F32),
        ] + scratch_pairs(
            (order, own), (own, own), (order, order), (order, own), (order, own), (own, own), (own, order), (own, own)
        ) + [pltpu.VMEM((order, own), F32)],
        [ANY] * 10, micros=1,
    )
    upper_home = lax.ppermute(upper_end, "col", home)
    tails = (order - own) // TILE
    leaf_scratch = [
        pltpu.VMEM((8, packed, TILE), F32), pltpu.SemaphoreType.DMA((10 + tails,)), pltpu.VMEM((tails, TILE, own), F32),
        pltpu.VMEM((own, own), F32), pltpu.VMEM((own, own), F32), pltpu.VMEM((order, STEP), F32),
        pltpu.VMEM((own, STEP), F32),
    ] + scratch_pairs(
        (order, own), (own, own), (order, order), (own, STEP), (order, STEP), (order, STEP), (own, STEP), (own, order),
        (own, own),
    )

    def leaves(first, theirs, end_rows):
        self_out, core_out, end_out, cross_out = call(
            functools.partial(leaf_kernel, first), here, blocks_l + [theirs, ext, grand],
            [(half + own, TILE)] * 2 + [(end_rows, TILE)] * 2, leaf_scratch, [ANY] * 7, micros=10,
        )
        return self_out, core_out, lax.ppermute(end_out, "col", home), lax.ppermute(cross_out, both, home_cross)

    chosen = after(blocks_l, (ext, upper_home))
    picked_34, picked_56 = move(swap_kernel, here, chosen, [(4, packed, TILE)] * 2, 8)
    other_34, other_56 = swapped(picked_34), swapped(picked_56)
    self_34, core_34, end_34, cross_34 = leaves(3, other_34, packed)
    self_56, core_56, end_56, cross_56 = leaves(5, after(other_56, self_34), half + own)

    def shared(kernel, parts, count):
        out = move(kernel, here, parts, [(count * (own // 2), TILE)], count)[0]
        return lax.ppermute(out, both, swap_ends)

    upper_shares = shared(upper_shares_kernel, [after(upper_home, (self_56, cross_34))], 3)
    shares_34 = shared(shares_kernel, [end_34, cross_34], 2)
    count = panels.shape[0]
    shapes = [(count, half, TILE), (count, own, TILE)]
    first_outputs = move(
        first_output_kernel, here,
        [
            upper_self, upper_home, upper_shares, self_34, swapped(core_34), end_34, cross_34, shares_34,
        ],
        shapes, 15,
    )
    ancestor_block, diagonal_block = pl.pallas_call(
        last_output_kernel,
        out_shape=[jax.ShapeDtypeStruct(shape, F32) for shape in shapes],
        in_specs=[pl.BlockSpec(memory_space=pltpu.SMEM)] + [ANY] * 6,
        out_specs=[ANY] * 2,
        scratch_shapes=[pltpu.VMEM((2, half + own, TILE), F32), pltpu.SemaphoreType.DMA((4,))],
        input_output_aliases={1: 0, 2: 1},
        compiler_params=pltpu.CompilerParams(vmem_limit_bytes=VMEM_LIMIT),
    )(here, *first_outputs, self_56, swapped(core_56), end_56, cross_56)
    return (ancestor_block[None], diagonal_block[None])


def child_blocks(ancestors, products, diagonals, parent_ids, picks, tile):
    count_parents = ancestors.shape[0]
    slot_count = ancestors.shape[1] // tile
    own_width = diagonals.shape[1]
    own_tiles = own_width // tile
    tail = picks[:, own_tiles:]
    living = tail >= 0
    indices = jnp.maximum(tail, 0)
    child_count = tail.shape[0]
    tail_count = tail.shape[1]
    a_tiles = ancestors.reshape(count_parents, slot_count, tile, slot_count, tile)
    corner = a_tiles[parent_ids[:, None, None], indices[:, :, None], :, indices[:, None, :], :]
    corner = jnp.transpose(corner, (0, 1, 3, 2, 4))
    weights = (living[:, :, None] & living[:, None, :]).astype(jnp.float32)
    corner = corner * weights[:, :, None, :, None]
    corner = corner.reshape(child_count, tail_count * tile, tail_count * tile)
    p_tiles = products.reshape(count_parents, slot_count, tile, own_width)
    side = p_tiles[parent_ids[:, None], indices]
    side = side * living.astype(jnp.float32)[:, :, None, None]
    side = side.reshape(child_count, tail_count * tile, own_width)
    top_left = jnp.take(diagonals, parent_ids, axis=0)
    upper = jnp.concatenate([top_left, -jnp.transpose(side, (0, 2, 1))], axis=2)
    lower = jnp.concatenate([-side, corner], axis=2)
    return jnp.concatenate([upper, lower], axis=1)


def body(sigma_top, panels, inverse_diag, slot_lists, parent_links):
    highest = lax.Precision.HIGHEST
    row_count = lax.axis_size("row")
    col_count = lax.axis_size("col")
    row_index = lax.axis_index("row")
    col_index = lax.axis_index("col")
    panel_local = panels[0]
    inverse_local = inverse_diag[0]
    picks_all = slot_lists[0]
    parents = parent_links[0]
    block_rows = panel_local.shape[1]
    block_cols = panel_local.shape[2]
    diag_width = inverse_local.shape[2]
    diag_rows = diag_width // row_count
    tile = TILE
    top_rows = lax.all_gather(sigma_top, ("leaf", "row"), axis=0, tiled=True)
    top_full = lax.all_gather(top_rows, "col", axis=1, tiled=True)
    partial_factor = jnp.einsum("vrk,vkj->vrj", panel_local, inverse_local, precision=highest)
    inverse_band = lax.dynamic_slice_in_dim(inverse_local, row_index * diag_rows, diag_rows, 2)
    partial_gram = jnp.einsum("vki,vkj->vij", inverse_band, inverse_local, precision=highest)
    factor_rows = lax.psum(partial_factor, "col")
    gram_mine = lax.psum_scatter(partial_gram, "col", scatter_dimension=2, tiled=True)
    slots_here = block_rows // tile
    slot_ids = row_index * slots_here + jnp.arange(slots_here, dtype=jnp.int32)
    listed = jnp.take(picks_all, slot_ids, axis=1) >= 0
    living = jnp.concatenate([jnp.ones((1, slots_here), jnp.bool_), listed], axis=0)
    row_weight = jnp.repeat(living.astype(jnp.float32), tile, axis=1)
    factor_rows = factor_rows * row_weight[:, :, None]
    factor_mine = lax.dynamic_slice_in_dim(factor_rows, col_index * block_cols, block_cols, 2)
    factor_cols = lax.all_gather(factor_mine, "row", axis=1, tiled=True)
    ancestors = top_full[None]
    ancestor_parts = []
    diagonal_parts = []
    bounds = ((0, 1), (1, 3), (3, 7))
    for level_id, (first_node, last_node) in enumerate(bounds):
        own_rows = lax.dynamic_slice_in_dim(ancestors, row_index * block_rows, block_rows, 1)
        product_mine = jnp.einsum(
            "vra,vac->vrc", own_rows, factor_cols[first_node:last_node], precision=highest
        )
        partial_diag = jnp.einsum(
            "vrj,vrc->vjc", factor_rows[first_node:last_node], product_mine, precision=highest
        )
        diag_piece = lax.psum_scatter(partial_diag, "row", scatter_dimension=1, tiled=True)
        diag_piece = diag_piece + gram_mine[first_node:last_node]
        ancestor_parts.append(-product_mine)
        if level_id == 2:
            diag_cols = lax.all_gather(diag_piece, "row", axis=1, tiled=True)
        else:
            width_nodes = last_node - first_node
            product_all, diag_all = (
                lax.all_gather(product_mine[:, None], ("row", "col"), axis=1, tiled=True),
                lax.all_gather(diag_piece[:, None], ("row", "col"), axis=1, tiled=True),
            )
            product_full = product_all.reshape(
                width_nodes, row_count, col_count, block_rows, block_cols
            )
            product_full = product_full.transpose(0, 1, 3, 2, 4).reshape(
                width_nodes, row_count * block_rows, col_count * block_cols
            )
            diag_full = diag_all.reshape(width_nodes, row_count, col_count, diag_rows, block_cols)
            diag_full = diag_full.transpose(0, 1, 3, 2, 4).reshape(
                width_nodes, row_count * diag_rows, col_count * block_cols
            )
            diag_cols = lax.dynamic_slice_in_dim(diag_full, col_index * block_cols, block_cols, 2)
            if level_id == 0:
                parent_ids = jnp.zeros((2,), jnp.int32)
                picks_level = picks_all[0:2]
            else:
                parent_ids = parents - 1
                picks_level = picks_all[2:6]
            ancestors = child_blocks(
                ancestors, product_full, diag_full, parent_ids, picks_level, tile
            )
        diagonal_parts.append(diag_cols)
    ancestor_block = jnp.concatenate(ancestor_parts, axis=0)[None]
    diagonal_block = jnp.concatenate(diagonal_parts, axis=0)[None]
    return (ancestor_block, diagonal_block)


def solution(mesh):
    two_middles = (mesh.shape["leaf"], mesh.shape["row"], mesh.shape["col"]) == (4, 2, 4)
    return jax.shard_map(
        chip_body if two_middles else body,
        mesh=mesh,
        in_specs=(
            P(("leaf", "row"), "col"),
            P("leaf", None, "row", "col"),
            P("leaf", None, "col", None),
            P("leaf", None, None),
            P("leaf", None),
        ),
        out_specs=(P("leaf", None, "row", "col"), P("leaf", None, None, "col")),
        check_vma=False,
    )
```

```python
import functools

import jax
import jax.numpy as jnp
from jax import lax
from jax.experimental import pallas as pl
from jax.experimental.pallas import tpu as pltpu
from jax.sharding import PartitionSpec as P

TILE = 128
STEP = 2 * TILE
QUARTER = TILE // 2
F32 = jnp.float32
BF16 = jnp.bfloat16
VMEM_LIMIT = 56 * 2**20
WHOLE = pl.BlockSpec(memory_space=pltpu.VMEM)
ANY = pl.BlockSpec(memory_space=pl.ANY)


def split(x):
    high = x.astype(BF16)
    return high, (x - high.astype(F32)).astype(BF16)


def dot3(a, b):
    dot = functools.partial(jnp.dot, preferred_element_type=F32)
    return dot(a[0], b[0]) + (dot(a[0], b[1]) + dot(a[1], b[0]))


def put(pair, index, value):
    high, low = split(value)
    pair[0][index] = high
    pair[1][index] = low


def get(pair, index):
    return pair[0][index], pair[1][index]


def at(start, size, unit=TILE):
    return pl.ds(pl.multiple_of(start, unit), size)


def tiles(size, step=STEP):
    return [slice(m, m + step) for m in range(0, size, step)]


ALL = slice(None)


def load_panels(blocks, r, p, d, pt, dt, half):
    for slot in range(4):
        for turn in range(2):
            ref = blocks[2 * slot + turn]
            side = r if turn == 0 else 1 - r
            panel = ref[0:half, :]
            put(p, (at(side * half, half), slice(slot * TILE, (slot + 1) * TILE)), panel)
            put(pt, (slice(slot * TILE, (slot + 1) * TILE), at(side * half, half)), panel.T)
            for j in range(4):
                rows = at(slot * TILE + side * QUARTER, QUARTER, QUARTER)
                place = slice(j * TILE, (j + 1) * TILE)
                put(d, (rows, place), ref[half + j * QUARTER:half + (j + 1) * QUARTER, :])
    for slot in range(4):
        for j in range(4):
            rows, cols = slice(slot * TILE, (slot + 1) * TILE), slice(j * TILE, (j + 1) * TILE)
            for whole, turned in zip(d, dt):
                turned[cols, rows] = whole[rows, cols].T


def solve(p, pt, dt, a, dc, f, w, t, weights, emit_ab, emit_dg, join):
    width = dc[0].shape[1]
    for rows in tiles(p[0].shape[0]):
        k = rows.start // TILE
        for cols in tiles(width):
            value = dot3(get(p, (rows, ALL)), get(dc, (ALL, cols)))
            value = jnp.concatenate([value[:TILE] * weights[k], value[TILE:] * weights[k + 1]], axis=0)
            put(f, (rows, cols), value)
    join()
    for cols in tiles(width):
        for rows in tiles(a[0].shape[0]):
            value = dot3(get(a, (rows, ALL)), get(f, (ALL, cols)))
            emit_ab(rows, cols, -value)
            put(w, (rows, cols), value)
        for rows in tiles(pt[0].shape[0]):
            value = dot3(get(pt, (rows, ALL)), get(w, (ALL, cols)))
            put(t, (rows, cols), value + dc[0][rows, cols].astype(F32) + dc[1][rows, cols].astype(F32))
        for rows in tiles(dt[0].shape[0]):
            emit_dg(rows, cols, dot3(get(dt, (rows, ALL)), get(t, (ALL, cols))))


def scratch_pairs(*shapes):
    return [pltpu.VMEM(shape, BF16) for shape in shapes for _ in range(2)]


def pairs(refs):
    return [(refs[i], refs[i + 1]) for i in range(0, len(refs), 2)]


def call(kernel, scalars, operands, outs, scratch, places=None, micros=1):
    return pl.pallas_call(
        kernel,
        out_shape=[jax.ShapeDtypeStruct(o, F32) for o in outs],
        in_specs=[pl.BlockSpec(memory_space=pltpu.SMEM)] + (places or [WHOLE] * len(operands)),
        out_specs=[WHOLE] * len(outs),
        scratch_shapes=scratch,
        compiler_params=pltpu.CompilerParams(vmem_limit_bytes=VMEM_LIMIT),
        cost_estimate=pl.CostEstimate(flops=micros * 10**9, bytes_accessed=1, transcendentals=0),
    )(scalars, *operands)


def copy_all(copies, sems):
    started = [pltpu.make_async_copy(src, dst, sems.at[i]) for i, (src, dst) in enumerate(copies)]
    for one in started:
        one.start()
    for one in started:
        one.wait()


def move(kernel, scalars, operands, outs, count, micros=1):
    return call(
        kernel, scalars, operands, outs, [pltpu.SemaphoreType.DMA((count,))], [ANY] * len(operands), micros
    )


LINKS, LIST = 4, 8


def tail_of(s, start, own, order):
    spots = [start + k for k in range(own // TILE, order // TILE)]
    return [jnp.maximum(s[k], 0) for k in spots], [(s[k] >= 0).astype(F32) for k in spots]


def weights_of(s, start, order):
    return [(s[start + j] >= 0).astype(F32) for j in range(order // TILE)]


def pack_kernel(first, s, panels, inverse, *rest):
    outs, sems = rest[:-1], rest[-1]
    half = panels.shape[1]
    copies = []
    node = first
    for out in outs:
        for i in range(out.shape[0]):
            copies.append((panels.at[node], out.at[i, pl.ds(0, half)]))
            for j in range(inverse.shape[2] // TILE):
                copies.append((
                    inverse.at[node, at(s[0] * QUARTER, QUARTER, QUARTER), pl.ds(j * TILE, TILE)],
                    out.at[i, pl.ds(half + j * QUARTER, QUARTER)],
                ))
            node += 1
    copy_all(copies, sems)


def join_columns_kernel(s, *refs):
    out, sems = refs[-2:]
    width = refs[0].shape[1]
    copy_all([(ref, out.at[:, pl.ds(k * width, width)]) for k, ref in enumerate(refs[:-2])], sems)


def stack_kernel(s, *refs):
    out, sems = refs[-2:]
    copy_all([(ref, out.at[k]) for k, ref in enumerate(refs[:-2])], sems)


def swap_kernel(s, *refs):
    blocks, outs, sems = refs[:4], refs[4:6], refs[6]
    copy_all([
        (ref.at[2 * pair + 1 - s[0]], out.at[k]) for pair, out in enumerate(outs) for k, ref in enumerate(blocks)
    ], sems)


def join_block(a, own, corner, rows_of, top, index, weight):
    put(a, (slice(0, own), slice(0, own)), top)
    for i in range(len(index)):
        place = slice(own + i * TILE, own + (i + 1) * TILE)
        value = rows_of(i) * weight[i]
        put(a, (place, slice(0, own)), value)
        put(a, (slice(0, own), place), value.T)
        for j in range(len(index)):
            put(a, (place, slice(own + j * TILE, own + (j + 1) * TILE)), corner(i, j) * (weight[i] * weight[j]))


def trunk_kernel(s, *refs):
    mine, theirs, sigmas = refs[:4], refs[4], refs[5:10]
    ext, grand, self_out, end_out = refs[10:14]
    stage, sigma, sems, corners, ab, dg = refs[14:20]
    p, d, a, f, w, t, pt, dt = pairs(refs[20:-1])
    r, c, leaf = s[0], s[1], s[2]
    order = a[0].shape[0]
    own = d[0].shape[0]
    half = order // 2
    far = c // 2
    count = 3

    def fetch(node, slot):
        found = []
        for k in range(4):
            found.append(pltpu.make_async_copy(mine[k].at[node], stage.at[slot, 2 * k], sems.at[slot, 2 * k]))
            found.append(pltpu.make_async_copy(theirs.at[k, node], stage.at[slot, 2 * k + 1], sems.at[slot, 2 * k + 1]))
        return found

    sigma_copies = [
        pltpu.make_async_copy(ref, sigma.at[k], sems.at[2, k])
        for k, ref in enumerate(list(sigmas[:4]) + [sigmas[4].at[m] for m in range(4)])
    ]
    for one in fetch(0, 0) + sigma_copies:
        one.start()

    def panels_of(node, slot):
        for one in fetch(node, slot):
            one.wait()
        load_panels([stage.at[slot, k] for k in range(8)], r, p, d, pt, dt, half)

    def emit_ab(rows, cols, value):
        ab[rows, cols] = value

    def emit_dg(rows, cols, value):
        dg[rows, cols] = value

    def columns_out(node):
        for out, col in ((self_out, c), (end_out, 3 * far)):
            out[node, 0:half, :] = ab[at(r * half, half), at(col * TILE, TILE)]
        self_out[node, half:, :] = dg[:, at(c * TILE, TILE)]
        end_out[node, half:, :] = dg[at(r * (own // 2), own // 2), at(3 * far * TILE, TILE)]

    panels_of(0, 0)
    for one in fetch(1, 1):
        one.start()

    def join_root():
        places = (c, 3 * far, 3 - c, 3 - 3 * far)
        span = order // 4
        for one in sigma_copies:
            one.wait()
        for m in range(4):
            for turn in range(2):
                side = r if turn == 0 else 1 - r
                rows = at(((leaf ^ m) * 2 + side) * TILE, TILE)
                for k in range(4):
                    value = sigma[4 * turn + m, :, k * span:(k + 1) * span]
                    put(a, (rows, at(places[k] * span, span)), value)

    solve(p, pt, dt, a, d, f, w, t, [1.0] * (order // TILE), emit_ab, emit_dg, join_root)
    columns_out(0)
    grand[...] = dg[...]
    for node in (1, 2):
        index, weight = tail_of(s, LIST + (node - 1) * (order // TILE), own, order)
        for i in range(len(index)):
            for j in range(len(index)):
                high, low = get(a, (at(index[i] * TILE, TILE), at(index[j] * TILE, TILE)))
                value = high.astype(F32) + low.astype(F32)
                corners[node - 1, i * TILE:(i + 1) * TILE, j * TILE:(j + 1) * TILE] = value
    for one in fetch(2, 0):
        one.start()
    root_ab = refs[-1]
    root_ab[...] = ab[...]

    @pl.loop(1, count)
    def _(node):
        start = LIST + (node - 1) * (order // TILE)
        index, weight = tail_of(s, start, own, order)
        panels_of(node, node % 2)

        def join():
            join_block(
                a, own,
                lambda i, j: corners[node - 1, i * TILE:(i + 1) * TILE, j * TILE:(j + 1) * TILE],
                lambda i: root_ab[at(index[i] * TILE, TILE), :], grand[...], index, weight,
            )

        solve(p, pt, dt, a, d, f, w, t, weights_of(s, start, order), emit_ab, emit_dg, join)
        columns_out(node)
        ext[node - 1, 0:half, :] = ab[0:half, :]
        ext[node - 1, half:, :] = dg[...]


def leaf_kernel(first, s, x0, x1, x2, x3, ex, ext, grand, self_out, core_out, end_out, cross_out, *rest):
    stage, sems, tails, top, grand_in, ab, dg = rest[:7]
    p, d, a, dc, f, w, t, pt, dt = pairs(rest[7:])
    r, c = s[0], s[1]
    blocks = [x for k, ref in enumerate((x0, x1, x2, x3)) for x in (ref.at[first - 3 + r], ex.at[k])]
    order = a[0].shape[0]
    own = d[0].shape[0]
    half = order // 2
    far = c // 2
    node = first + r
    start = LIST + (node - 1) * (order // TILE)
    index, weight = tail_of(s, start, own, order)
    parent = s[LINKS + node - 3] - 1
    copies = [pltpu.make_async_copy(ref, stage.at[k], sems.at[k]) for k, ref in enumerate(blocks)]
    later = [
        pltpu.make_async_copy(ext.at[parent, pl.ds(half, own)], top, sems.at[8]),
        pltpu.make_async_copy(grand, grand_in, sems.at[9]),
    ]
    for j, pick in enumerate(index):
        later.append(pltpu.make_async_copy(ext.at[parent, at(pick * TILE, TILE)], tails.at[j], sems.at[10 + j]))
    for one in copies + later:
        one.start()
    for one in copies:
        one.wait()
    load_panels([stage.at[k] for k in range(8)], r, p, d, pt, dt, half)
    dc[0][...] = d[0][:, at(far * STEP, STEP)]
    dc[1][...] = d[1][:, at(far * STEP, STEP)]

    def join():
        for one in later:
            one.wait()
        join_block(
            a, own, lambda i, j: grand_in[at(index[i] * TILE, TILE), at(index[j] * TILE, TILE)], lambda i: tails[i],
            top[...], index, weight,
        )

    def emit_ab(rows, cols, value):
        ab[rows, cols] = value

    def emit_dg(rows, cols, value):
        dg[rows, cols] = value

    solve(p, pt, dt, a, dc, f, w, t, weights_of(s, start, order), emit_ab, emit_dg, join)
    near_cols, end_cols = at((1 - far) * TILE, TILE), at(far * TILE, TILE)
    for out, side, cols in (
        (self_out, r, near_cols), (core_out, 1 - r, near_cols), (end_out, r, end_cols), (cross_out, 1 - r, end_cols)
    ):
        out[0:half, :] = ab[at(side * half, half), cols]
        share = out.shape[0] - half
        out[half:, :] = dg[:, cols] if share == own else dg[at(side * share, share), cols]


def shares_kernel(s, *refs):
    out, sems = refs[-2:]
    share = out.shape[0] // len(refs[:-2])
    copy_all([
        (ref.at[pl.ds(ref.shape[0] - share, share)], out.at[pl.ds(k * share, share)]) for k, ref in enumerate(refs[:-2])
    ], sems)


def upper_shares_kernel(s, upper, out, sems):
    shares_kernel(s, upper.at[0], upper.at[1], upper.at[2], out, sems)


def first_output_kernel(s, *refs):
    upper_self, upper_end, upper_shares, self_34, core_34, end_34, cross_34, shares_34 = refs[:8]
    ab, dg, sems = refs[-3:]
    r, c = s[0], s[1]
    half = ab.shape[1]
    share = half // 2
    middle = (c == 1) | (c == 2)
    for core in range(2):
        @pl.when((r == core) & middle)
        def _():
            pair = [self_34, core_34] if core == 0 else [core_34, self_34]
            copies = []
            for node, ref in enumerate([upper_self.at[k] for k in range(3)] + pair):
                copies.append((ref.at[pl.ds(0, half)], ab.at[node]))
                copies.append((ref.at[pl.ds(half, half)], dg.at[node]))
            copy_all(copies, sems)

        @pl.when((r == core) & jnp.logical_not(middle))
        def _():
            same, swapped = (3, 4) if core == 0 else (4, 3)
            found = [(k, upper_end.at[k], upper_shares, k) for k in range(3)]
            found += [(same, end_34, shares_34, 1), (swapped, cross_34, shares_34, 0)]
            copies = []
            for node, ref, shares, k in found:
                copies.append((ref.at[pl.ds(0, half)], ab.at[node]))
                copies.append((ref.at[pl.ds(half, share)], dg.at[node, pl.ds(core * share, share)]))
                copies.append((shares.at[pl.ds(k * share, share)], dg.at[node, pl.ds((1 - core) * share, share)]))
            copy_all(copies, sems)


def last_output_kernel(s, ab_in, dg_in, self_56, core_56, end_56, cross_56, ab, dg, stage, sems):
    r, c = s[0], s[1]
    half = ab.shape[1]
    middle = (c == 1) | (c == 2)
    for core in range(2):
        for inner in range(2):
            @pl.when((r == core) & (middle == (inner == 1)))
            def _():
                pair = [self_56, core_56] if inner else [end_56, cross_56]
                if core == 1:
                    pair = pair[::-1]
                copy_all([(ref, stage.at[k]) for k, ref in enumerate(pair)], sems)
    copies = []
    for k in range(2):
        copies.append((stage.at[k, pl.ds(0, half)], ab.at[5 + k]))
        copies.append((stage.at[k, pl.ds(half, half)], dg.at[5 + k]))
    copy_all(copies, sems)


def after(x, earlier):
    return lax.optimization_barrier((x, earlier))[0]


def chip_body(sigma_top, panels, inverse_diag, slot_lists, parent_links):
    r = lax.axis_index("row")
    c = lax.axis_index("col")
    leaf = lax.axis_index("leaf")
    panels, inverse, lists, links = panels[0], inverse_diag[0], slot_lists[0], parent_links[0]
    half = panels.shape[1]
    order = 2 * half
    own = inverse.shape[2]
    both = ("row", "col")
    routes = (((0, 1), (3, 2)), ((1, 2), (2, 1)), ((0, 2), (3, 1)))
    middles = (1, 2)
    swap = [(row * 4 + a, (1 - row) * 4 + a) for row in range(2) for a in middles]
    swap_ends = [(row * 4 + a, (1 - row) * 4 + a) for row in range(2) for a in (0, 3)]
    home = ((1, 0), (2, 3))
    home_cross = [(row * 4 + a, (1 - row) * 4 + b) for row in range(2) for a, b in home]
    leaf_routes = [
        [((lf * 2 + row) * 4 + a, ((lf ^ m) * 2 + row) * 4 + a) for lf in range(4) for row in range(2) for a in middles]
        for m in range(4)
    ]

    def straight(x):
        return [x] + [lax.ppermute(x, "col", route) for route in routes]

    def swapped(x):
        return lax.ppermute(x, both, swap)

    here = jnp.concatenate([jnp.stack([r, c, leaf, jnp.int32(0)]).astype(jnp.int32), links, lists.reshape(-1)])
    trunk = 3
    packed = half + own // 2

    def pack(first, count, sources):
        return move(functools.partial(pack_kernel, first), here, sources, [(count, packed, TILE)], 5 * count)[0]

    sigma_parts = straight(sigma_top)
    pack_t = pack(0, trunk, [panels, inverse])
    blocks_t = straight(pack_t)
    sigma_cols = move(join_columns_kernel, here, after(sigma_parts, pack_t), [(TILE, order)], 4)[0]
    sigma_rows = [sigma_cols] + [
        lax.ppermute(sigma_cols, ("leaf", "row", "col"), leaf_routes[m]) for m in range(1, 4)
    ]
    sigma_mine = move(stack_kernel, here, sigma_rows, [(4, TILE, order)], 4)[0]
    sigma_other = swapped(sigma_mine)
    pack_l = pack(trunk, 4, after([panels, inverse], pack_t))
    gathered = after(blocks_t, (sigma_mine, pack_l))
    other_t = swapped(move(stack_kernel, here, gathered, [(4, trunk, packed, TILE)], 4)[0])
    blocks_l = straight(after(pack_l, blocks_t[1:]))
    ext, grand, upper_self, upper_end = call(
        trunk_kernel, here, blocks_t + [other_t] + sigma_rows + [sigma_other],
        [(2, half + own, own), (own, own), (trunk, half + own, TILE), (trunk, packed, TILE)],
        [
            pltpu.VMEM((2, 8, packed, TILE), F32), pltpu.VMEM((8, TILE, order), F32), pltpu.SemaphoreType.DMA((3, 8)),
            pltpu.VMEM((2, order - own, order - own), F32), pltpu.VMEM((order, own), F32), pltpu.VMEM((own, own), F32),
        ] + scratch_pairs(
            (order, own), (own, own), (order, order), (order, own), (order, own), (own, own), (own, order), (own, own)
        ) + [pltpu.VMEM((order, own), F32)],
        [ANY] * 10, micros=1,
    )
    upper_home = lax.ppermute(upper_end, "col", home)
    tails = (order - own) // TILE
    leaf_scratch = [
        pltpu.VMEM((8, packed, TILE), F32), pltpu.SemaphoreType.DMA((10 + tails,)), pltpu.VMEM((tails, TILE, own), F32),
        pltpu.VMEM((own, own), F32), pltpu.VMEM((own, own), F32), pltpu.VMEM((order, STEP), F32),
        pltpu.VMEM((own, STEP), F32),
    ] + scratch_pairs(
        (order, own), (own, own), (order, order), (own, STEP), (order, STEP), (order, STEP), (own, STEP), (own, order),
        (own, own),
    )

    def leaves(first, theirs, end_rows):
        self_out, core_out, end_out, cross_out = call(
            functools.partial(leaf_kernel, first), here, blocks_l + [theirs, ext, grand],
            [(half + own, TILE)] * 2 + [(end_rows, TILE)] * 2, leaf_scratch, [ANY] * 7, micros=10,
        )
        return self_out, core_out, lax.ppermute(end_out, "col", home), lax.ppermute(cross_out, both, home_cross)

    chosen = after(blocks_l, (ext, upper_home))
    picked_34, picked_56 = move(swap_kernel, here, chosen, [(4, packed, TILE)] * 2, 8)
    other_34 = swapped(picked_34)
    self_34, core_34, end_34, cross_34 = leaves(3, other_34, packed)
    other_56 = swapped(after(picked_56, self_34))
    self_56, core_56, end_56, cross_56 = leaves(5, other_56, half + own)

    def shared(kernel, parts, count):
        out = move(kernel, here, parts, [(count * (own // 2), TILE)], count)[0]
        return lax.ppermute(out, both, swap_ends)

    upper_shares = shared(upper_shares_kernel, [after(upper_home, (self_56, cross_34))], 3)
    shares_34 = shared(shares_kernel, [end_34, cross_34], 2)
    count = panels.shape[0]
    shapes = [(count, half, TILE), (count, own, TILE)]
    first_outputs = move(
        first_output_kernel, here,
        [
            upper_self, upper_home, upper_shares, self_34, swapped(core_34), end_34, cross_34, shares_34,
        ],
        shapes, 15,
    )
    ancestor_block, diagonal_block = pl.pallas_call(
        last_output_kernel,
        out_shape=[jax.ShapeDtypeStruct(shape, F32) for shape in shapes],
        in_specs=[pl.BlockSpec(memory_space=pltpu.SMEM)] + [ANY] * 6,
        out_specs=[ANY] * 2,
        scratch_shapes=[pltpu.VMEM((2, half + own, TILE), F32), pltpu.SemaphoreType.DMA((4,))],
        input_output_aliases={1: 0, 2: 1},
        compiler_params=pltpu.CompilerParams(vmem_limit_bytes=VMEM_LIMIT),
    )(here, *first_outputs, self_56, swapped(core_56), end_56, cross_56)
    return (ancestor_block[None], diagonal_block[None])


def child_blocks(ancestors, products, diagonals, parent_ids, picks, tile):
    count_parents = ancestors.shape[0]
    slot_count = ancestors.shape[1] // tile
    own_width = diagonals.shape[1]
    own_tiles = own_width // tile
    tail = picks[:, own_tiles:]
    living = tail >= 0
    indices = jnp.maximum(tail, 0)
    child_count = tail.shape[0]
    tail_count = tail.shape[1]
    a_tiles = ancestors.reshape(count_parents, slot_count, tile, slot_count, tile)
    corner = a_tiles[parent_ids[:, None, None], indices[:, :, None], :, indices[:, None, :], :]
    corner = jnp.transpose(corner, (0, 1, 3, 2, 4))
    weights = (living[:, :, None] & living[:, None, :]).astype(jnp.float32)
    corner = corner * weights[:, :, None, :, None]
    corner = corner.reshape(child_count, tail_count * tile, tail_count * tile)
    p_tiles = products.reshape(count_parents, slot_count, tile, own_width)
    side = p_tiles[parent_ids[:, None], indices]
    side = side * living.astype(jnp.float32)[:, :, None, None]
    side = side.reshape(child_count, tail_count * tile, own_width)
    top_left = jnp.take(diagonals, parent_ids, axis=0)
    upper = jnp.concatenate([top_left, -jnp.transpose(side, (0, 2, 1))], axis=2)
    lower = jnp.concatenate([-side, corner], axis=2)
    return jnp.concatenate([upper, lower], axis=1)


def body(sigma_top, panels, inverse_diag, slot_lists, parent_links):
    highest = lax.Precision.HIGHEST
    row_count = lax.axis_size("row")
    col_count = lax.axis_size("col")
    row_index = lax.axis_index("row")
    col_index = lax.axis_index("col")
    panel_local = panels[0]
    inverse_local = inverse_diag[0]
    picks_all = slot_lists[0]
    parents = parent_links[0]
    block_rows = panel_local.shape[1]
    block_cols = panel_local.shape[2]
    diag_width = inverse_local.shape[2]
    diag_rows = diag_width // row_count
    tile = TILE
    top_rows = lax.all_gather(sigma_top, ("leaf", "row"), axis=0, tiled=True)
    top_full = lax.all_gather(top_rows, "col", axis=1, tiled=True)
    partial_factor = jnp.einsum("vrk,vkj->vrj", panel_local, inverse_local, precision=highest)
    inverse_band = lax.dynamic_slice_in_dim(inverse_local, row_index * diag_rows, diag_rows, 2)
    partial_gram = jnp.einsum("vki,vkj->vij", inverse_band, inverse_local, precision=highest)
    factor_rows = lax.psum(partial_factor, "col")
    gram_mine = lax.psum_scatter(partial_gram, "col", scatter_dimension=2, tiled=True)
    slots_here = block_rows // tile
    slot_ids = row_index * slots_here + jnp.arange(slots_here, dtype=jnp.int32)
    listed = jnp.take(picks_all, slot_ids, axis=1) >= 0
    living = jnp.concatenate([jnp.ones((1, slots_here), jnp.bool_), listed], axis=0)
    row_weight = jnp.repeat(living.astype(jnp.float32), tile, axis=1)
    factor_rows = factor_rows * row_weight[:, :, None]
    factor_mine = lax.dynamic_slice_in_dim(factor_rows, col_index * block_cols, block_cols, 2)
    factor_cols = lax.all_gather(factor_mine, "row", axis=1, tiled=True)
    ancestors = top_full[None]
    ancestor_parts = []
    diagonal_parts = []
    bounds = ((0, 1), (1, 3), (3, 7))
    for level_id, (first_node, last_node) in enumerate(bounds):
        own_rows = lax.dynamic_slice_in_dim(ancestors, row_index * block_rows, block_rows, 1)
        product_mine = jnp.einsum(
            "vra,vac->vrc", own_rows, factor_cols[first_node:last_node], precision=highest
        )
        partial_diag = jnp.einsum(
            "vrj,vrc->vjc", factor_rows[first_node:last_node], product_mine, precision=highest
        )
        diag_piece = lax.psum_scatter(partial_diag, "row", scatter_dimension=1, tiled=True)
        diag_piece = diag_piece + gram_mine[first_node:last_node]
        ancestor_parts.append(-product_mine)
        if level_id == 2:
            diag_cols = lax.all_gather(diag_piece, "row", axis=1, tiled=True)
        else:
            width_nodes = last_node - first_node
            product_all, diag_all = (
                lax.all_gather(product_mine[:, None], ("row", "col"), axis=1, tiled=True),
                lax.all_gather(diag_piece[:, None], ("row", "col"), axis=1, tiled=True),
            )
            product_full = product_all.reshape(
                width_nodes, row_count, col_count, block_rows, block_cols
            )
            product_full = product_full.transpose(0, 1, 3, 2, 4).reshape(
                width_nodes, row_count * block_rows, col_count * block_cols
            )
            diag_full = diag_all.reshape(width_nodes, row_count, col_count, diag_rows, block_cols)
            diag_full = diag_full.transpose(0, 1, 3, 2, 4).reshape(
                width_nodes, row_count * diag_rows, col_count * block_cols
            )
            diag_cols = lax.dynamic_slice_in_dim(diag_full, col_index * block_cols, block_cols, 2)
            if level_id == 0:
                parent_ids = jnp.zeros((2,), jnp.int32)
                picks_level = picks_all[0:2]
            else:
                parent_ids = parents - 1
                picks_level = picks_all[2:6]
            ancestors = child_blocks(
                ancestors, product_full, diag_full, parent_ids, picks_level, tile
            )
        diagonal_parts.append(diag_cols)
    ancestor_block = jnp.concatenate(ancestor_parts, axis=0)[None]
    diagonal_block = jnp.concatenate(diagonal_parts, axis=0)[None]
    return (ancestor_block, diagonal_block)


def solution(mesh):
    two_middles = (mesh.shape["leaf"], mesh.shape["row"], mesh.shape["col"]) == (4, 2, 4)
    return jax.shard_map(
        chip_body if two_middles else body,
        mesh=mesh,
        in_specs=(
            P(("leaf", "row"), "col"),
            P("leaf", None, "row", "col"),
            P("leaf", None, "col", None),
            P("leaf", None, None),
            P("leaf", None),
        ),
        out_specs=(P("leaf", None, "row", "col"), P("leaf", None, None, "col")),
        check_vma=False,
    )
```
